512 devices in a mesh: group: 4 (over x), sec: 128 (over z, y, core).
Axes of the slice: x: 4, y: 4, z: 16, core: 2. Of those that a mesh axis runs over, the one named last changes fastest.
Arguments:
- fixed_desc: bfloat16 [128, 64, 64, 512], P('sec', 'group'), may hold values from -16 to 16
- moving_desc: bfloat16 [128, 64, 64, 512], P('sec', 'group'), may hold values from -16 to 16
- offsets: int32 [128, 64, 2, 64], P('sec', 'group'), may hold values from -8 to 8
- owner: int32 [128, 64], P('sec', 'group'), may hold values from 0 to 31
- counts: int32 [128, 4], P('sec', 'group'), may hold values from 1 to 16, 40 in all within a row
- vert: float32 [128, 64, 1024], P('sec', 'group'), may hold values from 0.5 to 2
- hori: float32 [128, 64, 1024], P('sec', 'group'), may hold values from 0.5 to 2
Outputs:
- displacement: float32 [128, 2, 64, 1024], P('sec', None, 'group')
- residual: float32 [128, 2, 64, 1024], P('sec', None, 'group')
The draws below stay inside these ranges and needn't reach their ends.
Inputs may be any that keep to these rules, and one draw needn't show every extreme that they name: The counts of one section sum to 40, and in every section some block holds 16.
All inputs are finite; a program needn't handle non-finite values.
Results may differ from the reference program's by a relative error of at most 0.0003.
Values may be sent and summed in bfloat16 or wider, within the bound.
No kernel may reach another device: no remote copies, remote signals or barrier semaphores. Data moves between devices by JAX's collectives and lax.ppermute only.
A program may use at most 64 MiB of HBM per device.

```python
import math
import jax
import jax.numpy as jnp
import numpy as np
from jax import lax

ROWS_DEV = 16
COLS = 1024
TILE_W = 128
PATCH_DEV = 16
FLOW = 64
CAND = 64
CORR = 512
OUTER = 2
CG_STEPS = 1
SECTIONS = 128
NR = 64
PATCHES = 64
TILES = 32
N_GROUP = 4


def paired_features(key):
    fixed = jax.random.normal(jax.random.fold_in(key, 101), (SECTIONS, PATCHES, FLOW, CORR), jnp.float32)
    moving = jax.random.normal(jax.random.fold_in(key, 102), (SECTIONS, PATCHES, CAND, CORR), jnp.float32)
    return (fixed, moving)


def draw_fixed_desc(key, part):
    fixed, moving = paired_features(key)
    return jnp.clip(fixed, -16.0, 16.0).astype(jnp.bfloat16)


def draw_moving_desc(key, part):
    fixed, moving = paired_features(key)
    return jnp.clip(moving, -16.0, 16.0).astype(jnp.bfloat16)


def set_ends(result, rng, low, largest):
    shape = result.shape
    spot = [jax.random.randint(jax.random.fold_in(rng, axis), (), 0, shape[axis]) for axis in range(len(shape))]
    result = result.at[tuple(spot)].set(low)
    longest = shape.index(max(shape))
    spot[longest] = (spot[longest] + 1) % shape[longest]
    return result.at[tuple(spot)].set(largest)


def steps_of(own_key, extent, shards, smallest, high):
    factor_of = 1.0
    for position, shards_of in shards:
        draws = jax.random.uniform(jax.random.fold_in(jax.random.fold_in(own_key, 6), position), (shards_of,), jnp.float32, smallest / len(shards), high / len(shards))
        factor_of = factor_of * jnp.repeat(jnp.exp(draws), extent[position] // shards_of).reshape((-1,) + (1,) * (len(extent) - 1 - position))
    return factor_of


def length_profile(amount, total, limit, lean):
    portions = [(1 << 20) // math.isqrt(standing ** lean) + 1 for standing in range(2, amount + 1)]
    spare, given = total - limit - (amount - 1), [1] * (amount - 1)
    while spare > 0:
        candidates = [i for i in range(amount - 1) if given[i] < limit]
        pool, left = sum([portions[i] for i in candidates]), spare
        for i in candidates:
            more = min(limit - given[i], max(1, left * portions[i] // pool), spare)
            given[i] = given[i] + more
            spare = spare - more
    return np.array([limit] + given)


def ragged(stream_key, number_of, total, reach, skew):
    if number_of == 2:
        one = jax.random.randint(stream_key, (), max(1, total - reach), min(reach, total - 1) + 1)
        return jnp.stack([one, total - one])
    sizes = jnp.asarray(length_profile(number_of, total, reach, skew), jnp.int32)
    twos = (number_of - 1) // 2
    giver, taker = sizes[1:1 + 2 * twos:2], sizes[2:2 + 2 * twos:2]
    room = jnp.minimum(giver - 1, reach - taker)
    shifted = jax.random.randint(jax.random.fold_in(stream_key, 1), (twos,), 0, 1 << 20) % (room + 1)
    sizes = sizes.at[1:1 + 2 * twos:2].set(giver - shifted).at[2:2 + 2 * twos:2].set(taker + shifted)
    return sizes[jax.random.permutation(jax.random.fold_in(stream_key, 2), number_of)]


def setup_inputs(seed: int = 0) -> dict:
    keys = jax.random.split(jax.random.key(seed), 8)
    fixed_desc = draw_fixed_desc(jax.random.fold_in(keys[7], 71), 0)
    moving_desc = draw_moving_desc(jax.random.fold_in(keys[7], 71), 0)
    offsets = set_ends(jax.random.randint(keys[2], (SECTIONS, PATCHES, 2, CAND), -8, 9), jax.random.fold_in(keys[2], 1), -8, 8).astype(jnp.int32)
    owner = set_ends(jax.random.randint(keys[3], (SECTIONS, PATCHES), 0, TILES), jax.random.fold_in(keys[3], 1), 0, TILES - 1).astype(jnp.int32)
    counts = jax.vmap(lambda own: ragged(own, N_GROUP, 5 * PATCH_DEV // 2, PATCH_DEV, 0))(jax.random.split(keys[4], SECTIONS)).reshape((SECTIONS, N_GROUP)).astype(jnp.int32)
    vert = jnp.clip(jnp.exp(math.log(2.0) - 1.3862944 * jax.random.uniform(keys[5], (SECTIONS, NR, COLS), jnp.float32) ** steps_of(keys[5], (SECTIONS, NR, COLS), ((0, 128), (1, 4)), -0.2, 0.2)), 0.5, 2.0)
    hori = jnp.clip(jnp.exp(math.log(2.0) - 1.3862944 * jax.random.uniform(keys[6], (SECTIONS, NR, COLS), jnp.float32) ** steps_of(keys[6], (SECTIONS, NR, COLS), ((0, 128), (1, 4)), -0.2, 0.2)), 0.5, 2.0)
    return dict(fixed_desc=fixed_desc, moving_desc=moving_desc, offsets=offsets, owner=owner, counts=counts, vert=vert, hori=hori)


spread_sq = 4.0
highest = lax.Precision.HIGHEST

def tile_mean(field):
    lead = field.shape[:-2]
    blocks = field.reshape(lead + (N_GROUP, ROWS_DEV, COLS // TILE_W, TILE_W))
    return lax.optimization_barrier(jnp.mean(blocks, axis=(-3, -1))).reshape(lead + (TILES,))

def spread(values):
    lead = values.shape[:-1]
    blocks = values.reshape(lead + (N_GROUP, 1, COLS // TILE_W, 1))
    wide = jnp.broadcast_to(blocks, lead + (N_GROUP, ROWS_DEV, COLS // TILE_W, TILE_W))
    return wide.reshape(lead + (NR, COLS))

def match_section(inputs):
    fixed, moving, shifts = inputs
    scores = jnp.einsum('pic,pjc->pij', fixed.astype(jnp.float32), moving.astype(jnp.float32), precision=highest) / math.sqrt(CORR)
    likely = jax.nn.softmax(scores, axis=-1)
    flow_rows = jnp.einsum('pij,pkj->pki', likely, shifts.astype(jnp.float32), precision=highest)
    return lax.optimization_barrier(jnp.mean(flow_rows, axis=-1))

def reference(fixed_desc, moving_desc, offsets, owner, counts, vert, hori):
    partner = jnp.concatenate([moving_desc[1:], jnp.zeros_like(moving_desc[:1])], 0)
    targets = lax.map(match_section, (fixed_desc, partner, offsets))
    targets = jnp.transpose(targets, (0, 2, 1))
    slots = jnp.arange(PATCHES)
    validity = ((slots % PATCH_DEV)[None, :] < counts[:, slots // PATCH_DEV]).astype(jnp.float32)
    one_hot = (owner[:, :, None] == jnp.arange(TILES)[None, None, :]).astype(jnp.float32)
    not_last = (jnp.arange(SECTIONS) < SECTIONS - 1).astype(jnp.float32)
    vert_up = jnp.concatenate([jnp.zeros((SECTIONS, 1, COLS), jnp.float32), vert[:, :-1]], 1)[:, None]
    hori_left = jnp.concatenate([jnp.zeros((SECTIONS, NR, 1), jnp.float32), hori[:, :, :-1]], 2)[:, None]
    vert_here = vert[:, None]
    hori_here = hori[:, None]
    zero_row = jnp.zeros((SECTIONS, 2, 1, COLS), jnp.float32)
    zero_col = jnp.zeros((SECTIONS, 2, NR, 1), jnp.float32)
    zero_sec = jnp.zeros((1, 2, NR, COLS), jnp.float32)

    def neighbour_terms(field):
        below = jnp.concatenate([field[:, :, 1:], zero_row], 2)
        above = jnp.concatenate([zero_row, field[:, :, :-1]], 2)
        right = jnp.concatenate([field[:, :, :, 1:], zero_col], 3)
        left = jnp.concatenate([zero_col, field[:, :, :, :-1]], 3)
        upper = jnp.concatenate([field[1:], zero_sec], 0)
        lower = jnp.concatenate([zero_sec, field[:-1]], 0)
        spring = vert_here * (field - below) + vert_up * (field - above) + hori_here * (field - right) + hori_left * (field - left)
        return (spring, upper, lower)
    displacement = jnp.zeros((SECTIONS, 2, NR, COLS), jnp.float32)
    residual = displacement
    for outer_step in range(OUTER):
        spring, upper, lower = neighbour_terms(displacement)
        means = tile_mean(displacement - upper)
        look = jnp.einsum('skt,spt->skp', means, one_hot, precision=highest)
        mismatch = look - targets
        weight = validity / (1.0 + lax.optimization_barrier(jnp.sum(mismatch * mismatch, axis=1)) / spread_sq)
        terms = jnp.concatenate([weight[:, None], weight[:, None] * targets], 1)
        tile_sum = jnp.einsum('skp,spt->skt', terms, one_hot, precision=highest) * not_last[:, None, None]
        wfield = spread(tile_sum[:, 0:1])
        efield = spread(tile_sum[:, 1:3])
        wprev = jnp.concatenate([jnp.zeros_like(wfield[:1]), wfield[:-1]], 0)
        eprev = jnp.concatenate([jnp.zeros_like(efield[:1]), efield[:-1]], 0)
        rhs = efield - eprev

        def apply_op(field):
            spring_part, upper_part, lower_part = neighbour_terms(field)
            return spring_part + wfield * (field - upper_part) + wprev * (field - lower_part)
        image = spring + wfield * (displacement - upper) + wprev * (displacement - lower)
        residual = rhs - image
        direction = residual
        norm_now = jnp.sum(residual * residual)
        for iteration in range(CG_STEPS):
            image = apply_op(direction)
            alpha = norm_now / jnp.sum(direction * image)
            displacement = displacement + alpha * direction
            residual = residual - alpha * image
            norm_next = jnp.sum(residual * residual)
            direction = residual + norm_next / norm_now * direction
            norm_now = norm_next
    return (displacement, residual)
```

```python
import math

import jax
import jax.numpy as jnp
from jax import lax
from jax.experimental import pallas as pl
from jax.experimental.pallas import tpu as pltpu
from jax.sharding import Mesh, PartitionSpec as P

TILE_W = 128
SPREAD_SQ = 4.0
CHIPS_Y = 4
CORES = 2
SEC = ("z", "y", "core")
F32 = jnp.float32

COLUMN_KV, COLUMN_K2V, COLUMN_KXV, COLUMN_VL, COLUMN_VR, COLUMN_HT, COLUMN_HB = range(7)
COLUMN_DV, COLUMN_XBR, COLUMN_XBL, COLUMN_XTR, COLUMN_XTL = range(7, 12)
COLUMN_KH, COLUMN_K2H, COLUMN_KXH, COLUMN_DH, COLUMN_DT = range(12, 17)
COLUMN_OWNER = 17
COLUMN_NEAR = 19
COLUMN_FAR = 21
GROUP_LANES = 32


def iota(shape, axis):
    return lax.broadcasted_iota(jnp.int32, shape, axis)


def lane_sum(x):
    return jnp.sum(x, axis=1, keepdims=True)


def row_sum(x):
    return jnp.sum(x, axis=0, keepdims=True)


def total(x):
    return lane_sum(row_sum(x))


def edge_kernel(vert_ref, hori_ref, above_ref, out_ref):
    rows, cols = hori_ref.shape
    tiles = cols // TILE_W
    lane = iota((rows, TILE_W), 1)
    last = jnp.zeros((rows, TILE_W), F32)
    for j in range(tiles):
        out_ref[j : j + 1, :] = vert_ref[rows - 1 : rows, j * TILE_W : (j + 1) * TILE_W]
        column = hori_ref[:, (j + 1) * TILE_W - 1 : (j + 1) * TILE_W]
        last = jnp.where(lane == j, column, last)
    out_ref[tiles : 2 * tiles, :] = above_ref[...]
    out_ref[2 * tiles : 2 * tiles + rows, :] = last


def border_kernel(group_ref, vert_ref, hori_ref, own_ref, next_ref, owner_ref, out_ref, stack):
    rows, cols = hori_ref.shape
    tiles = cols // TILE_W
    last_group = group_ref[0] == group_ref[1]
    bottom = jnp.where(last_group, 1.0, 4.0).astype(F32)

    v_last = own_ref[0:tiles, :]
    v_above = own_ref[tiles : 2 * tiles, :]
    for j in range(tiles):
        span = slice(j * TILE_W, (j + 1) * TILE_W)
        stack[j : j + 1, :] = vert_ref[rows - 2 : rows - 1, span]
        stack[tiles + j : tiles + j + 1, :] = vert_ref[0:1, span]
        stack[2 * tiles + j : 2 * tiles + j + 1, :] = hori_ref[rows - 1 : rows, span]
        stack[3 * tiles + j : 3 * tiles + j + 1, :] = hori_ref[0:1, span]
    v_second, v_first = stack[0:tiles, :], stack[tiles : 2 * tiles, :]
    h_last, h_first = stack[2 * tiles : 3 * tiles, :], stack[3 * tiles : 4 * tiles, :]
    lane = iota((tiles, TILE_W), 1)
    inside = lane < TILE_W - 1
    square = v_last * v_last
    step_last = v_last - pltpu.roll(v_last, TILE_W - 1, 1)
    step_above = v_above - pltpu.roll(v_above, TILE_W - 1, 1)
    dh = lane_sum(
        bottom * square * v_last
        + v_second * square
        + jnp.where(inside, h_last * step_last * step_last, 0.0)
    )
    dt = lane_sum(
        v_first * v_above * v_above + jnp.where(inside, h_first * step_above * step_above, 0.0)
    )
    table = owner_ref[...]
    for column, value in (
        (COLUMN_KH, lane_sum(v_last)),
        (COLUMN_K2H, lane_sum(square)),
        (COLUMN_KXH, lane_sum(v_last * next_ref[0:tiles, :])),
        (COLUMN_DH, dh),
        (COLUMN_DT, dt),
    ):
        table = jnp.where(lane == column, value, table)

    tall = iota((rows, TILE_W), 1)
    zero = jnp.zeros((rows, TILE_W), F32)
    picked = {}
    for name, ref, column in (
        ("h0", hori_ref, 0),
        ("h126", hori_ref, TILE_W - 2),
        ("v0", vert_ref, 0),
        ("v1", vert_ref, 1),
        ("v126", vert_ref, TILE_W - 2),
        ("v127", vert_ref, TILE_W - 1),
    ):
        value = zero
        for j in range(tiles):
            at = j * TILE_W + column
            value = jnp.where(tall == j, ref[:, at : at + 1], value)
        picked[name] = value
    wide = iota((tiles, TILE_W), 0)
    diagonal = iota((tiles, TILE_W), 1) == wide

    def above_at(column):
        return row_sum(jnp.where(diagonal, v_above[:, column : column + 1], 0.0))

    a0, a1 = above_at(0), above_at(1)
    a126, a127 = above_at(TILE_W - 2), above_at(TILE_W - 1)
    right = own_ref[2 * tiles : 2 * tiles + rows, :]
    left = pltpu.roll(right, 1, 1)
    row = iota((rows, TILE_W), 0)
    within = row < rows - 1
    inner_tile = iota((1, TILE_W), 1) < tiles - 1
    step_right = right - pltpu.roll(right, rows - 1, 0)
    step_left = left - pltpu.roll(left, rows - 1, 0)
    right_sq, left_sq = right * right, left * left
    side_right = row_sum(
        picked["h126"] * right_sq + jnp.where(within, picked["v127"] * step_right * step_right, 0.0)
    )
    side_left = row_sum(
        picked["h0"] * left_sq + jnp.where(within, picked["v0"] * step_left * step_left, 0.0)
    )
    cube = row_sum(right_sq * right)
    dv = side_right + jnp.where(
        inner_tile, pltpu.roll(side_left, TILE_W - 1, 1) + 4.0 * cube, cube
    )
    end, pre = rows - 1, rows - 2
    v0, v1, v126, v127 = (picked[n] for n in ("v0", "v1", "v126", "v127"))
    h0, h126 = picked["h0"], picked["h126"]

    def at(x, r):
        return x[r : r + 1, :]

    xbr = at(h126, end) * (at(v127, end) - at(v126, end)) * at(right, end) + at(v127, pre) * at(
        v127, end
    ) * (at(right, end) - at(right, pre))
    xbl = -(
        at(h0, end) * (at(v0, end) - at(v1, end)) * at(left, end)
        + at(v0, pre) * at(v0, end) * (at(left, end) - at(left, pre))
    )
    xtr = -(
        at(h126, 0) * (a127 - a126) * at(right, 0)
        + at(v127, 0) * a127 * (at(right, 0) - at(right, 1))
    )
    xtl = at(h0, 0) * (a0 - a1) * at(left, 0) + at(v0, 0) * a0 * (at(left, 0) - at(left, 1))
    next_right = next_ref[2 * tiles : 2 * tiles + rows, :]
    stack[...] = jnp.zeros_like(stack)
    for column, value in (
        (COLUMN_KV, row_sum(right)),
        (COLUMN_K2V, row_sum(right_sq)),
        (COLUMN_KXV, row_sum(right * next_right)),
        (COLUMN_VL, at(v0, end)),
        (COLUMN_VR, at(v127, end)),
        (COLUMN_HT, at(right, 0)),
        (COLUMN_HB, at(right, end)),
        (COLUMN_DV, dv),
        (COLUMN_XBR, xbr),
        (COLUMN_XBL, xbl),
        (COLUMN_XTR, xtr),
        (COLUMN_XTL, xtl),
    ):
        stack[column : column + 1, :] = value
    turned = jnp.transpose(stack[...])[0:tiles, :]
    out_ref[...] = jnp.where(lane <= COLUMN_XTL, turned, table)


def match_kernel(column, last, fixed_ref, moving_ref, offsets_ref, table_ref, out_ref):
    patches, flow, corr = fixed_ref.shape[-3:]
    fixed = fixed_ref.reshape(patches * flow, corr)
    moving = moving_ref.reshape(patches * flow, corr)
    pair = 2 * flow
    lane = iota((flow, pair), 1)
    lower = lane < flow
    scale = 1.0 / math.sqrt(corr)
    shifts = offsets_ref[...]
    table = table_ref[...]
    spot_row = iota(table.shape, 0)
    spot_lane = iota(table.shape, 1)
    for first in range(0, patches, 2):
        at = slice(first * flow, (first + 2) * flow)
        scores = lax.dot_general(
            moving[at, :], fixed[at, :], (((1,), (1,)), ((), ())), preferred_element_type=F32
        )
        both = jnp.where(lower, scores[0:flow, :], scores[flow:pair, :])
        top = jnp.max(both, axis=0, keepdims=True)
        likely = jnp.exp((both - top) * scale)
        sums = lax.dot_general(
            shifts,
            likely,
            (((1,), (0,)), ((), ())),
            precision=lax.Precision.HIGHEST,
            preferred_element_type=F32,
        )
        weight = row_sum(likely)
        ratio = sums / (weight * flow)
        for half in range(2):
            keep = (iota((1, pair), 1) < flow) == (half == 0)
            for k in range(2):
                where = 2 * (first + half) + k
                value = lane_sum(jnp.where(keep, ratio[where : where + 1, :], 0.0))
                spot = (spot_row == first + half) & (spot_lane == column + k)
                table = jnp.where(spot, value, table)
    if not last:
        out_ref[...] = table
        return
    per_row = TILE_W // GROUP_LANES
    table = jnp.where(spot_lane < GROUP_LANES, table, 0.0)
    for half in range(table.shape[0] // per_row):
        line = jnp.zeros((1, TILE_W), F32)
        for j in range(per_row):
            source = table[half * per_row + j : half * per_row + j + 1, :]
            line = line + (pltpu.roll(source, j * GROUP_LANES, 1) if j else source)
        out_ref[half : half + 1, :] = line


def stack_kernel(
    dims, place_ref, seen_ref, vert_ref, hori_ref, own_ref, next_ref, prev_ref,
    disp_ref, res_ref, rows_ref, turn_ref, sums_ref, out_ref, field_ref,
):
    groups, sections, rows, tiles, chips_z = dims
    per_chip = sections // chips_z
    halves = tiles * GROUP_LANES // TILE_W
    count = groups * tiles
    nodes = float(rows * TILE_W)
    me, group = place_ref[0], place_ref[1]

    for core in range(CORES):
        for g in range(groups):
            for y in range(per_chip // CORES):
                base = ((core * groups + g) * (per_chip // CORES) + y) * chips_z * halves
                for h in range(halves):
                    rows_ref[g * halves + h, pl.ds(y * CORES + core, chips_z, stride=per_chip), :] = seen_ref[
                        pl.ds(base + h, chips_z, stride=halves), :
                    ]
    for g in range(groups):
        for h in range(halves):
            turn_ref[g, h * TILE_W : (h + 1) * TILE_W, :] = jnp.transpose(rows_ref[g * halves + h])

    def block(g, column):
        return turn_ref[g, pl.ds(column, tiles, stride=GROUP_LANES), :]

    def figure(column):
        return jnp.concatenate([block(g, column) for g in range(groups)], 0)

    def slots(near, far, turn):
        parts = []
        for g in range(groups):
            parts.append(block(g, near))
            other = block(g, far)
            parts.append(pltpu.roll(other, sections - 1, 1) if turn else other)
        return jnp.concatenate(parts, 0)

    lane = iota((count, sections), 1)
    tile_row = iota((count, sections), 0)
    along = lax.rem(tile_row, tiles)
    not_last = lane < sections - 1

    def up(x):
        return jnp.where(not_last, pltpu.roll(x, sections - 1, 1), 0.0)

    def low(x):
        return jnp.where(lane > 0, pltpu.roll(x, 1, 1), 0.0)

    zero_tiles = jnp.zeros((tiles, sections), F32)

    def from_above(x):
        return jnp.concatenate([zero_tiles, x[: count - tiles]], 0)

    def from_below(x):
        return jnp.concatenate([x[tiles:], zero_tiles], 0)

    def from_left(x):
        return jnp.where(along > 0, pltpu.roll(x, 1, 0), 0.0)

    def from_right(x):
        return jnp.where(along < tiles - 1, pltpu.roll(x, count - 1, 0), 0.0)

    owner = slots(COLUMN_OWNER, COLUMN_OWNER + 1, False)
    targets = [slots(COLUMN_NEAR + k, COLUMN_FAR + k, True) for k in range(2)]
    valid = jnp.where(owner >= 0.0, 1.0, 0.0)

    def tile_sums(miss):
        weight = valid / (1.0 + (miss[0] * miss[0] + miss[1] * miss[1]) / SPREAD_SQ)
        terms = (weight, weight * targets[0], weight * targets[1])
        for t in range(count):
            mine = owner == float(t)
            for n, term in enumerate(terms):
                sums_ref[n, t : t + 1, :] = row_sum(jnp.where(mine, term, 0.0))
        return [jnp.where(not_last, sums_ref[n], 0.0) for n in range(3)]

    kh, kv = figure(COLUMN_KH), figure(COLUMN_KV)
    k2h, k2v = figure(COLUMN_K2H), figure(COLUMN_K2V)
    kxh, kxv = figure(COLUMN_KXH), figure(COLUMN_KXV)
    vl, vr = figure(COLUMN_VL), figure(COLUMN_VR)
    ht, hb = figure(COLUMN_HT), figure(COLUMN_HB)
    dh, dt, dv = figure(COLUMN_DH), figure(COLUMN_DT), figure(COLUMN_DV)
    xbr, xbl, xtr, xtl = (figure(c) for c in (COLUMN_XBR, COLUMN_XBL, COLUMN_XTR, COLUMN_XTL))
    fold_h = jnp.where(tile_row < count - tiles, 2.0, 1.0)
    fold_v = jnp.where(along < tiles - 1, 2.0, 1.0)

    def differences(x):
        return x - from_below(x), x - from_right(x)

    def corners(diff_h, diff_v):
        return (
            (vr * diff_h, hb * diff_v),
            (vl * diff_h, -from_left(hb * diff_v)),
            (-from_above(vr * diff_h), ht * diff_v),
            (-from_above(vl * diff_h), -from_left(ht * diff_v)),
        )

    def tile_product(along_h, along_v, first, second):
        value = along_h + from_above(along_h) + along_v + from_left(along_v)
        for (ah, av), (bh, bv) in zip(first, second):
            value = value + ah * bv + av * bh
        return value

    weight, *pull = tile_sums(targets)
    flat = [e - low(e) for e in pull]
    step = [differences(d) for d in flat]
    gap = [d - up(d) for d in flat]
    norm = total(flat[0] * flat[0] + flat[1] * flat[1]) * nodes
    energy = sum(kh * h * h + kv * v * v for h, v in step)
    energy = energy + nodes * weight * (gap[0] * gap[0] + gap[1] * gap[1])
    alpha = norm / total(energy)

    for k in range(2):
        sums_ref[k] = alpha * gap[k]
    look = [jnp.zeros_like(owner), jnp.zeros_like(owner)]
    for t in range(count):
        mine = owner == float(t)
        for k in range(2):
            look[k] = jnp.where(mine, sums_ref[k, t : t + 1, :], look[k])
    weight, *pull = tile_sums([look[k] - targets[k] for k in range(2)])
    weight_low = low(weight)
    const = [
        pull[k] - low(pull[k]) - alpha * (weight * gap[k] - weight_low * low(gap[k]))
        for k in range(2)
    ]
    plain = jnp.zeros_like(kh)
    mixed = jnp.zeros_like(kh)
    quad = jnp.zeros_like(kh)
    p_energy = jnp.zeros_like(kh)
    m_energy = jnp.zeros_like(kh)
    q_energy = jnp.zeros_like(kh)
    for k in range(2):
        c = const[k]
        ch, cv = differences(c)
        h, v = step[k]
        ends = corners(h, v)
        c_ends = corners(ch, cv)
        square = tile_product(k2h * h * h, k2v * v * v, ends, ends)
        across = tile_product(
            kxh * h * up(h), kxv * v * up(v), ends, [(up(a), up(b)) for a, b in ends]
        )
        gap_square = square + up(square) - 2.0 * across
        flux_h, flux_v = kh * h, kv * v
        inner = flux_h - from_above(flux_h) + flux_v - from_left(flux_v)
        gap_c = c - up(c)
        gap_q = inner - up(inner)
        plain = plain + c * c
        mixed = mixed + c * inner
        quad = quad + square
        p_energy = p_energy + kh * ch * ch + kv * cv * cv + nodes * weight * gap_c * gap_c
        m_energy = (
            m_energy
            + tile_product(k2h * ch * h, k2v * cv * v, c_ends, ends)
            + weight * gap_c * gap_q
        )
        above_h, left_v = from_above(h), from_left(v)
        value = dh * h * h + dt * above_h * above_h + dv * v * v
        value = value + 2.0 * (
            xbr * h * v + xbl * h * left_v + xtr * above_h * v + xtl * above_h * left_v
        )
        (br_h, br_v), (bl_h, bl_v), (tr_h, tr_v), (tl_h, tl_v) = ends
        for stiff, part, extra, fold in (
            (vr, br_h, br_v - from_below(tr_v), fold_h),
            (vl, bl_h, bl_v - from_below(tl_v), fold_h),
            (hb, br_v, br_h - from_right(bl_h), fold_v),
            (ht, tr_v, tr_h - from_right(tl_h), fold_v),
        ):
            value = value + stiff * extra * (2.0 * fold * part + extra)
        q_energy = q_energy + value + weight * gap_square
    norm = nodes * total(plain) - 2.0 * alpha * total(mixed) + alpha * alpha * total(quad)
    energy = total(p_energy) - 2.0 * alpha * total(m_energy) + alpha * alpha * total(q_energy)
    beta = norm / energy

    own_figures = (*flat, *const, step[0][0], step[1][0], step[0][1], step[1][1], ht, hb, weight, weight_low)
    beside = (*const, step[0][0], step[1][0], step[0][1], step[1][1])
    wanted = [(x, me) for x in own_figures] + [(x, me + 1) for x in beside] + [(x, me - 1) for x in beside]
    for n, (x, section) in enumerate(wanted):
        out_ref[n, 0:tiles, :] = zero_tiles
        out_ref[n, tiles + count : 2 * tiles + count, :] = zero_tiles
        picked = lane_sum(jnp.where(lane == section, x, 0.0))
        out_ref[n, tiles : tiles + count, :] = jnp.broadcast_to(picked, (count, sections))

    def spread(n, shift):
        start = pl.multiple_of((group + 1 + shift) * tiles, tiles)
        return out_ref[n, pl.ds(start, tiles), :]

    wide_lane = iota((rows, TILE_W), 1)
    wide_row = iota((rows, TILE_W), 0)
    first_lane, last_lane = wide_lane == 0, wide_lane == TILE_W - 1
    first_row, last_row = wide_row == 0, wide_row == rows - 1
    line_first, line_last = first_lane[0:1], last_lane[0:1]
    inside = jnp.where(group < groups - 1, 1.0, 0.0).astype(F32)

    def image(edges, offset, k, j):
        def line(n, shift=0, at=j):
            return spread(offset + n + k, shift)[at : at + 1, :]

        value = jnp.where(last_row, edges[j : j + 1, :] * line(0), 0.0)
        value = value - jnp.where(first_row, edges[tiles + j : tiles + j + 1, :] * line(0, -1), 0.0)
        columns = edges[2 * tiles : 2 * tiles + rows, :]
        value = value + jnp.where(last_lane, columns[:, j : j + 1] * line(2), 0.0)
        if j:
            value = value - jnp.where(first_lane, columns[:, j - 1 : j] * line(2, 0, j - 1), 0.0)
        return value

    own_edges, next_edges, prev_edges = own_ref[...], next_ref[...], prev_ref[...]
    for k in range(2):
        for j in range(tiles):
            span = slice(j * TILE_W, (j + 1) * TILE_W)

            def line(n, shift, at=j):
                return spread(n + k, shift)[at : at + 1, :]

            field_ref[k, tiles : tiles + rows, span] = line(2, 0) - alpha * image(own_edges, 4, k, j)
            near = -inside * own_edges[j : j + 1, :] * line(4, 0)
            near = near + jnp.where(line_last, spread(8, 1)[j : j + 1, :] * line(6, 1), 0.0)
            far = own_edges[tiles + j : tiles + j + 1, :] * line(4, -1)
            far = far + jnp.where(line_last, spread(9, -1)[j : j + 1, :] * line(6, -1), 0.0)
            if j:
                near = near - jnp.where(line_first, spread(8, 1)[j - 1 : j, :] * line(6, 1, j - 1), 0.0)
                far = far - jnp.where(line_first, spread(9, -1)[j - 1 : j, :] * line(6, -1, j - 1), 0.0)
            field_ref[k, tiles + rows : tiles + rows + 1, span] = line(2, 1) - alpha * near
            field_ref[k, tiles - 1 : tiles, span] = line(2, -1) - alpha * far
    weight_rows, weight_low_rows = spread(10, 0), spread(11, 0)
    for k in range(2):
        flux_left = None
        for j in range(tiles):
            span = slice(j * TILE_W, (j + 1) * TILE_W)
            r = field_ref[k, tiles : tiles + rows, span]
            right = pltpu.roll(r, TILE_W - 1, 1)
            if j < tiles - 1:
                beyond = field_ref[k, tiles : tiles + rows, (j + 1) * TILE_W : (j + 2) * TILE_W]
                right = jnp.where(last_lane, pltpu.roll(beyond, TILE_W - 1, 1), right)
            else:
                right = jnp.where(last_lane, 0.0, right)
            flux = hori_ref[:, span] * (r - right)
            turned = pltpu.roll(flux, 1, 1)
            before = jnp.where(first_lane, 0.0 if flux_left is None else flux_left, turned)
            flux_left = turned
            below = field_ref[k, tiles + 1 : tiles + rows + 1, span]
            fall = vert_ref[:, span] * (r - below)
            edge = own_edges[tiles + j : tiles + j + 1, :] * (field_ref[k, tiles - 1 : tiles, span] - r[0:1, :])
            fall_above = jnp.where(first_row, edge, pltpu.roll(fall, 1, 0))
            applied = flux - before + fall - fall_above
            r_next = spread(12 + k, 0)[j : j + 1, :] - alpha * image(next_edges, 14, k, j)
            r_prev = spread(18 + k, 0)[j : j + 1, :] - alpha * image(prev_edges, 20, k, j)
            applied = applied + weight_rows[j : j + 1, :] * (r - r_next) + weight_low_rows[j : j + 1, :] * (r - r_prev)
            disp_ref[k, :, span] = alpha * spread(k, 0)[j : j + 1, :] + beta * r
            res_ref[k, :, span] = r - beta * applied


def from_behind(block, axis, distance):
    devices = range(lax.axis_size(axis))
    route = [(i - distance, i) for i in devices if i - distance in devices]
    return lax.ppermute(block, axis, route)


def gather(block, axis):
    size = lax.axis_size(axis)
    copies = jnp.broadcast_to(block[None], (size,) + block.shape)
    return lax.all_to_all(copies, axis, 0, 0, tiled=True)


def body(fixed_desc, moving_desc, offsets, owner, counts, vert, hori):
    groups = lax.axis_size("group")
    sections = lax.axis_size(SEC)
    chips_z = lax.axis_size("z")
    group = lax.axis_index("group")
    section = lax.axis_index(SEC)
    patches, flow, corr = fixed_desc.shape[1:]
    half = patches // 2
    rows, cols = vert.shape[1:]
    tiles = cols // TILE_W
    vert, hori = vert[0], hori[0]

    moving_near = from_behind(moving_desc[0, :half], SEC, -1)
    fixed_far = from_behind(fixed_desc[0, half:], SEC, 1)
    shifts = offsets[0].astype(F32).reshape(patches * 2, offsets.shape[-1])
    shifts_far = from_behind(shifts[patches:], SEC, 1)
    above = from_behind(vert[rows - 1 :], "group", 1).reshape(tiles, TILE_W)
    edge_rows = 2 * tiles + rows
    edges = pl.pallas_call(
        edge_kernel, out_shape=jax.ShapeDtypeStruct((edge_rows, TILE_W), F32), name="edges"
    )(vert, hori, above)
    edges_next = from_behind(edges, SEC, -1)
    edges_prev = from_behind(edges, SEC, 1)

    live = jnp.where(jnp.arange(patches) < counts[0, 0], owner[0], -1).astype(F32)
    owners = jnp.pad(
        live.reshape(2, half).T, ((0, 0), (COLUMN_OWNER, TILE_W - COLUMN_OWNER - 2))
    )
    table = pl.pallas_call(
        border_kernel,
        out_shape=jax.ShapeDtypeStruct((tiles, TILE_W), F32),
        in_specs=[pl.BlockSpec(memory_space=pltpu.SMEM)] + [pl.BlockSpec(memory_space=pltpu.VMEM)] * 5,
        scratch_shapes=[pltpu.VMEM((TILE_W, TILE_W), F32)],
        name="borders",
    )(jnp.stack([group, jnp.int32(groups - 1)]).astype(jnp.int32), vert, hori, edges, edges_next, owners)

    def match(column, last, fixed, moving, part, known):
        def features(x):
            if x.ndim == 4:
                which = part[0] if x is fixed else part[1]
                return pl.BlockSpec((pl.Squeezed(), half, flow, corr), lambda i, w=which: (0, w, 0, 0))
            return pl.BlockSpec((half, flow, corr), lambda i: (0, 0, 0))

        shape = (tiles * GROUP_LANES // TILE_W if last else tiles, TILE_W)

        def kernel(*refs):
            match_kernel(column, last, *refs)

        return pl.pallas_call(
            kernel,
            grid=(1,),
            out_shape=jax.ShapeDtypeStruct(shape, F32),
            in_specs=[
                features(fixed),
                features(moving),
                pl.BlockSpec((patches, offsets.shape[-1]), lambda i: (0, 0)),
                pl.BlockSpec((tiles, TILE_W), lambda i: (0, 0)),
            ],
            out_specs=pl.BlockSpec(shape, lambda i: (0, 0)),
            name="match_far" if last else "match_near",
        )(fixed, moving, shifts[:patches] if not last else shifts_far, known)

    table = match(COLUMN_NEAR, False, fixed_desc, moving_near, (0, 0), table)
    mine = match(COLUMN_FAR, True, fixed_far, moving_desc, (0, 1), table)

    seen = gather(mine, "z").reshape(-1, TILE_W)
    seen = gather(seen, ("group", "y")).reshape(-1, TILE_W)
    seen = lax.all_gather(seen, "core", axis=0, tiled=True)

    dims = (groups, sections, rows, tiles, chips_z)
    halves = tiles * GROUP_LANES // TILE_W
    count = groups * tiles

    def both_iterations(*refs):
        stack_kernel(dims, *refs)

    field = jax.ShapeDtypeStruct((2, rows, cols), F32)
    displacement, residual = pl.pallas_call(
        both_iterations,
        out_shape=(field, field),
        in_specs=[pl.BlockSpec(memory_space=pltpu.SMEM)] + [pl.BlockSpec(memory_space=pltpu.VMEM)] * 6,
        scratch_shapes=[
            pltpu.VMEM((groups * halves, sections, TILE_W), F32),
            pltpu.VMEM((groups, halves * TILE_W, sections), F32),
            pltpu.VMEM((3, count, sections), F32),
            pltpu.VMEM((24, count + 2 * tiles, sections), F32),
            pltpu.VMEM((2, rows + 2 * tiles, cols), F32),
        ],
        compiler_params=pltpu.CompilerParams(vmem_limit_bytes=32 << 20),
        name="stack",
    )(jnp.stack([section, group]).astype(jnp.int32), seen, vert, hori, edges, edges_next, edges_prev)
    return (displacement[None], residual[None])


def solution(mesh):
    groups, sections = mesh.devices.shape
    devices = mesh.devices.reshape(groups, sections // (CHIPS_Y * CORES), CHIPS_Y, CORES)
    fine = Mesh(devices, ("group",) + SEC)
    in_specs = (
        P(SEC, "group", None, None),
        P(SEC, "group", None, None),
        P(SEC, "group", None, None),
        P(SEC, "group"),
        P(SEC, "group"),
        P(SEC, "group", None),
        P(SEC, "group", None),
    )
    out_specs = (P(SEC, None, "group", None), P(SEC, None, "group", None))
    return jax.shard_map(body, mesh=fine, in_specs=in_specs, out_specs=out_specs, check_vma=False)
```

```python
import math

import jax
import jax.numpy as jnp
from jax import lax
from jax.experimental import pallas as pl
from jax.experimental.pallas import tpu as pltpu
from jax.sharding import Mesh, PartitionSpec as P

TILE_W = 128
SPREAD_SQ = 4.0
CHIPS_Y = 4
CORES = 2
SEC = ("z", "y", "core")
F32 = jnp.float32

COLUMN_KV, COLUMN_K2V, COLUMN_KXV, COLUMN_VL, COLUMN_VR, COLUMN_HT, COLUMN_HB = range(7)
COLUMN_DV, COLUMN_XBR, COLUMN_XBL, COLUMN_XTR, COLUMN_XTL = range(7, 12)
COLUMN_KH, COLUMN_K2H, COLUMN_KXH, COLUMN_DH, COLUMN_DT = range(12, 17)
COLUMN_OWNER = 17
COLUMN_NEAR = 19
COLUMN_FAR = 21
GROUP_LANES = 32
PARTS = 4


def iota(shape, axis):
    return lax.broadcasted_iota(jnp.int32, shape, axis)


def lane_sum(x):
    return jnp.sum(x, axis=1, keepdims=True)


def row_sum(x):
    return jnp.sum(x, axis=0, keepdims=True)


def total(x):
    return lane_sum(row_sum(x))


def three_parts(x):
    high = x.astype(jnp.bfloat16).astype(F32)
    middle = (x - high).astype(jnp.bfloat16).astype(F32)
    return high, middle, x - high - middle


def pack_kernel(
    moving_ref, fixed_ref, vert_ref, hori_ref, offsets_ref, near_ref, far_ref, line_ref,
    vert, hori, offsets, extra, sems,
):
    rows, cols = hori.shape
    tiles = cols // TILE_W
    length = moving_ref.shape[0] // 2
    part = length // PARTS
    copies = []
    for n in range(PARTS):
        at = pl.ds(n * part, part)
        copies.append(pltpu.make_async_copy(moving_ref.at[at], near_ref.at[at], sems.at[2 * n]))
        behind = pl.ds(length + n * part, part)
        copies.append(pltpu.make_async_copy(fixed_ref.at[behind], far_ref.at[at], sems.at[2 * n + 1]))
    first = 2 * PARTS
    loads = [
        pltpu.make_async_copy(vert_ref.at[0], vert, sems.at[first]),
        pltpu.make_async_copy(hori_ref.at[0], hori, sems.at[first + 1]),
        pltpu.make_async_copy(offsets_ref.at[0], offsets, sems.at[first + 2]),
    ]
    for copy in copies + loads:
        copy.start()
    for copy in loads:
        copy.wait()
    lane = iota((rows, TILE_W), 1)
    column = jnp.zeros((rows, TILE_W), F32)
    for j in range(tiles):
        span = slice(j * TILE_W, (j + 1) * TILE_W)
        line_ref[j : j + 1, :] = vert[rows - 1 : rows, span]
        end = (j + 1) * TILE_W - 1
        column = jnp.where(lane == j, hori[:, end : end + 1], column)
    high, middle, small = three_parts(column)
    columns = high + pltpu.roll(middle, tiles, 1) + pltpu.roll(small, 2 * tiles, 1)
    half = offsets.shape[0] // 2
    shifts = jnp.concatenate([offsets[half:, 0, :], offsets[half:, 1, :]], 1).astype(F32)
    blank = jnp.zeros((tiles, TILE_W), F32)
    for n, value in enumerate(three_parts(line_ref[...])):
        span = slice(n * TILE_W, (n + 1) * TILE_W)
        extra[0, :, span] = jnp.concatenate([value, blank], 0).astype(jnp.bfloat16)
        extra[1, :, span] = jnp.concatenate([value, blank if n else shifts], 0).astype(jnp.bfloat16)
    for n in range(2):
        extra[n, :, 3 * TILE_W :] = columns.astype(jnp.bfloat16)
    tail = [
        pltpu.make_async_copy(extra.at[n], ref.at[pl.ds(length, rows)], sems.at[first + 3 + n])
        for n, ref in enumerate((near_ref, far_ref))
    ]
    for copy in tail:
        copy.start()
    for copy in copies + tail:
        copy.wait()


def unpack(extra, tiles):
    parts = [extra[:, n * TILE_W : (n + 1) * TILE_W].astype(F32) for n in range(4)]
    line = parts[0][:tiles] + (parts[1][:tiles] + parts[2][:tiles])
    columns = parts[3]
    back = TILE_W - tiles
    columns = columns + (pltpu.roll(columns, back, 1) + pltpu.roll(columns, back - tiles, 1))
    return line, columns, parts[0][tiles:]


def border_kernel(groups, owner_ref, counts_ref, vert_ref, hori_ref, line_ref, above_ref, out_ref, stack):
    rows, cols = hori_ref.shape
    tiles = cols // TILE_W
    last_group = lax.axis_index("group") == groups - 1
    bottom = jnp.where(last_group, 1.0, 4.0).astype(F32)

    v_last = line_ref[...]
    v_above = above_ref[...]
    for j in range(tiles):
        span = slice(j * TILE_W, (j + 1) * TILE_W)
        stack[j : j + 1, :] = vert_ref[rows - 2 : rows - 1, span]
        stack[tiles + j : tiles + j + 1, :] = vert_ref[0:1, span]
        stack[2 * tiles + j : 2 * tiles + j + 1, :] = hori_ref[rows - 1 : rows, span]
        stack[3 * tiles + j : 3 * tiles + j + 1, :] = hori_ref[0:1, span]
    v_second, v_first = stack[0:tiles, :], stack[tiles : 2 * tiles, :]
    h_last, h_first = stack[2 * tiles : 3 * tiles, :], stack[3 * tiles : 4 * tiles, :]
    lane = iota((tiles, TILE_W), 1)
    inside = lane < TILE_W - 1
    square = v_last * v_last
    step_last = v_last - pltpu.roll(v_last, TILE_W - 1, 1)
    step_above = v_above - pltpu.roll(v_above, TILE_W - 1, 1)
    dh = lane_sum(
        bottom * square * v_last
        + v_second * square
        + jnp.where(inside, h_last * step_last * step_last, 0.0)
    )
    dt = lane_sum(
        v_first * v_above * v_above + jnp.where(inside, h_first * step_above * step_above, 0.0)
    )
    sub = iota((tiles, TILE_W), 0)
    table = jnp.zeros((tiles, TILE_W), F32)
    for p in range(owner_ref.shape[1]):
        live = jnp.where(p < counts_ref[0, 0], owner_ref[0, p], -1).astype(F32)
        spot = (sub == p % tiles) & (lane == COLUMN_OWNER + p // tiles)
        table = jnp.where(spot, live, table)
    for column, value in (
        (COLUMN_KH, lane_sum(v_last)),
        (COLUMN_K2H, lane_sum(square)),
        (COLUMN_DH, dh),
        (COLUMN_DT, dt),
    ):
        table = jnp.where(lane == column, value, table)

    tall = iota((rows, TILE_W), 1)
    zero = jnp.zeros((rows, TILE_W), F32)
    picked = {}
    for name, ref, column in (
        ("h127", hori_ref, TILE_W - 1),
        ("h0", hori_ref, 0),
        ("h126", hori_ref, TILE_W - 2),
        ("v0", vert_ref, 0),
        ("v1", vert_ref, 1),
        ("v126", vert_ref, TILE_W - 2),
        ("v127", vert_ref, TILE_W - 1),
    ):
        value = zero
        for j in range(tiles):
            at = j * TILE_W + column
            value = jnp.where(tall == j, ref[:, at : at + 1], value)
        picked[name] = value
    wide = iota((tiles, TILE_W), 0)
    diagonal = iota((tiles, TILE_W), 1) == wide

    def above_at(column):
        return row_sum(jnp.where(diagonal, v_above[:, column : column + 1], 0.0))

    a0, a1 = above_at(0), above_at(1)
    a126, a127 = above_at(TILE_W - 2), above_at(TILE_W - 1)
    right = picked["h127"]
    left = pltpu.roll(right, 1, 1)
    row = iota((rows, TILE_W), 0)
    within = row < rows - 1
    inner_tile = iota((1, TILE_W), 1) < tiles - 1
    step_right = right - pltpu.roll(right, rows - 1, 0)
    step_left = left - pltpu.roll(left, rows - 1, 0)
    right_sq, left_sq = right * right, left * left
    side_right = row_sum(
        picked["h126"] * right_sq + jnp.where(within, picked["v127"] * step_right * step_right, 0.0)
    )
    side_left = row_sum(
        picked["h0"] * left_sq + jnp.where(within, picked["v0"] * step_left * step_left, 0.0)
    )
    cube = row_sum(right_sq * right)
    dv = side_right + jnp.where(
        inner_tile, pltpu.roll(side_left, TILE_W - 1, 1) + 4.0 * cube, cube
    )
    end, pre = rows - 1, rows - 2
    v0, v1, v126, v127 = (picked[n] for n in ("v0", "v1", "v126", "v127"))
    h0, h126 = picked["h0"], picked["h126"]

    def at(x, r):
        return x[r : r + 1, :]

    xbr = at(h126, end) * (at(v127, end) - at(v126, end)) * at(right, end) + at(v127, pre) * at(
        v127, end
    ) * (at(right, end) - at(right, pre))
    xbl = -(
        at(h0, end) * (at(v0, end) - at(v1, end)) * at(left, end)
        + at(v0, pre) * at(v0, end) * (at(left, end) - at(left, pre))
    )
    xtr = -(
        at(h126, 0) * (a127 - a126) * at(right, 0)
        + at(v127, 0) * a127 * (at(right, 0) - at(right, 1))
    )
    xtl = at(h0, 0) * (a0 - a1) * at(left, 0) + at(v0, 0) * a0 * (at(left, 0) - at(left, 1))
    stack[...] = jnp.zeros_like(stack)
    for column, value in (
        (COLUMN_KV, row_sum(right)),
        (COLUMN_K2V, row_sum(right_sq)),
        (COLUMN_VL, at(v0, end)),
        (COLUMN_VR, at(v127, end)),
        (COLUMN_HT, at(right, 0)),
        (COLUMN_HB, at(right, end)),
        (COLUMN_DV, dv),
        (COLUMN_XBR, xbr),
        (COLUMN_XBL, xbl),
        (COLUMN_XTR, xtr),
        (COLUMN_XTL, xtl),
    ):
        stack[column : column + 1, :] = value
    turned = jnp.transpose(stack[...])[0:tiles, :]
    out_ref[...] = jnp.where(lane <= COLUMN_XTL, turned, table)


def match_kernel(
    fixed_ref, moving_ref, offsets_ref, table_ref, line_ref, hori_ref, near_ref, far_ref,
    out_ref, next_line_ref, next_columns_ref, prev_line_ref, prev_columns_ref,
    near, far, scores_ref, sems,
):
    patches, flow, corr = fixed_ref.shape[1:]
    half = patches // 2
    length = half * flow
    part = length // PARTS
    rows, cols = hori_ref.shape[-2:]
    tiles = cols // TILE_W
    pair = 2 * flow
    arrivals = [
        pltpu.make_async_copy(near_ref.at[pl.ds(length, rows)], near.at[pl.ds(length, rows)], sems.at[2 * PARTS]),
        pltpu.make_async_copy(far_ref.at[pl.ds(length, rows)], far.at[pl.ds(length, rows)], sems.at[2 * PARTS + 1]),
    ]
    loads = []
    for side, (source, target) in enumerate(((near_ref, near), (far_ref, far))):
        for n in range(PARTS):
            at = pl.ds(n * part, part)
            loads.append(pltpu.make_async_copy(source.at[at], target.at[at], sems.at[side * PARTS + n]))
    for copy in loads + arrivals:
        copy.start()

    lower = iota((flow, pair), 1) < flow
    for side in range(2):
        for n in range(PARTS):
            loads[side * PARTS + n].wait()
            for first in range(n * half // PARTS, (n + 1) * half // PARTS, 2):
                at = slice(first * flow, (first + 2) * flow)
                if side == 0:
                    fixed = fixed_ref[0, first : first + 2].reshape(pair, corr)
                    moving = near[at, :]
                else:
                    fixed = far[at, :]
                    moving = moving_ref[0, half + first : half + first + 2].reshape(pair, corr)
                scores = lax.dot_general(
                    moving, fixed, (((1,), (1,)), ((), ())), preferred_element_type=F32
                )
                both = jnp.where(lower, scores[0:flow, :], scores[flow:pair, :])
                scores_ref[side, :, at] = both
    for copy in arrivals:
        copy.wait()
    next_line, next_columns, _ = unpack(near[length : length + rows, :], tiles)
    prev_line, prev_columns, shifts = unpack(far[length : length + rows, :], tiles)
    next_line_ref[...] = next_line
    next_columns_ref[...] = next_columns
    prev_line_ref[...] = prev_line
    prev_columns_ref[...] = prev_columns

    table = table_ref[...]
    lane = iota(table.shape, 1)
    own_shifts = [offsets_ref[0, 0:half, k, :].astype(F32) for k in range(2)]
    far_shifts = [shifts[:, 0:flow], shifts[:, flow:pair]]
    scale = 1.0 / math.sqrt(corr)
    slot = lax.rem(iota((2 * half, length), 0), half)
    mine = slot == lax.div(iota((2 * half, length), 1), flow)
    for side, offsets in enumerate((own_shifts, far_shifts)):
        both = scores_ref[side]
        top = jnp.max(both, axis=0, keepdims=True)
        likely = jnp.exp((both - top) * scale)
        sums = lax.dot_general(
            jnp.concatenate(offsets, 0),
            likely,
            (((1,), (0,)), ((), ())),
            precision=lax.Precision.HIGHEST,
            preferred_element_type=F32,
        )
        weight = row_sum(likely)
        ratio = lane_sum(jnp.where(mine, sums, 0.0) / (weight * flow))
        for k in range(2):
            column = (COLUMN_FAR if side else COLUMN_NEAR) + k
            table = jnp.where(lane == column, ratio[k * half : (k + 1) * half], table)

    table = jnp.where(lane == COLUMN_KXH, lane_sum(line_ref[...] * next_line), table)
    diagonal = iota(table.shape, 0) == lane
    columns = jnp.zeros((rows, TILE_W), F32)
    tall = iota((rows, TILE_W), 1)
    for j in range(tiles):
        end = (j + 1) * TILE_W - 1
        columns = jnp.where(tall == j, hori_ref[:, end : end + 1], columns)
    across = row_sum(columns * next_columns)
    table = jnp.where(lane == COLUMN_KXV, lane_sum(jnp.where(diagonal, across, 0.0)), table)

    table = jnp.where(lane < GROUP_LANES, table, 0.0)
    per_row = TILE_W // GROUP_LANES
    for part in range(tiles // per_row):
        line = jnp.zeros((1, TILE_W), F32)
        for j in range(per_row):
            source = table[part * per_row + j : part * per_row + j + 1, :]
            line = line + (pltpu.roll(source, j * GROUP_LANES, 1) if j else source)
        for n in range(out_ref.shape[0]):
            out_ref[n, part : part + 1, :] = line


def stack_kernel(
    dims, seen_ref, vert_ref, hori_ref, own_line_ref, own_above_ref,
    next_line_ref, next_above_ref, next_columns_ref, prev_line_ref, prev_above_ref, prev_columns_ref,
    disp_ref, res_ref, rows_ref, turn_ref, sums_ref, out_ref, field_ref,
):
    groups, sections, rows, tiles, chips_z = dims
    per_chip = sections // chips_z
    halves = tiles * GROUP_LANES // TILE_W
    count = groups * tiles
    nodes = float(rows * TILE_W)
    me, group = lax.axis_index(SEC), lax.axis_index("group")

    for core in range(CORES):
        for g in range(groups):
            for y in range(per_chip // CORES):
                base = ((core * groups + g) * (per_chip // CORES) + y) * chips_z * halves
                for h in range(halves):
                    rows_ref[g * halves + h, pl.ds(y * CORES + core, chips_z, stride=per_chip), :] = seen_ref[
                        pl.ds(base + h, chips_z, stride=halves), :
                    ]
    for g in range(groups):
        for h in range(halves):
            turn_ref[g, h * TILE_W : (h + 1) * TILE_W, :] = jnp.transpose(rows_ref[g * halves + h])

    def block(g, column):
        return turn_ref[g, pl.ds(column, tiles, stride=GROUP_LANES), :]

    def figure(column):
        return jnp.concatenate([block(g, column) for g in range(groups)], 0)

    def slots(near, far, turn):
        parts = []
        for g in range(groups):
            parts.append(block(g, near))
            other = block(g, far)
            parts.append(pltpu.roll(other, sections - 1, 1) if turn else other)
        return jnp.concatenate(parts, 0)

    lane = iota((count, sections), 1)
    tile_row = iota((count, sections), 0)
    along = lax.rem(tile_row, tiles)
    not_last = lane < sections - 1

    def up(x):
        return jnp.where(not_last, pltpu.roll(x, sections - 1, 1), 0.0)

    def low(x):
        return jnp.where(lane > 0, pltpu.roll(x, 1, 1), 0.0)

    zero_tiles = jnp.zeros((tiles, sections), F32)

    def from_above(x):
        return jnp.concatenate([zero_tiles, x[: count - tiles]], 0)

    def from_below(x):
        return jnp.concatenate([x[tiles:], zero_tiles], 0)

    def from_left(x):
        return jnp.where(along > 0, pltpu.roll(x, 1, 0), 0.0)

    def from_right(x):
        return jnp.where(along < tiles - 1, pltpu.roll(x, count - 1, 0), 0.0)

    owner = slots(COLUMN_OWNER, COLUMN_OWNER + 1, False)
    targets = [slots(COLUMN_NEAR + k, COLUMN_FAR + k, True) for k in range(2)]
    valid = jnp.where(owner >= 0.0, 1.0, 0.0)

    def tile_sums(miss):
        weight = valid / (1.0 + (miss[0] * miss[0] + miss[1] * miss[1]) / SPREAD_SQ)
        terms = (weight, weight * targets[0], weight * targets[1])
        for t in range(count):
            mine = owner == float(t)
            for n, term in enumerate(terms):
                sums_ref[n, t : t + 1, :] = row_sum(jnp.where(mine, term, 0.0))
        return [jnp.where(not_last, sums_ref[n], 0.0) for n in range(3)]

    kh, kv = figure(COLUMN_KH), figure(COLUMN_KV)
    k2h, k2v = figure(COLUMN_K2H), figure(COLUMN_K2V)
    kxh, kxv = figure(COLUMN_KXH), figure(COLUMN_KXV)
    vl, vr = figure(COLUMN_VL), figure(COLUMN_VR)
    ht, hb = figure(COLUMN_HT), figure(COLUMN_HB)
    dh, dt, dv = figure(COLUMN_DH), figure(COLUMN_DT), figure(COLUMN_DV)
    xbr, xbl, xtr, xtl = (figure(c) for c in (COLUMN_XBR, COLUMN_XBL, COLUMN_XTR, COLUMN_XTL))
    fold_h = jnp.where(tile_row < count - tiles, 2.0, 1.0)
    fold_v = jnp.where(along < tiles - 1, 2.0, 1.0)

    def differences(x):
        return x - from_below(x), x - from_right(x)

    def corners(diff_h, diff_v):
        return (
            (vr * diff_h, hb * diff_v),
            (vl * diff_h, -from_left(hb * diff_v)),
            (-from_above(vr * diff_h), ht * diff_v),
            (-from_above(vl * diff_h), -from_left(ht * diff_v)),
        )

    def tile_product(along_h, along_v, first, second):
        value = along_h + from_above(along_h) + along_v + from_left(along_v)
        for (ah, av), (bh, bv) in zip(first, second):
            value = value + ah * bv + av * bh
        return value

    weight, *pull = tile_sums(targets)
    flat = [e - low(e) for e in pull]
    step = [differences(d) for d in flat]
    gap = [d - up(d) for d in flat]
    norm = total(flat[0] * flat[0] + flat[1] * flat[1]) * nodes
    energy = sum(kh * h * h + kv * v * v for h, v in step)
    energy = energy + nodes * weight * (gap[0] * gap[0] + gap[1] * gap[1])
    alpha = norm / total(energy)

    for k in range(2):
        sums_ref[k] = alpha * gap[k]
    look = [jnp.zeros_like(owner), jnp.zeros_like(owner)]
    for t in range(count):
        mine = owner == float(t)
        for k in range(2):
            look[k] = jnp.where(mine, sums_ref[k, t : t + 1, :], look[k])
    weight, *pull = tile_sums([look[k] - targets[k] for k in range(2)])
    weight_low = low(weight)
    const = [
        pull[k] - low(pull[k]) - alpha * (weight * gap[k] - weight_low * low(gap[k]))
        for k in range(2)
    ]
    plain = jnp.zeros_like(kh)
    mixed = jnp.zeros_like(kh)
    quad = jnp.zeros_like(kh)
    p_energy = jnp.zeros_like(kh)
    m_energy = jnp.zeros_like(kh)
    q_energy = jnp.zeros_like(kh)
    for k in range(2):
        c = const[k]
        ch, cv = differences(c)
        h, v = step[k]
        ends = corners(h, v)
        c_ends = corners(ch, cv)
        square = tile_product(k2h * h * h, k2v * v * v, ends, ends)
        across = tile_product(
            kxh * h * up(h), kxv * v * up(v), ends, [(up(a), up(b)) for a, b in ends]
        )
        gap_square = square + up(square) - 2.0 * across
        flux_h, flux_v = kh * h, kv * v
        inner = flux_h - from_above(flux_h) + flux_v - from_left(flux_v)
        gap_c = c - up(c)
        gap_q = inner - up(inner)
        plain = plain + c * c
        mixed = mixed + c * inner
        quad = quad + square
        p_energy = p_energy + kh * ch * ch + kv * cv * cv + nodes * weight * gap_c * gap_c
        m_energy = (
            m_energy
            + tile_product(k2h * ch * h, k2v * cv * v, c_ends, ends)
            + weight * gap_c * gap_q
        )
        above_h, left_v = from_above(h), from_left(v)
        value = dh * h * h + dt * above_h * above_h + dv * v * v
        value = value + 2.0 * (
            xbr * h * v + xbl * h * left_v + xtr * above_h * v + xtl * above_h * left_v
        )
        (br_h, br_v), (bl_h, bl_v), (tr_h, tr_v), (tl_h, tl_v) = ends
        for stiff, part, extra, fold in (
            (vr, br_h, br_v - from_below(tr_v), fold_h),
            (vl, bl_h, bl_v - from_below(tl_v), fold_h),
            (hb, br_v, br_h - from_right(bl_h), fold_v),
            (ht, tr_v, tr_h - from_right(tl_h), fold_v),
        ):
            value = value + stiff * extra * (2.0 * fold * part + extra)
        q_energy = q_energy + value + weight * gap_square
    norm = nodes * total(plain) - 2.0 * alpha * total(mixed) + alpha * alpha * total(quad)
    energy = total(p_energy) - 2.0 * alpha * total(m_energy) + alpha * alpha * total(q_energy)
    beta = norm / energy

    own_figures = (*flat, *const, step[0][0], step[1][0], step[0][1], step[1][1], ht, hb, weight, weight_low)
    beside = (*const, step[0][0], step[1][0], step[0][1], step[1][1])
    wanted = [(x, me) for x in own_figures] + [(x, me + 1) for x in beside] + [(x, me - 1) for x in beside]
    for n, (x, section) in enumerate(wanted):
        out_ref[n, 0:tiles, :] = zero_tiles
        out_ref[n, tiles + count : 2 * tiles + count, :] = zero_tiles
        picked = lane_sum(jnp.where(lane == section, x, 0.0))
        out_ref[n, tiles : tiles + count, :] = jnp.broadcast_to(picked, (count, sections))

    def spread(n, shift):
        start = pl.multiple_of((group + 1 + shift) * tiles, tiles)
        return out_ref[n, pl.ds(start, tiles), :]

    wide_lane = iota((rows, TILE_W), 1)
    wide_row = iota((rows, TILE_W), 0)
    first_lane, last_lane = wide_lane == 0, wide_lane == TILE_W - 1
    first_row, last_row = wide_row == 0, wide_row == rows - 1
    line_first, line_last = first_lane[0:1], last_lane[0:1]
    inside = jnp.where(group < groups - 1, 1.0, 0.0).astype(F32)

    def image(edges, offset, k, j):
        last_line, above_line, columns = edges
        def line(n, shift=0, at=j):
            return spread(offset + n + k, shift)[at : at + 1, :]

        value = jnp.where(last_row, last_line[j : j + 1, :] * line(0), 0.0)
        value = value - jnp.where(first_row, above_line[j : j + 1, :] * line(0, -1), 0.0)
        value = value + jnp.where(last_lane, columns(j) * line(2), 0.0)
        if j:
            value = value - jnp.where(first_lane, columns(j - 1) * line(2, 0, j - 1), 0.0)
        return value

    own_line, own_above = own_line_ref[...], own_above_ref[...]
    next_columns, prev_columns = next_columns_ref[...], prev_columns_ref[...]
    own_edges = (own_line, own_above, lambda j: hori_ref[:, (j + 1) * TILE_W - 1 : (j + 1) * TILE_W])
    next_edges = (next_line_ref[...], next_above_ref[...], lambda j: next_columns[:, j : j + 1])
    prev_edges = (prev_line_ref[...], prev_above_ref[...], lambda j: prev_columns[:, j : j + 1])
    for k in range(2):
        for j in range(tiles):
            span = slice(j * TILE_W, (j + 1) * TILE_W)

            def line(n, shift, at=j):
                return spread(n + k, shift)[at : at + 1, :]

            field_ref[k, tiles : tiles + rows, span] = line(2, 0) - alpha * image(own_edges, 4, k, j)
            near = -inside * own_line[j : j + 1, :] * line(4, 0)
            near = near + jnp.where(line_last, spread(8, 1)[j : j + 1, :] * line(6, 1), 0.0)
            far = own_above[j : j + 1, :] * line(4, -1)
            far = far + jnp.where(line_last, spread(9, -1)[j : j + 1, :] * line(6, -1), 0.0)
            if j:
                near = near - jnp.where(line_first, spread(8, 1)[j - 1 : j, :] * line(6, 1, j - 1), 0.0)
                far = far - jnp.where(line_first, spread(9, -1)[j - 1 : j, :] * line(6, -1, j - 1), 0.0)
            field_ref[k, tiles + rows : tiles + rows + 1, span] = line(2, 1) - alpha * near
            field_ref[k, tiles - 1 : tiles, span] = line(2, -1) - alpha * far
    weight_rows, weight_low_rows = spread(10, 0), spread(11, 0)
    for k in range(2):
        flux_left = None
        for j in range(tiles):
            span = slice(j * TILE_W, (j + 1) * TILE_W)
            r = field_ref[k, tiles : tiles + rows, span]
            right = pltpu.roll(r, TILE_W - 1, 1)
            if j < tiles - 1:
                beyond = field_ref[k, tiles : tiles + rows, (j + 1) * TILE_W : (j + 2) * TILE_W]
                right = jnp.where(last_lane, pltpu.roll(beyond, TILE_W - 1, 1), right)
            else:
                right = jnp.where(last_lane, 0.0, right)
            flux = hori_ref[:, span] * (r - right)
            turned = pltpu.roll(flux, 1, 1)
            before = jnp.where(first_lane, 0.0 if flux_left is None else flux_left, turned)
            flux_left = turned
            below = field_ref[k, tiles + 1 : tiles + rows + 1, span]
            fall = vert_ref[:, span] * (r - below)
            edge = own_above[j : j + 1, :] * (field_ref[k, tiles - 1 : tiles, span] - r[0:1, :])
            fall_above = jnp.where(first_row, edge, pltpu.roll(fall, 1, 0))
            applied = flux - before + fall - fall_above
            r_next = spread(12 + k, 0)[j : j + 1, :] - alpha * image(next_edges, 14, k, j)
            r_prev = spread(18 + k, 0)[j : j + 1, :] - alpha * image(prev_edges, 20, k, j)
            applied = applied + weight_rows[j : j + 1, :] * (r - r_next) + weight_low_rows[j : j + 1, :] * (r - r_prev)
            disp_ref[k, :, span] = alpha * spread(k, 0)[j : j + 1, :] + beta * r
            res_ref[k, :, span] = r - beta * applied


def from_behind(block, axis, distance):
    devices = range(lax.axis_size(axis))
    route = [(i - distance, i) for i in devices if i - distance in devices]
    return lax.ppermute(block, axis, route)


def from_above(block, distance):
    groups, sections = lax.axis_size("group"), lax.axis_size(SEC)
    route = [
        ((g - 1) * sections + s - distance, g * sections + s)
        for g in range(1, groups)
        for s in range(sections)
        if 0 <= s - distance < sections
    ]
    return lax.ppermute(block, ("group",) + SEC, route)


def gather(block, axis):
    size = lax.axis_size(axis)
    copies = jnp.broadcast_to(block[None], (size,) + block.shape)
    return lax.all_to_all(copies, axis, 0, 0, tiled=True)


def body(fixed_desc, moving_desc, offsets, owner, counts, vert, hori):
    groups = lax.axis_size("group")
    sections = lax.axis_size(SEC)
    chips_z = lax.axis_size("z")
    patches, flow, corr = fixed_desc.shape[1:]
    rows, cols = vert.shape[1:]
    tiles = cols // TILE_W
    length = patches * flow
    halves = tiles * GROUP_LANES // TILE_W

    anywhere = pl.BlockSpec(memory_space=pl.ANY)
    hbm = pl.BlockSpec(memory_space=pltpu.HBM)
    local = pl.BlockSpec(memory_space=pltpu.VMEM)
    scalars = pl.BlockSpec(memory_space=pltpu.SMEM)
    packed = jax.ShapeDtypeStruct((length // 2 + rows, corr), fixed_desc.dtype)
    border = jax.ShapeDtypeStruct((tiles, TILE_W), F32)
    upright = jax.ShapeDtypeStruct((rows, TILE_W), F32)
    near, far, line = pl.pallas_call(
        pack_kernel,
        out_shape=(packed, packed, border),
        in_specs=[hbm] * 5,
        out_specs=(anywhere, anywhere, local),
        scratch_shapes=[
            pltpu.VMEM((rows, cols), F32),
            pltpu.VMEM((rows, cols), F32),
            pltpu.VMEM(offsets.shape[1:], jnp.int32),
            pltpu.VMEM((2, rows, corr), fixed_desc.dtype),
            pltpu.SemaphoreType.DMA((2 * PARTS + 5,)),
        ],
        name="pack",
    )(moving_desc.reshape(length, corr), fixed_desc.reshape(length, corr), vert, hori, offsets)
    near = from_behind(near, SEC, -1)
    far = from_behind(far, SEC, 1)
    above = from_above(line, 0)
    next_above = from_above(line, -1)
    prev_above = from_above(line, 1)

    vert, hori = vert[0], hori[0]

    def borders(*refs):
        border_kernel(groups, *refs)

    table = pl.pallas_call(
        borders,
        out_shape=border,
        in_specs=[scalars] * 2 + [local] * 4,
        scratch_shapes=[pltpu.VMEM((TILE_W, TILE_W), F32)],
        name="borders",
    )(owner, counts, vert, hori, line, above)
    near, far, next_above, prev_above = lax.optimization_barrier((near, far, next_above, prev_above))
    mine, next_line, next_columns, prev_line, prev_columns = pl.pallas_call(
        match_kernel,
        out_shape=(
            jax.ShapeDtypeStruct((chips_z, halves, TILE_W), F32), border, upright, border, upright,
        ),
        in_specs=[local] * 6 + [anywhere] * 2,
        out_specs=(local,) * 5,
        scratch_shapes=[
            pltpu.VMEM(packed.shape, packed.dtype),
            pltpu.VMEM(packed.shape, packed.dtype),
            pltpu.VMEM((2, flow, length // 2), F32),
            pltpu.SemaphoreType.DMA((2 * PARTS + 2,)),
        ],
        compiler_params=pltpu.CompilerParams(vmem_limit_bytes=32 << 20),
        name="match",
    )(fixed_desc, moving_desc, offsets, table, line, hori, near, far)

    seen = lax.all_to_all(mine, "z", 0, 0, tiled=True).reshape(-1, TILE_W)
    seen = gather(seen, ("group", "y")).reshape(-1, TILE_W)
    seen = lax.all_gather(seen, "core", axis=0, tiled=True)

    dims = (groups, sections, rows, tiles, chips_z)
    count = groups * tiles

    def both_iterations(*refs):
        stack_kernel(dims, *refs)

    field = jax.ShapeDtypeStruct((2, rows, cols), F32)
    displacement, residual = pl.pallas_call(
        both_iterations,
        out_shape=(field, field),
        in_specs=[local] * 11,
        scratch_shapes=[
            pltpu.VMEM((groups * halves, sections, TILE_W), F32),
            pltpu.VMEM((groups, halves * TILE_W, sections), F32),
            pltpu.VMEM((3, count, sections), F32),
            pltpu.VMEM((24, count + 2 * tiles, sections), F32),
            pltpu.VMEM((2, rows + 2 * tiles, cols), F32),
        ],
        compiler_params=pltpu.CompilerParams(vmem_limit_bytes=32 << 20),
        name="stack",
    )(
        seen, vert, hori, line, above,
        next_line, next_above, next_columns, prev_line, prev_above, prev_columns,
    )
    return (displacement[None], residual[None])


def solution(mesh):
    groups, sections = mesh.devices.shape
    devices = mesh.devices.reshape(groups, sections // (CHIPS_Y * CORES), CHIPS_Y, CORES)
    fine = Mesh(devices, ("group",) + SEC)
    in_specs = (
        P(SEC, "group", None, None),
        P(SEC, "group", None, None),
        P(SEC, "group", None, None),
        P(SEC, "group"),
        P(SEC, "group"),
        P(SEC, "group", None),
        P(SEC, "group", None),
    )
    out_specs = (P(SEC, None, "group", None), P(SEC, None, "group", None))
    return jax.shard_map(body, mesh=fine, in_specs=in_specs, out_specs=out_specs, check_vma=False)
```

```python
import math

import jax
import jax.numpy as jnp
from jax import lax
from jax.experimental import pallas as pl
from jax.experimental.pallas import tpu as pltpu
from jax.sharding import Mesh, PartitionSpec as P

TILE_W = 128
SPREAD_SQ = 4.0
CHIPS_Y = 4
CORES = 2
SEC = ("z", "y", "core")
F32 = jnp.float32

COLUMN_KV, COLUMN_K2V, COLUMN_KXV, COLUMN_VL, COLUMN_VR, COLUMN_HT, COLUMN_HB = range(7)
COLUMN_DV, COLUMN_XBR, COLUMN_XBL, COLUMN_XTR, COLUMN_XTL = range(7, 12)
COLUMN_KH, COLUMN_K2H, COLUMN_KXH, COLUMN_DH, COLUMN_DT = range(12, 17)
COLUMN_OWNER = 17
COLUMN_NEAR = 19
COLUMN_FAR = 21
GROUP_LANES = 32
PARTS = 4


def iota(shape, axis):
    return lax.broadcasted_iota(jnp.int32, shape, axis)


def lane_sum(x):
    return jnp.sum(x, axis=1, keepdims=True)


def row_sum(x):
    return jnp.sum(x, axis=0, keepdims=True)


def total(x):
    return lane_sum(row_sum(x))


def three_parts(x):
    high = x.astype(jnp.bfloat16).astype(F32)
    middle = (x - high).astype(jnp.bfloat16).astype(F32)
    return high, middle, x - high - middle


def pack_kernel(
    moving_ref, fixed_ref, vert_ref, hori_ref, offsets_ref, near, far, line_ref,
    vert, hori, offsets, sems,
):
    rows, cols = hori.shape
    tiles = cols // TILE_W
    length = moving_ref.shape[0] // 2
    part = length // PARTS
    tail = slice(length, length + rows)
    loads = [
        pltpu.make_async_copy(vert_ref.at[0], vert, sems.at[0]),
        pltpu.make_async_copy(hori_ref.at[0], hori, sems.at[1]),
        pltpu.make_async_copy(offsets_ref.at[0], offsets, sems.at[2]),
    ]
    arrive = []
    for n in range(PARTS):
        at = pl.ds(n * part, part)
        behind = pl.ds(length + n * part, part)
        arrive.append(pltpu.make_async_copy(moving_ref.at[at], near.at[at], sems.at[3 + 2 * n]))
        arrive.append(pltpu.make_async_copy(fixed_ref.at[behind], far.at[at], sems.at[4 + 2 * n]))
    for copy in loads + arrive:
        copy.start()
    for copy in loads:
        copy.wait()
    lane = iota((rows, TILE_W), 1)
    column = jnp.zeros((rows, TILE_W), F32)
    for j in range(tiles):
        span = slice(j * TILE_W, (j + 1) * TILE_W)
        line_ref[j : j + 1, :] = vert[rows - 1 : rows, span]
        end = (j + 1) * TILE_W - 1
        column = jnp.where(lane == j, hori[:, end : end + 1], column)
    high, middle, small = three_parts(column)
    columns = high + pltpu.roll(middle, tiles, 1) + pltpu.roll(small, 2 * tiles, 1)
    half = offsets.shape[0] // 2
    shifts = jnp.concatenate([offsets[half:, 0, :], offsets[half:, 1, :]], 1).astype(F32)
    blank = jnp.zeros((tiles, TILE_W), F32)
    for n, value in enumerate(three_parts(line_ref[...])):
        span = slice(n * TILE_W, (n + 1) * TILE_W)
        near[tail, span] = jnp.concatenate([value, blank], 0).astype(jnp.bfloat16)
        far[tail, span] = jnp.concatenate([value, blank if n else shifts], 0).astype(jnp.bfloat16)
    for block in (near, far):
        block[tail, 3 * TILE_W :] = columns.astype(jnp.bfloat16)
    for copy in arrive:
        copy.wait()


def unpack(extra, tiles):
    parts = [extra[:, n * TILE_W : (n + 1) * TILE_W].astype(F32) for n in range(4)]
    line = parts[0][:tiles] + (parts[1][:tiles] + parts[2][:tiles])
    columns = parts[3]
    back = TILE_W - tiles
    columns = columns + (pltpu.roll(columns, back, 1) + pltpu.roll(columns, back - tiles, 1))
    return line, columns, parts[0][tiles:]


def border_kernel(groups, owner_ref, counts_ref, vert_ref, hori_ref, line_ref, above_ref, out_ref, stack):
    rows, cols = hori_ref.shape
    tiles = cols // TILE_W
    last_group = lax.axis_index("group") == groups - 1
    bottom = jnp.where(last_group, 1.0, 4.0).astype(F32)

    v_last = line_ref[...]
    v_above = above_ref[...]
    for j in range(tiles):
        span = slice(j * TILE_W, (j + 1) * TILE_W)
        stack[j : j + 1, :] = vert_ref[rows - 2 : rows - 1, span]
        stack[tiles + j : tiles + j + 1, :] = vert_ref[0:1, span]
        stack[2 * tiles + j : 2 * tiles + j + 1, :] = hori_ref[rows - 1 : rows, span]
        stack[3 * tiles + j : 3 * tiles + j + 1, :] = hori_ref[0:1, span]
    v_second, v_first = stack[0:tiles, :], stack[tiles : 2 * tiles, :]
    h_last, h_first = stack[2 * tiles : 3 * tiles, :], stack[3 * tiles : 4 * tiles, :]
    lane = iota((tiles, TILE_W), 1)
    inside = lane < TILE_W - 1
    square = v_last * v_last
    step_last = v_last - pltpu.roll(v_last, TILE_W - 1, 1)
    step_above = v_above - pltpu.roll(v_above, TILE_W - 1, 1)
    dh = lane_sum(
        bottom * square * v_last
        + v_second * square
        + jnp.where(inside, h_last * step_last * step_last, 0.0)
    )
    dt = lane_sum(
        v_first * v_above * v_above + jnp.where(inside, h_first * step_above * step_above, 0.0)
    )
    sub = iota((tiles, TILE_W), 0)
    table = jnp.zeros((tiles, TILE_W), F32)
    for p in range(owner_ref.shape[1]):
        live = jnp.where(p < counts_ref[0, 0], owner_ref[0, p], -1).astype(F32)
        spot = (sub == p % tiles) & (lane == COLUMN_OWNER + p // tiles)
        table = jnp.where(spot, live, table)
    for column, value in (
        (COLUMN_KH, lane_sum(v_last)),
        (COLUMN_K2H, lane_sum(square)),
        (COLUMN_DH, dh),
        (COLUMN_DT, dt),
    ):
        table = jnp.where(lane == column, value, table)

    tall = iota((rows, TILE_W), 1)
    zero = jnp.zeros((rows, TILE_W), F32)
    picked = {}
    for name, ref, column in (
        ("h127", hori_ref, TILE_W - 1),
        ("h0", hori_ref, 0),
        ("h126", hori_ref, TILE_W - 2),
        ("v0", vert_ref, 0),
        ("v1", vert_ref, 1),
        ("v126", vert_ref, TILE_W - 2),
        ("v127", vert_ref, TILE_W - 1),
    ):
        value = zero
        for j in range(tiles):
            at = j * TILE_W + column
            value = jnp.where(tall == j, ref[:, at : at + 1], value)
        picked[name] = value
    wide = iota((tiles, TILE_W), 0)
    diagonal = iota((tiles, TILE_W), 1) == wide

    def above_at(column):
        return row_sum(jnp.where(diagonal, v_above[:, column : column + 1], 0.0))

    a0, a1 = above_at(0), above_at(1)
    a126, a127 = above_at(TILE_W - 2), above_at(TILE_W - 1)
    right = picked["h127"]
    left = pltpu.roll(right, 1, 1)
    row = iota((rows, TILE_W), 0)
    within = row < rows - 1
    inner_tile = iota((1, TILE_W), 1) < tiles - 1
    step_right = right - pltpu.roll(right, rows - 1, 0)
    step_left = left - pltpu.roll(left, rows - 1, 0)
    right_sq, left_sq = right * right, left * left
    side_right = row_sum(
        picked["h126"] * right_sq + jnp.where(within, picked["v127"] * step_right * step_right, 0.0)
    )
    side_left = row_sum(
        picked["h0"] * left_sq + jnp.where(within, picked["v0"] * step_left * step_left, 0.0)
    )
    cube = row_sum(right_sq * right)
    dv = side_right + jnp.where(
        inner_tile, pltpu.roll(side_left, TILE_W - 1, 1) + 4.0 * cube, cube
    )
    end, pre = rows - 1, rows - 2
    v0, v1, v126, v127 = (picked[n] for n in ("v0", "v1", "v126", "v127"))
    h0, h126 = picked["h0"], picked["h126"]

    def at(x, r):
        return x[r : r + 1, :]

    xbr = at(h126, end) * (at(v127, end) - at(v126, end)) * at(right, end) + at(v127, pre) * at(
        v127, end
    ) * (at(right, end) - at(right, pre))
    xbl = -(
        at(h0, end) * (at(v0, end) - at(v1, end)) * at(left, end)
        + at(v0, pre) * at(v0, end) * (at(left, end) - at(left, pre))
    )
    xtr = -(
        at(h126, 0) * (a127 - a126) * at(right, 0)
        + at(v127, 0) * a127 * (at(right, 0) - at(right, 1))
    )
    xtl = at(h0, 0) * (a0 - a1) * at(left, 0) + at(v0, 0) * a0 * (at(left, 0) - at(left, 1))
    stack[...] = jnp.zeros_like(stack)
    for column, value in (
        (COLUMN_KV, row_sum(right)),
        (COLUMN_K2V, row_sum(right_sq)),
        (COLUMN_VL, at(v0, end)),
        (COLUMN_VR, at(v127, end)),
        (COLUMN_HT, at(right, 0)),
        (COLUMN_HB, at(right, end)),
        (COLUMN_DV, dv),
        (COLUMN_XBR, xbr),
        (COLUMN_XBL, xbl),
        (COLUMN_XTR, xtr),
        (COLUMN_XTL, xtl),
    ):
        stack[column : column + 1, :] = value
    turned = jnp.transpose(stack[...])[0:tiles, :]
    out_ref[...] = jnp.where(lane <= COLUMN_XTL, turned, table)


def match_kernel(
    fixed_ref, moving_ref, offsets_ref, table_ref, line_ref, hori_ref, near_ref, far_ref,
    out_ref, next_line_ref, next_columns_ref, prev_line_ref, prev_columns_ref,
    scores_ref,
):
    patches, flow, corr = fixed_ref.shape[1:]
    half = patches // 2
    length = half * flow
    rows, cols = hori_ref.shape[-2:]
    tiles = cols // TILE_W
    pair = 2 * flow
    lower = iota((flow, pair), 1) < flow
    for side in range(2):
        for first in range(0, half, 2):
            at = slice(first * flow, (first + 2) * flow)
            if side == 0:
                fixed = fixed_ref[0, first : first + 2].reshape(pair, corr)
                moving = near_ref[at, :]
            else:
                fixed = far_ref[at, :]
                moving = moving_ref[0, half + first : half + first + 2].reshape(pair, corr)
            scores = lax.dot_general(
                moving, fixed, (((1,), (1,)), ((), ())), preferred_element_type=F32
            )
            scores_ref[side, :, at] = jnp.where(lower, scores[0:flow, :], scores[flow:pair, :])
    next_line, next_columns, _ = unpack(near_ref[length : length + rows, :], tiles)
    prev_line, prev_columns, shifts = unpack(far_ref[length : length + rows, :], tiles)
    next_line_ref[...] = next_line
    next_columns_ref[...] = next_columns
    prev_line_ref[...] = prev_line
    prev_columns_ref[...] = prev_columns

    table = table_ref[...]
    lane = iota(table.shape, 1)
    own_shifts = [offsets_ref[0, 0:half, k, :].astype(F32) for k in range(2)]
    far_shifts = [shifts[:, 0:flow], shifts[:, flow:pair]]
    scale = 1.0 / math.sqrt(corr)
    slot = lax.rem(iota((2 * half, length), 0), half)
    mine = slot == lax.div(iota((2 * half, length), 1), flow)
    for side, offsets in enumerate((own_shifts, far_shifts)):
        both = scores_ref[side]
        top = jnp.max(both, axis=0, keepdims=True)
        likely = jnp.exp((both - top) * scale)
        sums = lax.dot_general(
            jnp.concatenate(offsets, 0),
            likely,
            (((1,), (0,)), ((), ())),
            precision=lax.Precision.HIGHEST,
            preferred_element_type=F32,
        )
        weight = row_sum(likely)
        ratio = lane_sum(jnp.where(mine, sums, 0.0) / (weight * flow))
        for k in range(2):
            column = (COLUMN_FAR if side else COLUMN_NEAR) + k
            table = jnp.where(lane == column, ratio[k * half : (k + 1) * half], table)

    table = jnp.where(lane == COLUMN_KXH, lane_sum(line_ref[...] * next_line), table)
    diagonal = iota(table.shape, 0) == lane
    columns = jnp.zeros((rows, TILE_W), F32)
    tall = iota((rows, TILE_W), 1)
    for j in range(tiles):
        end = (j + 1) * TILE_W - 1
        columns = jnp.where(tall == j, hori_ref[:, end : end + 1], columns)
    across = row_sum(columns * next_columns)
    table = jnp.where(lane == COLUMN_KXV, lane_sum(jnp.where(diagonal, across, 0.0)), table)

    table = jnp.where(lane < GROUP_LANES, table, 0.0)
    per_row = TILE_W // GROUP_LANES
    for part in range(tiles // per_row):
        line = jnp.zeros((1, TILE_W), F32)
        for j in range(per_row):
            source = table[part * per_row + j : part * per_row + j + 1, :]
            line = line + (pltpu.roll(source, j * GROUP_LANES, 1) if j else source)
        for n in range(out_ref.shape[0]):
            out_ref[n, part : part + 1, :] = line


def stack_kernel(
    dims, seen_ref, vert_ref, hori_ref, own_line_ref, own_above_ref,
    next_line_ref, next_above_ref, next_columns_ref, prev_line_ref, prev_above_ref, prev_columns_ref,
    disp_ref, res_ref, rows_ref, turn_ref, sums_ref, out_ref, field_ref,
):
    groups, sections, rows, tiles, chips_z = dims
    per_chip = sections // chips_z
    halves = tiles * GROUP_LANES // TILE_W
    count = groups * tiles
    nodes = float(rows * TILE_W)
    me, group = lax.axis_index(SEC), lax.axis_index("group")

    for core in range(CORES):
        for g in range(groups):
            for y in range(per_chip // CORES):
                base = ((core * groups + g) * (per_chip // CORES) + y) * chips_z * halves
                for h in range(halves):
                    rows_ref[g * halves + h, pl.ds(y * CORES + core, chips_z, stride=per_chip), :] = seen_ref[
                        pl.ds(base + h, chips_z, stride=halves), :
                    ]
    for g in range(groups):
        for h in range(halves):
            turn_ref[g, h * TILE_W : (h + 1) * TILE_W, :] = jnp.transpose(rows_ref[g * halves + h])

    def block(g, column):
        return turn_ref[g, pl.ds(column, tiles, stride=GROUP_LANES), :]

    def figure(column):
        return jnp.concatenate([block(g, column) for g in range(groups)], 0)

    def slots(near, far, turn):
        parts = []
        for g in range(groups):
            parts.append(block(g, near))
            other = block(g, far)
            parts.append(pltpu.roll(other, sections - 1, 1) if turn else other)
        return jnp.concatenate(parts, 0)

    lane = iota((count, sections), 1)
    tile_row = iota((count, sections), 0)
    along = lax.rem(tile_row, tiles)
    not_last = lane < sections - 1

    def up(x):
        return jnp.where(not_last, pltpu.roll(x, sections - 1, 1), 0.0)

    def low(x):
        return jnp.where(lane > 0, pltpu.roll(x, 1, 1), 0.0)

    zero_tiles = jnp.zeros((tiles, sections), F32)

    def from_above(x):
        return jnp.concatenate([zero_tiles, x[: count - tiles]], 0)

    def from_below(x):
        return jnp.concatenate([x[tiles:], zero_tiles], 0)

    def from_left(x):
        return jnp.where(along > 0, pltpu.roll(x, 1, 0), 0.0)

    def from_right(x):
        return jnp.where(along < tiles - 1, pltpu.roll(x, count - 1, 0), 0.0)

    owner = slots(COLUMN_OWNER, COLUMN_OWNER + 1, False)
    targets = [slots(COLUMN_NEAR + k, COLUMN_FAR + k, True) for k in range(2)]
    valid = jnp.where(owner >= 0.0, 1.0, 0.0)

    def tile_sums(miss):
        weight = valid / (1.0 + (miss[0] * miss[0] + miss[1] * miss[1]) / SPREAD_SQ)
        terms = (weight, weight * targets[0], weight * targets[1])
        for t in range(count):
            mine = owner == float(t)
            for n, term in enumerate(terms):
                sums_ref[n, t : t + 1, :] = row_sum(jnp.where(mine, term, 0.0))
        return [jnp.where(not_last, sums_ref[n], 0.0) for n in range(3)]

    kh, kv = figure(COLUMN_KH), figure(COLUMN_KV)
    k2h, k2v = figure(COLUMN_K2H), figure(COLUMN_K2V)
    kxh, kxv = figure(COLUMN_KXH), figure(COLUMN_KXV)
    vl, vr = figure(COLUMN_VL), figure(COLUMN_VR)
    ht, hb = figure(COLUMN_HT), figure(COLUMN_HB)
    dh, dt, dv = figure(COLUMN_DH), figure(COLUMN_DT), figure(COLUMN_DV)
    xbr, xbl, xtr, xtl = (figure(c) for c in (COLUMN_XBR, COLUMN_XBL, COLUMN_XTR, COLUMN_XTL))
    fold_h = jnp.where(tile_row < count - tiles, 2.0, 1.0)
    fold_v = jnp.where(along < tiles - 1, 2.0, 1.0)

    def differences(x):
        return x - from_below(x), x - from_right(x)

    def corners(diff_h, diff_v):
        return (
            (vr * diff_h, hb * diff_v),
            (vl * diff_h, -from_left(hb * diff_v)),
            (-from_above(vr * diff_h), ht * diff_v),
            (-from_above(vl * diff_h), -from_left(ht * diff_v)),
        )

    def tile_product(along_h, along_v, first, second):
        value = along_h + from_above(along_h) + along_v + from_left(along_v)
        for (ah, av), (bh, bv) in zip(first, second):
            value = value + ah * bv + av * bh
        return value

    weight, *pull = tile_sums(targets)
    flat = [e - low(e) for e in pull]
    step = [differences(d) for d in flat]
    gap = [d - up(d) for d in flat]
    norm = total(flat[0] * flat[0] + flat[1] * flat[1]) * nodes
    energy = sum(kh * h * h + kv * v * v for h, v in step)
    energy = energy + nodes * weight * (gap[0] * gap[0] + gap[1] * gap[1])
    alpha = norm / total(energy)

    for k in range(2):
        sums_ref[k] = alpha * gap[k]
    look = [jnp.zeros_like(owner), jnp.zeros_like(owner)]
    for t in range(count):
        mine = owner == float(t)
        for k in range(2):
            look[k] = jnp.where(mine, sums_ref[k, t : t + 1, :], look[k])
    weight, *pull = tile_sums([look[k] - targets[k] for k in range(2)])
    weight_low = low(weight)
    const = [
        pull[k] - low(pull[k]) - alpha * (weight * gap[k] - weight_low * low(gap[k]))
        for k in range(2)
    ]
    plain = jnp.zeros_like(kh)
    mixed = jnp.zeros_like(kh)
    quad = jnp.zeros_like(kh)
    p_energy = jnp.zeros_like(kh)
    m_energy = jnp.zeros_like(kh)
    q_energy = jnp.zeros_like(kh)
    for k in range(2):
        c = const[k]
        ch, cv = differences(c)
        h, v = step[k]
        ends = corners(h, v)
        c_ends = corners(ch, cv)
        square = tile_product(k2h * h * h, k2v * v * v, ends, ends)
        across = tile_product(
            kxh * h * up(h), kxv * v * up(v), ends, [(up(a), up(b)) for a, b in ends]
        )
        gap_square = square + up(square) - 2.0 * across
        flux_h, flux_v = kh * h, kv * v
        inner = flux_h - from_above(flux_h) + flux_v - from_left(flux_v)
        gap_c = c - up(c)
        gap_q = inner - up(inner)
        plain = plain + c * c
        mixed = mixed + c * inner
        quad = quad + square
        p_energy = p_energy + kh * ch * ch + kv * cv * cv + nodes * weight * gap_c * gap_c
        m_energy = (
            m_energy
            + tile_product(k2h * ch * h, k2v * cv * v, c_ends, ends)
            + weight * gap_c * gap_q
        )
        above_h, left_v = from_above(h), from_left(v)
        value = dh * h * h + dt * above_h * above_h + dv * v * v
        value = value + 2.0 * (
            xbr * h * v + xbl * h * left_v + xtr * above_h * v + xtl * above_h * left_v
        )
        (br_h, br_v), (bl_h, bl_v), (tr_h, tr_v), (tl_h, tl_v) = ends
        for stiff, part, extra, fold in (
            (vr, br_h, br_v - from_below(tr_v), fold_h),
            (vl, bl_h, bl_v - from_below(tl_v), fold_h),
            (hb, br_v, br_h - from_right(bl_h), fold_v),
            (ht, tr_v, tr_h - from_right(tl_h), fold_v),
        ):
            value = value + stiff * extra * (2.0 * fold * part + extra)
        q_energy = q_energy + value + weight * gap_square
    norm = nodes * total(plain) - 2.0 * alpha * total(mixed) + alpha * alpha * total(quad)
    energy = total(p_energy) - 2.0 * alpha * total(m_energy) + alpha * alpha * total(q_energy)
    beta = norm / energy

    own_figures = (*flat, *const, step[0][0], step[1][0], step[0][1], step[1][1], ht, hb, weight, weight_low)
    beside = (*const, step[0][0], step[1][0], step[0][1], step[1][1])
    wanted = [(x, me) for x in own_figures] + [(x, me + 1) for x in beside] + [(x, me - 1) for x in beside]
    for n, (x, section) in enumerate(wanted):
        out_ref[n, 0:tiles, :] = zero_tiles
        out_ref[n, tiles + count : 2 * tiles + count, :] = zero_tiles
        picked = lane_sum(jnp.where(lane == section, x, 0.0))
        out_ref[n, tiles : tiles + count, :] = jnp.broadcast_to(picked, (count, sections))

    def spread(n, shift):
        start = pl.multiple_of((group + 1 + shift) * tiles, tiles)
        return out_ref[n, pl.ds(start, tiles), :]

    wide_lane = iota((rows, TILE_W), 1)
    wide_row = iota((rows, TILE_W), 0)
    first_lane, last_lane = wide_lane == 0, wide_lane == TILE_W - 1
    first_row, last_row = wide_row == 0, wide_row == rows - 1
    line_first, line_last = first_lane[0:1], last_lane[0:1]
    inside = jnp.where(group < groups - 1, 1.0, 0.0).astype(F32)

    def image(edges, offset, k, j):
        last_line, above_line, columns = edges
        def line(n, shift=0, at=j):
            return spread(offset + n + k, shift)[at : at + 1, :]

        value = jnp.where(last_row, last_line[j : j + 1, :] * line(0), 0.0)
        value = value - jnp.where(first_row, above_line[j : j + 1, :] * line(0, -1), 0.0)
        value = value + jnp.where(last_lane, columns(j) * line(2), 0.0)
        if j:
            value = value - jnp.where(first_lane, columns(j - 1) * line(2, 0, j - 1), 0.0)
        return value

    own_line, own_above = own_line_ref[...], own_above_ref[...]
    next_columns, prev_columns = next_columns_ref[...], prev_columns_ref[...]
    own_edges = (own_line, own_above, lambda j: hori_ref[:, (j + 1) * TILE_W - 1 : (j + 1) * TILE_W])
    next_edges = (next_line_ref[...], next_above_ref[...], lambda j: next_columns[:, j : j + 1])
    prev_edges = (prev_line_ref[...], prev_above_ref[...], lambda j: prev_columns[:, j : j + 1])
    for k in range(2):
        for j in range(tiles):
            span = slice(j * TILE_W, (j + 1) * TILE_W)

            def line(n, shift, at=j):
                return spread(n + k, shift)[at : at + 1, :]

            field_ref[k, tiles : tiles + rows, span] = line(2, 0) - alpha * image(own_edges, 4, k, j)
            near = -inside * own_line[j : j + 1, :] * line(4, 0)
            near = near + jnp.where(line_last, spread(8, 1)[j : j + 1, :] * line(6, 1), 0.0)
            far = own_above[j : j + 1, :] * line(4, -1)
            far = far + jnp.where(line_last, spread(9, -1)[j : j + 1, :] * line(6, -1), 0.0)
            if j:
                near = near - jnp.where(line_first, spread(8, 1)[j - 1 : j, :] * line(6, 1, j - 1), 0.0)
                far = far - jnp.where(line_first, spread(9, -1)[j - 1 : j, :] * line(6, -1, j - 1), 0.0)
            field_ref[k, tiles + rows : tiles + rows + 1, span] = line(2, 1) - alpha * near
            field_ref[k, tiles - 1 : tiles, span] = line(2, -1) - alpha * far
    weight_rows, weight_low_rows = spread(10, 0), spread(11, 0)
    for k in range(2):
        flux_left = None
        for j in range(tiles):
            span = slice(j * TILE_W, (j + 1) * TILE_W)
            r = field_ref[k, tiles : tiles + rows, span]
            right = pltpu.roll(r, TILE_W - 1, 1)
            if j < tiles - 1:
                beyond = field_ref[k, tiles : tiles + rows, (j + 1) * TILE_W : (j + 2) * TILE_W]
                right = jnp.where(last_lane, pltpu.roll(beyond, TILE_W - 1, 1), right)
            else:
                right = jnp.where(last_lane, 0.0, right)
            flux = hori_ref[:, span] * (r - right)
            turned = pltpu.roll(flux, 1, 1)
            before = jnp.where(first_lane, 0.0 if flux_left is None else flux_left, turned)
            flux_left = turned
            below = field_ref[k, tiles + 1 : tiles + rows + 1, span]
            fall = vert_ref[:, span] * (r - below)
            edge = own_above[j : j + 1, :] * (field_ref[k, tiles - 1 : tiles, span] - r[0:1, :])
            fall_above = jnp.where(first_row, edge, pltpu.roll(fall, 1, 0))
            applied = flux - before + fall - fall_above
            r_next = spread(12 + k, 0)[j : j + 1, :] - alpha * image(next_edges, 14, k, j)
            r_prev = spread(18 + k, 0)[j : j + 1, :] - alpha * image(prev_edges, 20, k, j)
            applied = applied + weight_rows[j : j + 1, :] * (r - r_next) + weight_low_rows[j : j + 1, :] * (r - r_prev)
            disp_ref[k, :, span] = alpha * spread(k, 0)[j : j + 1, :] + beta * r
            res_ref[k, :, span] = r - beta * applied


def in_vmem(x):
    return pltpu.VMEM(x.shape, x.dtype)


def from_behind(block, axis, distance):
    devices = range(lax.axis_size(axis))
    route = [(i - distance, i) for i in devices if i - distance in devices]
    return lax.ppermute(block, axis, route)


def from_above(block, distance):
    groups, sections = lax.axis_size("group"), lax.axis_size(SEC)
    route = [
        ((g - 1) * sections + s - distance, g * sections + s)
        for g in range(1, groups)
        for s in range(sections)
        if 0 <= s - distance < sections
    ]
    return lax.ppermute(block, ("group",) + SEC, route)


def gather(block, axis):
    size = lax.axis_size(axis)
    copies = jnp.broadcast_to(block[None], (size,) + block.shape)
    return lax.all_to_all(copies, axis, 0, 0, tiled=True)


def body(fixed_desc, moving_desc, offsets, owner, counts, vert, hori):
    groups = lax.axis_size("group")
    sections = lax.axis_size(SEC)
    chips_z = lax.axis_size("z")
    patches, flow, corr = fixed_desc.shape[1:]
    rows, cols = vert.shape[1:]
    tiles = cols // TILE_W
    length = patches * flow
    halves = tiles * GROUP_LANES // TILE_W

    hbm = pl.BlockSpec(memory_space=pltpu.HBM)
    local = pl.BlockSpec(memory_space=pltpu.VMEM)
    scalars = pl.BlockSpec(memory_space=pltpu.SMEM)
    modest = pltpu.CompilerParams(vmem_limit_bytes=16 << 20)
    packed = jax.ShapeDtypeStruct((length // 2 + rows, corr), fixed_desc.dtype)
    border = jax.ShapeDtypeStruct((tiles, TILE_W), F32)
    upright = jax.ShapeDtypeStruct((rows, TILE_W), F32)
    near, far, line = pl.pallas_call(
        pack_kernel,
        out_shape=(in_vmem(packed), in_vmem(packed), in_vmem(border)),
        in_specs=[hbm] * 5,
        out_specs=(local,) * 3,
        scratch_shapes=[
            pltpu.VMEM((rows, cols), F32),
            pltpu.VMEM((rows, cols), F32),
            pltpu.VMEM(offsets.shape[1:], jnp.int32),
            pltpu.SemaphoreType.DMA((2 * PARTS + 3,)),
        ],
        compiler_params=modest,
        name="pack",
    )(
        *(
            pltpu.with_memory_space_constraint(x, pltpu.HBM)
            for x in (moving_desc.reshape(length, corr), fixed_desc.reshape(length, corr), vert, hori, offsets)
        )
    )
    near = from_behind(near, SEC, -1)
    far = from_behind(far, SEC, 1)
    above = from_above(line, 0)
    next_above = from_above(line, -1)
    prev_above = from_above(line, 1)

    vert, hori = vert[0], hori[0]

    def borders(*refs):
        border_kernel(groups, *refs)

    table = pl.pallas_call(
        borders,
        out_shape=border,
        in_specs=[scalars] * 2 + [local] * 4,
        scratch_shapes=[pltpu.VMEM((TILE_W, TILE_W), F32)],
        compiler_params=modest,
        name="borders",
    )(owner, counts, vert, hori, line, above)
    near, far, next_above, prev_above = lax.optimization_barrier((near, far, next_above, prev_above))
    mine, next_line, next_columns, prev_line, prev_columns = pl.pallas_call(
        match_kernel,
        out_shape=(
            jax.ShapeDtypeStruct((chips_z, halves, TILE_W), F32), border, upright, border, upright,
        ),
        in_specs=[local] * 8,
        out_specs=(local,) * 5,
        scratch_shapes=[pltpu.VMEM((2, flow, length // 2), F32)],
        compiler_params=modest,
        name="match",
    )(fixed_desc, moving_desc, offsets, table, line, hori, near, far)

    seen = lax.all_to_all(mine, "z", 0, 0, tiled=True).reshape(-1, TILE_W)
    seen = gather(seen, ("group", "y")).reshape(-1, TILE_W)
    seen = lax.all_gather(seen, "core", axis=0, tiled=True)

    dims = (groups, sections, rows, tiles, chips_z)
    count = groups * tiles

    def both_iterations(*refs):
        stack_kernel(dims, *refs)

    field = jax.ShapeDtypeStruct((2, rows, cols), F32)
    displacement, residual = pl.pallas_call(
        both_iterations,
        out_shape=(field, field),
        in_specs=[local] * 11,
        scratch_shapes=[
            pltpu.VMEM((groups * halves, sections, TILE_W), F32),
            pltpu.VMEM((groups, halves * TILE_W, sections), F32),
            pltpu.VMEM((3, count, sections), F32),
            pltpu.VMEM((24, count + 2 * tiles, sections), F32),
            pltpu.VMEM((2, rows + 2 * tiles, cols), F32),
        ],
        compiler_params=modest,
        name="stack",
    )(
        seen, vert, hori, line, above,
        next_line, next_above, next_columns, prev_line, prev_above, prev_columns,
    )
    return (displacement[None], residual[None])


def solution(mesh):
    groups, sections = mesh.devices.shape
    devices = mesh.devices.reshape(groups, sections // (CHIPS_Y * CORES), CHIPS_Y, CORES)
    fine = Mesh(devices, ("group",) + SEC)
    in_specs = (
        P(SEC, "group", None, None),
        P(SEC, "group", None, None),
        P(SEC, "group", None, None),
        P(SEC, "group"),
        P(SEC, "group"),
        P(SEC, "group", None),
        P(SEC, "group", None),
    )
    out_specs = (P(SEC, None, "group", None), P(SEC, None, "group", None))
    return jax.shard_map(body, mesh=fine, in_specs=in_specs, out_specs=out_specs, check_vma=False)
```

```python
import math

import jax
import jax.numpy as jnp
from jax import lax
from jax.experimental import pallas as pl
from jax.experimental.pallas import tpu as pltpu
from jax.sharding import Mesh, PartitionSpec as P

TILE_W = 128
SPREAD_SQ = 4.0
CHIPS_Y = 4
CORES = 2
SEC = ("z", "y", "core")
F32 = jnp.float32

COLUMN_KV, COLUMN_K2V, COLUMN_KXV, COLUMN_VL, COLUMN_VR, COLUMN_HT, COLUMN_HB = range(7)
COLUMN_DV, COLUMN_XBR, COLUMN_XBL, COLUMN_XTR, COLUMN_XTL = range(7, 12)
COLUMN_KH, COLUMN_K2H, COLUMN_KXH, COLUMN_DH, COLUMN_DT = range(12, 17)
COLUMN_OWNER = 17
COLUMN_NEAR = 19
COLUMN_FAR = 21
COLUMN_HELP = 23
GROUP_LANES = 32
PARTS = 2


def iota(shape, axis):
    return lax.broadcasted_iota(jnp.int32, shape, axis)


def lane_sum(x):
    return jnp.sum(x, axis=1, keepdims=True)


def row_sum(x):
    return jnp.sum(x, axis=0, keepdims=True)


def total(x):
    return lane_sum(row_sum(x))


def three_parts(x):
    high = x.astype(jnp.bfloat16).astype(F32)
    middle = (x - high).astype(jnp.bfloat16).astype(F32)
    return high, middle, x - high - middle


def pack_kernel(
    moving_ref, fixed_ref, vert_ref, hori_ref, offsets_ref, across_ref, beside_ref, line_ref,
    vert, hori, offsets, sems,
):
    rows, cols = hori.shape
    tiles = cols // TILE_W
    length = moving_ref.shape[0] // 2
    part = length // PARTS
    loads = [
        pltpu.make_async_copy(vert_ref.at[0], vert, sems.at[0]),
        pltpu.make_async_copy(hori_ref.at[0], hori, sems.at[1]),
        pltpu.make_async_copy(offsets_ref.at[0], offsets, sems.at[2]),
    ]
    for copy in loads:
        copy.start()

    def features(back, ahead):
        copies = []
        for n in range(PARTS):
            at, behind = pl.ds(n * part, part), pl.ds(length + n * part, part)
            copies.append(pltpu.make_async_copy(moving_ref.at[at], back.at[at], sems.at[3 + 2 * n]))
            copies.append(pltpu.make_async_copy(fixed_ref.at[behind], ahead.at[at], sems.at[4 + 2 * n]))
        return copies

    first = lax.axis_index("core") == 0

    @pl.when(first)
    def _():
        for copy in features(across_ref, beside_ref):
            copy.start()

    @pl.when(jnp.logical_not(first))
    def _():
        for copy in features(beside_ref, across_ref):
            copy.start()

    for copy in loads:
        copy.wait()
    lane = iota((rows, TILE_W), 1)
    column = jnp.zeros((rows, TILE_W), F32)
    for j in range(tiles):
        span = slice(j * TILE_W, (j + 1) * TILE_W)
        line_ref[j : j + 1, :] = vert[rows - 1 : rows, span]
        end = (j + 1) * TILE_W - 1
        column = jnp.where(lane == j, hori[:, end : end + 1], column)
    high, middle, small = three_parts(column)
    columns = high + pltpu.roll(middle, tiles, 1) + pltpu.roll(small, 2 * tiles, 1)
    half = offsets.shape[0] // 2
    shifts = jnp.concatenate([offsets[half:, 0, :], offsets[half:, 1, :]], 1).astype(F32)
    blank = jnp.zeros((tiles, TILE_W), F32)
    for ref in (across_ref, beside_ref):
        for n, value in enumerate(three_parts(line_ref[...])):
            block = jnp.concatenate([value, blank if n else shifts], 0)
            ref[length:, n * TILE_W : (n + 1) * TILE_W] = block.astype(jnp.bfloat16)
        ref[length:, 3 * TILE_W :] = columns.astype(jnp.bfloat16)
    for copy in features(across_ref, beside_ref):
        copy.wait()


def unpack(extra, tiles):
    parts = [extra[:, n * TILE_W : (n + 1) * TILE_W].astype(F32) for n in range(4)]
    line = parts[0][:tiles] + (parts[1][:tiles] + parts[2][:tiles])
    columns = parts[3]
    back = TILE_W - tiles
    columns = columns + (pltpu.roll(columns, back, 1) + pltpu.roll(columns, back - tiles, 1))
    return line, columns, parts[0][tiles:]


def border_kernel(groups, owner_ref, counts_ref, vert_ref, hori_ref, line_ref, out_ref, firsts_ref, right_ref, stack):
    rows, cols = hori_ref.shape
    tiles = cols // TILE_W
    last_group = lax.axis_index("group") == groups - 1
    bottom = jnp.where(last_group, 1.0, 4.0).astype(F32)

    v_last = line_ref[...]
    for j in range(tiles):
        span = slice(j * TILE_W, (j + 1) * TILE_W)
        stack[j : j + 1, :] = vert_ref[rows - 2 : rows - 1, span]
        stack[tiles + j : tiles + j + 1, :] = hori_ref[rows - 1 : rows, span]
        firsts_ref[j : j + 1, :] = vert_ref[0:1, span]
        firsts_ref[tiles + j : tiles + j + 1, :] = hori_ref[0:1, span]
    v_second, h_last = stack[0:tiles, :], stack[tiles : 2 * tiles, :]
    lane = iota((tiles, TILE_W), 1)
    inside = lane < TILE_W - 1
    square = v_last * v_last
    step_last = v_last - pltpu.roll(v_last, TILE_W - 1, 1)
    dh = lane_sum(
        bottom * square * v_last
        + v_second * square
        + jnp.where(inside, h_last * step_last * step_last, 0.0)
    )
    sub = iota((tiles, TILE_W), 0)
    table = jnp.zeros((tiles, TILE_W), F32)
    for p in range(owner_ref.shape[1]):
        live = jnp.where(p < counts_ref[0, 0], owner_ref[0, p], -1).astype(F32)
        spot = (sub == p % tiles) & (lane == COLUMN_OWNER + p // tiles)
        table = jnp.where(spot, live, table)
    for column, value in (
        (COLUMN_KH, lane_sum(v_last)),
        (COLUMN_K2H, lane_sum(square)),
        (COLUMN_DH, dh),
    ):
        table = jnp.where(lane == column, value, table)

    tall = iota((rows, TILE_W), 1)
    zero = jnp.zeros((rows, TILE_W), F32)
    picked = {}
    for name, ref, column in (
        ("h127", hori_ref, TILE_W - 1),
        ("h0", hori_ref, 0),
        ("h126", hori_ref, TILE_W - 2),
        ("v0", vert_ref, 0),
        ("v1", vert_ref, 1),
        ("v126", vert_ref, TILE_W - 2),
        ("v127", vert_ref, TILE_W - 1),
    ):
        value = zero
        for j in range(tiles):
            at = j * TILE_W + column
            value = jnp.where(tall == j, ref[:, at : at + 1], value)
        picked[name] = value
    right = picked["h127"]
    left = pltpu.roll(right, 1, 1)
    row = iota((rows, TILE_W), 0)
    within = row < rows - 1
    inner_tile = iota((1, TILE_W), 1) < tiles - 1
    step_right = right - pltpu.roll(right, rows - 1, 0)
    step_left = left - pltpu.roll(left, rows - 1, 0)
    right_sq, left_sq = right * right, left * left
    side_right = row_sum(
        picked["h126"] * right_sq + jnp.where(within, picked["v127"] * step_right * step_right, 0.0)
    )
    side_left = row_sum(
        picked["h0"] * left_sq + jnp.where(within, picked["v0"] * step_left * step_left, 0.0)
    )
    cube = row_sum(right_sq * right)
    dv = side_right + jnp.where(
        inner_tile, pltpu.roll(side_left, TILE_W - 1, 1) + 4.0 * cube, cube
    )
    end, pre = rows - 1, rows - 2
    v0, v1, v126, v127 = (picked[n] for n in ("v0", "v1", "v126", "v127"))
    h0, h126 = picked["h0"], picked["h126"]

    def at(x, r):
        return x[r : r + 1, :]

    xbr = at(h126, end) * (at(v127, end) - at(v126, end)) * at(right, end) + at(v127, pre) * at(
        v127, end
    ) * (at(right, end) - at(right, pre))
    xbl = -(
        at(h0, end) * (at(v0, end) - at(v1, end)) * at(left, end)
        + at(v0, pre) * at(v0, end) * (at(left, end) - at(left, pre))
    )
    along_last, along_first = at(h126, 0) * at(right, 0), at(h0, 0) * at(left, 0)
    fall_last = at(v127, 0) * (at(right, 0) - at(right, 1))
    fall_first = at(v0, 0) * (at(left, 0) - at(left, 1))
    right_ref[...] = right
    stack[...] = jnp.zeros_like(stack)
    for column, value in (
        (COLUMN_KV, row_sum(right)),
        (COLUMN_K2V, row_sum(right_sq)),
        (COLUMN_VL, at(v0, end)),
        (COLUMN_VR, at(v127, end)),
        (COLUMN_HT, at(right, 0)),
        (COLUMN_HB, at(right, end)),
        (COLUMN_DV, dv),
        (COLUMN_XBR, xbr),
        (COLUMN_XBL, xbl),
        (COLUMN_HELP, -along_last - fall_last),
        (COLUMN_HELP + 1, along_last),
        (COLUMN_HELP + 2, along_first + fall_first),
        (COLUMN_HELP + 3, -along_first),
    ):
        stack[column : column + 1, :] = value
    turned = jnp.transpose(stack[...])[0:tiles, :]
    upright = (lane <= COLUMN_XTL) | (lane >= COLUMN_HELP)
    out_ref[...] = jnp.where(upright, turned, table)


def match_kernel(
    fixed_ref, moving_ref, offsets_ref, table_ref, firsts_ref, right_ref, line_ref, above_ref, across_ref, beside_ref,
    out_ref, lines_ref, next_columns_ref, prev_columns_ref, scores_ref, shifts_ref,
):
    patches, flow, corr = fixed_ref.shape[1:]
    half = patches // 2
    rows = right_ref.shape[0]
    tiles = line_ref.shape[0]
    pair = 2 * flow
    lower = iota((flow, pair), 1) < flow

    def receive(near_ref, far_ref):
        for first in range(0, patches, 2):
            own = slice(first, first + 2)
            if first < half:
                fixed = fixed_ref[0, own].reshape(pair, corr)
                moving = near_ref[first * flow : (first + 2) * flow, :]
            else:
                fixed = far_ref[(first - half) * flow : (first + 2 - half) * flow, :]
                moving = moving_ref[0, own].reshape(pair, corr)
            scores = lax.dot_general(moving, fixed, (((1,), (1,)), ((), ())), preferred_element_type=F32)
            scores_ref[:, first * flow : (first + 2) * flow] = jnp.where(
                lower, scores[0:flow, :], scores[flow:pair, :]
            )
        next_line, next_columns, _ = unpack(near_ref[half * flow :, :], tiles)
        prev_line, prev_columns, shifts = unpack(far_ref[half * flow :, :], tiles)
        lines_ref[0:tiles, :] = next_line
        lines_ref[tiles:, :] = prev_line
        next_columns_ref[...] = next_columns
        prev_columns_ref[...] = prev_columns
        shifts_ref[...] = shifts

    first_core = lax.axis_index("core") == 0

    @pl.when(first_core)
    def _():
        receive(beside_ref, across_ref)

    @pl.when(jnp.logical_not(first_core))
    def _():
        receive(across_ref, beside_ref)

    next_line, next_columns, shifts = lines_ref[0:tiles, :], next_columns_ref[...], shifts_ref[...]
    scores = scores_ref[...]
    top = jnp.max(scores, axis=0, keepdims=True)
    likely = jnp.exp((scores - top) * (1.0 / math.sqrt(corr)))
    offsets = []
    for k in range(2):
        offsets.append(offsets_ref[0, 0:half, k, :].astype(F32))
        offsets.append(shifts[:, k * flow : (k + 1) * flow])
    sums = lax.dot_general(
        jnp.concatenate(offsets, 0),
        likely,
        (((1,), (0,)), ((), ())),
        precision=lax.Precision.HIGHEST,
        preferred_element_type=F32,
    )
    weight = row_sum(likely) * flow
    mine = lax.rem(iota(sums.shape, 0), patches) == lax.div(iota(sums.shape, 1), flow)
    ratio = lane_sum(jnp.where(mine, sums, 0.0) / weight)

    table = table_ref[...]
    lane = iota(table.shape, 1)

    def helper(n):
        return table[:, COLUMN_HELP + n : COLUMN_HELP + n + 1]

    line, above = line_ref[...], above_ref[...]
    step = above - pltpu.roll(above, TILE_W - 1, 1)
    top_energy = firsts_ref[0:tiles, :] * above * above + jnp.where(
        lane < TILE_W - 1, firsts_ref[tiles:, :] * step * step, 0.0
    )
    diagonal = iota(table.shape, 0) == lane
    across = row_sum(right_ref[...] * next_columns)
    columns = [
        (COLUMN_XTR, above[:, TILE_W - 1 :] * helper(0) + above[:, TILE_W - 2 : TILE_W - 1] * helper(1)),
        (COLUMN_XTL, above[:, 0:1] * helper(2) + above[:, 1:2] * helper(3)),
        (COLUMN_DT, lane_sum(top_energy)),
        (COLUMN_KXH, lane_sum(line * next_line)),
        (COLUMN_KXV, lane_sum(jnp.where(diagonal, across, 0.0))),
    ]
    for k in range(2):
        columns.append((COLUMN_NEAR + k, ratio[2 * k * half : (2 * k + 1) * half]))
        columns.append((COLUMN_FAR + k, ratio[(2 * k + 1) * half : (2 * k + 2) * half]))
    for column, value in columns:
        table = jnp.where(lane == column, value, table)

    table = jnp.where(lane < COLUMN_HELP, table, 0.0)
    per_row = TILE_W // GROUP_LANES
    for part in range(tiles // per_row):
        packed = jnp.zeros((1, TILE_W), F32)
        for j in range(per_row):
            source = table[part * per_row + j : part * per_row + j + 1, :]
            packed = packed + (pltpu.roll(source, j * GROUP_LANES, 1) if j else source)
        for n in range(out_ref.shape[0]):
            out_ref[n, part : part + 1, :] = packed


def copies_kernel(seen_ref, out_ref):
    seen = seen_ref[...]
    for n in range(out_ref.shape[0]):
        out_ref[n] = seen


def stack_kernel(
    dims, seen_ref, vert_ref, hori_ref, own_line_ref, own_above_ref,
    lines_ref, aboves_ref, next_columns_ref, prev_columns_ref,
    disp_ref, res_ref, rows_ref, turn_ref, sums_ref, out_ref, field_ref,
):
    groups, sections, rows, tiles, chips_z = dims
    per_chip = sections // chips_z
    halves = tiles * GROUP_LANES // TILE_W
    count = groups * tiles
    nodes = float(rows * TILE_W)
    me, group = lax.axis_index(SEC), lax.axis_index("group")

    for core in range(CORES):
        for g in range(groups):
            for y in range(per_chip // CORES):
                base = ((core * groups + g) * (per_chip // CORES) + y) * chips_z * halves
                for h in range(halves):
                    rows_ref[g * halves + h, pl.ds(y * CORES + core, chips_z, stride=per_chip), :] = seen_ref[
                        pl.ds(base + h, chips_z, stride=halves), :
                    ]
    for g in range(groups):
        for h in range(halves):
            turn_ref[g, h * TILE_W : (h + 1) * TILE_W, :] = jnp.transpose(rows_ref[g * halves + h])

    def block(g, column):
        return turn_ref[g, pl.ds(column, tiles, stride=GROUP_LANES), :]

    def figure(column):
        return jnp.concatenate([block(g, column) for g in range(groups)], 0)

    def slots(near, far, turn):
        parts = []
        for g in range(groups):
            parts.append(block(g, near))
            other = block(g, far)
            parts.append(pltpu.roll(other, sections - 1, 1) if turn else other)
        return jnp.concatenate(parts, 0)

    lane = iota((count, sections), 1)
    tile_row = iota((count, sections), 0)
    along = lax.rem(tile_row, tiles)
    not_last = lane < sections - 1

    def up(x):
        return jnp.where(not_last, pltpu.roll(x, sections - 1, 1), 0.0)

    def low(x):
        return jnp.where(lane > 0, pltpu.roll(x, 1, 1), 0.0)

    zero_tiles = jnp.zeros((tiles, sections), F32)

    def from_above(x):
        return jnp.concatenate([zero_tiles, x[: count - tiles]], 0)

    def from_below(x):
        return jnp.concatenate([x[tiles:], zero_tiles], 0)

    def from_left(x):
        return jnp.where(along > 0, pltpu.roll(x, 1, 0), 0.0)

    def from_right(x):
        return jnp.where(along < tiles - 1, pltpu.roll(x, count - 1, 0), 0.0)

    owner = slots(COLUMN_OWNER, COLUMN_OWNER + 1, False)
    targets = [slots(COLUMN_NEAR + k, COLUMN_FAR + k, True) for k in range(2)]
    valid = jnp.where(owner >= 0.0, 1.0, 0.0)

    def tile_sums(miss):
        weight = valid / (1.0 + (miss[0] * miss[0] + miss[1] * miss[1]) / SPREAD_SQ)
        terms = (weight, weight * targets[0], weight * targets[1])
        for t in range(count):
            mine = owner == float(t)
            for n, term in enumerate(terms):
                sums_ref[n, t : t + 1, :] = row_sum(jnp.where(mine, term, 0.0))
        return [jnp.where(not_last, sums_ref[n], 0.0) for n in range(3)]

    kh, kv = figure(COLUMN_KH), figure(COLUMN_KV)
    k2h, k2v = figure(COLUMN_K2H), figure(COLUMN_K2V)
    kxh, kxv = figure(COLUMN_KXH), figure(COLUMN_KXV)
    vl, vr = figure(COLUMN_VL), figure(COLUMN_VR)
    ht, hb = figure(COLUMN_HT), figure(COLUMN_HB)
    dh, dt, dv = figure(COLUMN_DH), figure(COLUMN_DT), figure(COLUMN_DV)
    xbr, xbl, xtr, xtl = (figure(c) for c in (COLUMN_XBR, COLUMN_XBL, COLUMN_XTR, COLUMN_XTL))
    fold_h = jnp.where(tile_row < count - tiles, 2.0, 1.0)
    fold_v = jnp.where(along < tiles - 1, 2.0, 1.0)

    def differences(x):
        return x - from_below(x), x - from_right(x)

    def corners(diff_h, diff_v):
        return (
            (vr * diff_h, hb * diff_v),
            (vl * diff_h, -from_left(hb * diff_v)),
            (-from_above(vr * diff_h), ht * diff_v),
            (-from_above(vl * diff_h), -from_left(ht * diff_v)),
        )

    def tile_product(along_h, along_v, first, second):
        value = along_h + from_above(along_h) + along_v + from_left(along_v)
        for (ah, av), (bh, bv) in zip(first, second):
            value = value + ah * bv + av * bh
        return value

    weight, *pull = tile_sums(targets)
    flat = [e - low(e) for e in pull]
    step = [differences(d) for d in flat]
    gap = [d - up(d) for d in flat]
    norm = total(flat[0] * flat[0] + flat[1] * flat[1]) * nodes
    energy = sum(kh * h * h + kv * v * v for h, v in step)
    energy = energy + nodes * weight * (gap[0] * gap[0] + gap[1] * gap[1])
    alpha = norm / total(energy)

    for k in range(2):
        sums_ref[k] = alpha * gap[k]
    look = [jnp.zeros_like(owner), jnp.zeros_like(owner)]
    for t in range(count):
        mine = owner == float(t)
        for k in range(2):
            look[k] = jnp.where(mine, sums_ref[k, t : t + 1, :], look[k])
    weight, *pull = tile_sums([look[k] - targets[k] for k in range(2)])
    weight_low = low(weight)
    const = [
        pull[k] - low(pull[k]) - alpha * (weight * gap[k] - weight_low * low(gap[k]))
        for k in range(2)
    ]
    plain = jnp.zeros_like(kh)
    mixed = jnp.zeros_like(kh)
    quad = jnp.zeros_like(kh)
    p_energy = jnp.zeros_like(kh)
    m_energy = jnp.zeros_like(kh)
    q_energy = jnp.zeros_like(kh)
    for k in range(2):
        c = const[k]
        ch, cv = differences(c)
        h, v = step[k]
        ends = corners(h, v)
        c_ends = corners(ch, cv)
        square = tile_product(k2h * h * h, k2v * v * v, ends, ends)
        across = tile_product(
            kxh * h * up(h), kxv * v * up(v), ends, [(up(a), up(b)) for a, b in ends]
        )
        gap_square = square + up(square) - 2.0 * across
        flux_h, flux_v = kh * h, kv * v
        inner = flux_h - from_above(flux_h) + flux_v - from_left(flux_v)
        gap_c = c - up(c)
        gap_q = inner - up(inner)
        plain = plain + c * c
        mixed = mixed + c * inner
        quad = quad + square
        p_energy = p_energy + kh * ch * ch + kv * cv * cv + nodes * weight * gap_c * gap_c
        m_energy = (
            m_energy
            + tile_product(k2h * ch * h, k2v * cv * v, c_ends, ends)
            + weight * gap_c * gap_q
        )
        above_h, left_v = from_above(h), from_left(v)
        value = dh * h * h + dt * above_h * above_h + dv * v * v
        value = value + 2.0 * (
            xbr * h * v + xbl * h * left_v + xtr * above_h * v + xtl * above_h * left_v
        )
        (br_h, br_v), (bl_h, bl_v), (tr_h, tr_v), (tl_h, tl_v) = ends
        for stiff, part, extra, fold in (
            (vr, br_h, br_v - from_below(tr_v), fold_h),
            (vl, bl_h, bl_v - from_below(tl_v), fold_h),
            (hb, br_v, br_h - from_right(bl_h), fold_v),
            (ht, tr_v, tr_h - from_right(tl_h), fold_v),
        ):
            value = value + stiff * extra * (2.0 * fold * part + extra)
        q_energy = q_energy + value + weight * gap_square
    norm = nodes * total(plain) - 2.0 * alpha * total(mixed) + alpha * alpha * total(quad)
    energy = total(p_energy) - 2.0 * alpha * total(m_energy) + alpha * alpha * total(q_energy)
    beta = norm / energy

    own_figures = (*flat, *const, step[0][0], step[1][0], step[0][1], step[1][1], ht, hb, weight, weight_low)
    beside = (*const, step[0][0], step[1][0], step[0][1], step[1][1])
    wanted = [(x, me) for x in own_figures] + [(x, me + 1) for x in beside] + [(x, me - 1) for x in beside]
    for n, (x, section) in enumerate(wanted):
        out_ref[n, 0:tiles, :] = zero_tiles
        out_ref[n, tiles + count : 2 * tiles + count, :] = zero_tiles
        picked = lane_sum(jnp.where(lane == section, x, 0.0))
        out_ref[n, tiles : tiles + count, :] = jnp.broadcast_to(picked, (count, sections))

    def spread(n, shift):
        start = pl.multiple_of((group + 1 + shift) * tiles, tiles)
        return out_ref[n, pl.ds(start, tiles), :]

    wide_lane = iota((rows, TILE_W), 1)
    wide_row = iota((rows, TILE_W), 0)
    first_lane, last_lane = wide_lane == 0, wide_lane == TILE_W - 1
    first_row, last_row = wide_row == 0, wide_row == rows - 1
    line_first, line_last = first_lane[0:1], last_lane[0:1]
    inside = jnp.where(group < groups - 1, 1.0, 0.0).astype(F32)

    def image(edges, offset, k, j):
        last_line, above_line, columns = edges
        def line(n, shift=0, at=j):
            return spread(offset + n + k, shift)[at : at + 1, :]

        value = jnp.where(last_row, last_line[j : j + 1, :] * line(0), 0.0)
        value = value - jnp.where(first_row, above_line[j : j + 1, :] * line(0, -1), 0.0)
        value = value + jnp.where(last_lane, columns(j) * line(2), 0.0)
        if j:
            value = value - jnp.where(first_lane, columns(j - 1) * line(2, 0, j - 1), 0.0)
        return value

    own_line, own_above = own_line_ref[...], own_above_ref[...]
    next_columns, prev_columns = next_columns_ref[...], prev_columns_ref[...]
    own_edges = (own_line, own_above, lambda j: hori_ref[:, (j + 1) * TILE_W - 1 : (j + 1) * TILE_W])
    next_edges = (lines_ref[0:tiles, :], aboves_ref[0:tiles, :], lambda j: next_columns[:, j : j + 1])
    prev_edges = (lines_ref[tiles:, :], aboves_ref[tiles:, :], lambda j: prev_columns[:, j : j + 1])
    for k in range(2):
        for j in range(tiles):
            span = slice(j * TILE_W, (j + 1) * TILE_W)

            def line(n, shift, at=j):
                return spread(n + k, shift)[at : at + 1, :]

            field_ref[k, tiles : tiles + rows, span] = line(2, 0) - alpha * image(own_edges, 4, k, j)
            near = -inside * own_line[j : j + 1, :] * line(4, 0)
            near = near + jnp.where(line_last, spread(8, 1)[j : j + 1, :] * line(6, 1), 0.0)
            far = own_above[j : j + 1, :] * line(4, -1)
            far = far + jnp.where(line_last, spread(9, -1)[j : j + 1, :] * line(6, -1), 0.0)
            if j:
                near = near - jnp.where(line_first, spread(8, 1)[j - 1 : j, :] * line(6, 1, j - 1), 0.0)
                far = far - jnp.where(line_first, spread(9, -1)[j - 1 : j, :] * line(6, -1, j - 1), 0.0)
            field_ref[k, tiles + rows : tiles + rows + 1, span] = line(2, 1) - alpha * near
            field_ref[k, tiles - 1 : tiles, span] = line(2, -1) - alpha * far
    weight_rows, weight_low_rows = spread(10, 0), spread(11, 0)
    for k in range(2):
        flux_left = None
        for j in range(tiles):
            span = slice(j * TILE_W, (j + 1) * TILE_W)
            r = field_ref[k, tiles : tiles + rows, span]
            right = pltpu.roll(r, TILE_W - 1, 1)
            if j < tiles - 1:
                beyond = field_ref[k, tiles : tiles + rows, (j + 1) * TILE_W : (j + 2) * TILE_W]
                right = jnp.where(last_lane, pltpu.roll(beyond, TILE_W - 1, 1), right)
            else:
                right = jnp.where(last_lane, 0.0, right)
            flux = hori_ref[:, span] * (r - right)
            turned = pltpu.roll(flux, 1, 1)
            before = jnp.where(first_lane, 0.0 if flux_left is None else flux_left, turned)
            flux_left = turned
            below = field_ref[k, tiles + 1 : tiles + rows + 1, span]
            fall = vert_ref[:, span] * (r - below)
            edge = own_above[j : j + 1, :] * (field_ref[k, tiles - 1 : tiles, span] - r[0:1, :])
            fall_above = jnp.where(first_row, edge, pltpu.roll(fall, 1, 0))
            applied = flux - before + fall - fall_above
            r_next = spread(12 + k, 0)[j : j + 1, :] - alpha * image(next_edges, 14, k, j)
            r_prev = spread(18 + k, 0)[j : j + 1, :] - alpha * image(prev_edges, 20, k, j)
            applied = applied + weight_rows[j : j + 1, :] * (r - r_next) + weight_low_rows[j : j + 1, :] * (r - r_prev)
            disp_ref[k, :, span] = alpha * spread(k, 0)[j : j + 1, :] + beta * r
            res_ref[k, :, span] = r - beta * applied


def in_vmem(x):
    return pltpu.VMEM(x.shape, x.dtype)


def from_behind(block, axis, distance):
    devices = range(lax.axis_size(axis))
    route = [(i - distance, i) for i in devices if i - distance in devices]
    return lax.ppermute(block, axis, route)


def swap(block, first):
    route = []
    for s in range(first, lax.axis_size(SEC) - 1, 2):
        route += [(s, s + 1), (s + 1, s)]
    return lax.ppermute(block, SEC, route)


def body(fixed_desc, moving_desc, offsets, owner, counts, vert, hori):
    groups = lax.axis_size("group")
    sections = lax.axis_size(SEC)
    chips_z = lax.axis_size("z")
    patches, flow, corr = fixed_desc.shape[1:]
    rows, cols = vert.shape[1:]
    tiles = cols // TILE_W
    length = patches * flow
    halves = tiles * GROUP_LANES // TILE_W

    hbm = pl.BlockSpec(memory_space=pltpu.HBM)
    local = pl.BlockSpec(memory_space=pltpu.VMEM)
    scalars = pl.BlockSpec(memory_space=pltpu.SMEM)
    modest = pltpu.CompilerParams(vmem_limit_bytes=16 << 20)
    border = jax.ShapeDtypeStruct((tiles, TILE_W), F32)
    upright = jax.ShapeDtypeStruct((rows, TILE_W), F32)
    lines_shape = jax.ShapeDtypeStruct((2 * tiles, TILE_W), F32)
    packed = pltpu.VMEM((length // 2 + rows, corr), fixed_desc.dtype)
    across, beside, line = pl.pallas_call(
        pack_kernel,
        out_shape=(packed, packed, in_vmem(border)),
        in_specs=[hbm] * 5,
        out_specs=(local,) * 3,
        scratch_shapes=[
            pltpu.VMEM((rows, cols), F32),
            pltpu.VMEM((rows, cols), F32),
            pltpu.VMEM(offsets.shape[1:], jnp.int32),
            pltpu.SemaphoreType.DMA((2 * PARTS + 3,)),
        ],
        compiler_params=modest,
        name="pack",
    )(
        *(
            pltpu.with_memory_space_constraint(x, pltpu.HBM)
            for x in (moving_desc.reshape(length, corr), fixed_desc.reshape(length, corr), vert, hori, offsets)
        )
    )
    across = swap(across, 1)
    beside = swap(beside, 0)
    above = from_behind(line, "group", 1)

    vert, hori = vert[0], hori[0]

    def borders(*refs):
        border_kernel(groups, *refs)

    table, firsts, right = pl.pallas_call(
        borders,
        out_shape=(in_vmem(border), in_vmem(lines_shape), in_vmem(upright)),
        in_specs=[scalars] * 2 + [local] * 3,
        out_specs=(local,) * 3,
        scratch_shapes=[pltpu.VMEM((TILE_W, TILE_W), F32)],
        compiler_params=modest,
        name="borders",
    )(owner, counts, vert, hori, line)
    mine, lines, next_columns, prev_columns = pl.pallas_call(
        match_kernel,
        out_shape=(
            pltpu.VMEM((chips_z, halves, TILE_W), F32),
            in_vmem(lines_shape), in_vmem(upright), in_vmem(upright),
        ),
        in_specs=[local] * 10,
        out_specs=(local,) * 4,
        scratch_shapes=[pltpu.VMEM((flow, length), F32), pltpu.VMEM((tiles, TILE_W), F32)],
        compiler_params=modest,
        name="match",
    )(fixed_desc, moving_desc, offsets, table, firsts, right, line, above, across, beside)

    seen = lax.all_to_all(mine, "z", 0, 0, tiled=True).reshape(-1, TILE_W)
    lines, seen = lax.optimization_barrier((lines, seen))
    aboves = from_behind(lines, "group", 1)
    peers = groups * lax.axis_size("y")
    copies = pl.pallas_call(
        copies_kernel,
        out_shape=pltpu.VMEM((peers,) + seen.shape, F32),
        in_specs=[local],
        out_specs=local,
        compiler_params=modest,
        name="copies",
    )(seen)
    seen = lax.all_to_all(copies, ("group", "y"), 0, 0, tiled=True).reshape(-1, TILE_W)
    seen = lax.all_gather(seen, "core", axis=0, tiled=True)

    dims = (groups, sections, rows, tiles, chips_z)
    count = groups * tiles

    def both_iterations(*refs):
        stack_kernel(dims, *refs)

    field = jax.ShapeDtypeStruct((2, rows, cols), F32)
    displacement, residual = pl.pallas_call(
        both_iterations,
        out_shape=(field, field),
        in_specs=[local] * 9,
        scratch_shapes=[
            pltpu.VMEM((groups * halves, sections, TILE_W), F32),
            pltpu.VMEM((groups, halves * TILE_W, sections), F32),
            pltpu.VMEM((3, count, sections), F32),
            pltpu.VMEM((24, count + 2 * tiles, sections), F32),
            pltpu.VMEM((2, rows + 2 * tiles, cols), F32),
        ],
        compiler_params=modest,
        name="stack",
    )(seen, vert, hori, line, above, lines, aboves, next_columns, prev_columns)
    return (displacement[None], residual[None])


def solution(mesh):
    groups, sections = mesh.devices.shape
    devices = mesh.devices.reshape(groups, sections // (CHIPS_Y * CORES), CHIPS_Y, CORES)
    fine = Mesh(devices, ("group",) + SEC)
    in_specs = (
        P(SEC, "group", None, None),
        P(SEC, "group", None, None),
        P(SEC, "group", None, None),
        P(SEC, "group"),
        P(SEC, "group"),
        P(SEC, "group", None),
        P(SEC, "group", None),
    )
    out_specs = (P(SEC, None, "group", None), P(SEC, None, "group", None))
    return jax.shard_map(body, mesh=fine, in_specs=in_specs, out_specs=out_specs, check_vma=False)
```

```python
import math

import jax
import jax.numpy as jnp
from jax import lax
from jax.experimental import pallas as pl
from jax.experimental.pallas import tpu as pltpu
from jax.sharding import Mesh, PartitionSpec as P

TILE_W = 128
SPREAD_SQ = 4.0
CHIPS_Y = 4
CORES = 2
SEC = ("z", "y", "core")
F32 = jnp.float32

COLUMN_KV, COLUMN_K2V, COLUMN_KXV, COLUMN_VL, COLUMN_VR, COLUMN_HT, COLUMN_HB = range(7)
COLUMN_DV, COLUMN_XBR, COLUMN_XBL, COLUMN_XTR, COLUMN_XTL = range(7, 12)
COLUMN_KH, COLUMN_K2H, COLUMN_KXH, COLUMN_DH, COLUMN_DT = range(12, 17)
COLUMN_OWNER = 17
COLUMN_NEAR = 19
COLUMN_FAR = 21
COLUMN_HELP = 23
GROUP_LANES = 24
FIRST_GROUP = 2
FIRST_CHIP = (0, 3)
PARTS = 2


def iota(shape, axis):
    return lax.broadcasted_iota(jnp.int32, shape, axis)


def lane_sum(x):
    return jnp.sum(x, axis=1, keepdims=True)


def row_sum(x):
    return jnp.sum(x, axis=0, keepdims=True)


def total(x):
    return lane_sum(row_sum(x))


def three_parts(x):
    high = x.astype(jnp.bfloat16).astype(F32)
    middle = (x - high).astype(jnp.bfloat16).astype(F32)
    return high, middle, x - high - middle


def pack_kernel(
    moving_ref, fixed_ref, vert_ref, hori_ref, offsets_ref, across_ref, beside_ref, line_ref,
    vert, hori, offsets, sems,
):
    rows, cols = hori.shape
    tiles = cols // TILE_W
    length = moving_ref.shape[0] // 2
    part = length // PARTS
    loads = [
        pltpu.make_async_copy(vert_ref.at[0], vert, sems.at[0]),
        pltpu.make_async_copy(hori_ref.at[0], hori, sems.at[1]),
        pltpu.make_async_copy(offsets_ref.at[0], offsets, sems.at[2]),
    ]
    for copy in loads:
        copy.start()

    def features(back, ahead):
        copies = []
        for n in range(PARTS):
            at, behind = pl.ds(n * part, part), pl.ds(length + n * part, part)
            copies.append(pltpu.make_async_copy(moving_ref.at[at], back.at[at], sems.at[3 + 2 * n]))
            copies.append(pltpu.make_async_copy(fixed_ref.at[behind], ahead.at[at], sems.at[4 + 2 * n]))
        return copies

    first = lax.axis_index("core") == 0

    @pl.when(first)
    def _():
        for copy in features(across_ref, beside_ref):
            copy.start()

    @pl.when(jnp.logical_not(first))
    def _():
        for copy in features(beside_ref, across_ref):
            copy.start()

    for copy in loads:
        copy.wait()
    lane = iota((rows, TILE_W), 1)
    column = jnp.zeros((rows, TILE_W), F32)
    for j in range(tiles):
        span = slice(j * TILE_W, (j + 1) * TILE_W)
        line_ref[j : j + 1, :] = vert[rows - 1 : rows, span]
        end = (j + 1) * TILE_W - 1
        column = jnp.where(lane == j, hori[:, end : end + 1], column)
    high, middle, small = three_parts(column)
    columns = high + pltpu.roll(middle, tiles, 1) + pltpu.roll(small, 2 * tiles, 1)
    half = offsets.shape[0] // 2
    shifts = jnp.concatenate([offsets[half:, 0, :], offsets[half:, 1, :]], 1).astype(F32)
    blank = jnp.zeros((tiles, TILE_W), F32)
    for ref in (across_ref, beside_ref):
        for n, value in enumerate(three_parts(line_ref[...])):
            block = jnp.concatenate([value, blank if n else shifts], 0)
            ref[length:, n * TILE_W : (n + 1) * TILE_W] = block.astype(jnp.bfloat16)
        ref[length:, 3 * TILE_W :] = columns.astype(jnp.bfloat16)
    for copy in features(across_ref, beside_ref):
        copy.wait()


def unpack(extra, tiles):
    parts = [extra[:, n * TILE_W : (n + 1) * TILE_W].astype(F32) for n in range(4)]
    line = parts[0][:tiles] + (parts[1][:tiles] + parts[2][:tiles])
    columns = parts[3]
    back = TILE_W - tiles
    columns = columns + (pltpu.roll(columns, back, 1) + pltpu.roll(columns, back - tiles, 1))
    return line, columns, parts[0][tiles:]


def border_kernel(groups, owner_ref, counts_ref, vert_ref, hori_ref, line_ref, out_ref, firsts_ref, right_ref, stack):
    rows, cols = hori_ref.shape
    tiles = cols // TILE_W
    last_group = lax.axis_index("group") == groups - 1
    bottom = jnp.where(last_group, 1.0, 4.0).astype(F32)

    v_last = line_ref[...]
    for j in range(tiles):
        span = slice(j * TILE_W, (j + 1) * TILE_W)
        stack[j : j + 1, :] = vert_ref[rows - 2 : rows - 1, span]
        stack[tiles + j : tiles + j + 1, :] = hori_ref[rows - 1 : rows, span]
        firsts_ref[j : j + 1, :] = vert_ref[0:1, span]
        firsts_ref[tiles + j : tiles + j + 1, :] = hori_ref[0:1, span]
    v_second, h_last = stack[0:tiles, :], stack[tiles : 2 * tiles, :]
    lane = iota((tiles, TILE_W), 1)
    inside = lane < TILE_W - 1
    square = v_last * v_last
    step_last = v_last - pltpu.roll(v_last, TILE_W - 1, 1)
    dh = lane_sum(
        bottom * square * v_last
        + v_second * square
        + jnp.where(inside, h_last * step_last * step_last, 0.0)
    )
    sub = iota((tiles, TILE_W), 0)
    table = jnp.zeros((tiles, TILE_W), F32)
    for p in range(owner_ref.shape[1]):
        live = jnp.where(p < counts_ref[0, 0], owner_ref[0, p], -1).astype(F32)
        spot = (sub == p % tiles) & (lane == COLUMN_OWNER + p // tiles)
        table = jnp.where(spot, live, table)
    for column, value in (
        (COLUMN_KH, lane_sum(v_last)),
        (COLUMN_K2H, lane_sum(square)),
        (COLUMN_DH, dh),
    ):
        table = jnp.where(lane == column, value, table)

    tall = iota((rows, TILE_W), 1)
    zero = jnp.zeros((rows, TILE_W), F32)
    picked = {}
    for name, ref, column in (
        ("h127", hori_ref, TILE_W - 1),
        ("h0", hori_ref, 0),
        ("h126", hori_ref, TILE_W - 2),
        ("v0", vert_ref, 0),
        ("v1", vert_ref, 1),
        ("v126", vert_ref, TILE_W - 2),
        ("v127", vert_ref, TILE_W - 1),
    ):
        value = zero
        for j in range(tiles):
            at = j * TILE_W + column
            value = jnp.where(tall == j, ref[:, at : at + 1], value)
        picked[name] = value
    right = picked["h127"]
    left = pltpu.roll(right, 1, 1)
    row = iota((rows, TILE_W), 0)
    within = row < rows - 1
    inner_tile = iota((1, TILE_W), 1) < tiles - 1
    step_right = right - pltpu.roll(right, rows - 1, 0)
    step_left = left - pltpu.roll(left, rows - 1, 0)
    right_sq, left_sq = right * right, left * left
    side_right = row_sum(
        picked["h126"] * right_sq + jnp.where(within, picked["v127"] * step_right * step_right, 0.0)
    )
    side_left = row_sum(
        picked["h0"] * left_sq + jnp.where(within, picked["v0"] * step_left * step_left, 0.0)
    )
    cube = row_sum(right_sq * right)
    dv = side_right + jnp.where(
        inner_tile, pltpu.roll(side_left, TILE_W - 1, 1) + 4.0 * cube, cube
    )
    end, pre = rows - 1, rows - 2
    v0, v1, v126, v127 = (picked[n] for n in ("v0", "v1", "v126", "v127"))
    h0, h126 = picked["h0"], picked["h126"]

    def at(x, r):
        return x[r : r + 1, :]

    xbr = at(h126, end) * (at(v127, end) - at(v126, end)) * at(right, end) + at(v127, pre) * at(
        v127, end
    ) * (at(right, end) - at(right, pre))
    xbl = -(
        at(h0, end) * (at(v0, end) - at(v1, end)) * at(left, end)
        + at(v0, pre) * at(v0, end) * (at(left, end) - at(left, pre))
    )
    along_last, along_first = at(h126, 0) * at(right, 0), at(h0, 0) * at(left, 0)
    fall_last = at(v127, 0) * (at(right, 0) - at(right, 1))
    fall_first = at(v0, 0) * (at(left, 0) - at(left, 1))
    right_ref[...] = right
    stack[...] = jnp.zeros_like(stack)
    for column, value in (
        (COLUMN_KV, row_sum(right)),
        (COLUMN_K2V, row_sum(right_sq)),
        (COLUMN_VL, at(v0, end)),
        (COLUMN_VR, at(v127, end)),
        (COLUMN_HT, at(right, 0)),
        (COLUMN_HB, at(right, end)),
        (COLUMN_DV, dv),
        (COLUMN_XBR, xbr),
        (COLUMN_XBL, xbl),
        (COLUMN_HELP, -along_last - fall_last),
        (COLUMN_HELP + 1, along_last),
        (COLUMN_HELP + 2, along_first + fall_first),
        (COLUMN_HELP + 3, -along_first),
    ):
        stack[column : column + 1, :] = value
    turned = jnp.transpose(stack[...])[0:tiles, :]
    upright = (lane <= COLUMN_XTL) | (lane >= COLUMN_HELP)
    out_ref[...] = jnp.where(upright, turned, table)


def match_kernel(
    fixed_ref, moving_ref, offsets_ref, table_ref, firsts_ref, right_ref, line_ref, above_ref, across_ref, beside_ref,
    out_ref, lines_ref, next_columns_ref, prev_columns_ref, scores_ref, shifts_ref,
):
    patches, flow, corr = fixed_ref.shape[1:]
    half = patches // 2
    rows = right_ref.shape[0]
    tiles = line_ref.shape[0]
    pair = 2 * flow
    lower = iota((flow, pair), 1) < flow

    def receive(near_ref, far_ref):
        for first in range(0, patches, 2):
            own = slice(first, first + 2)
            if first < half:
                fixed = fixed_ref[0, own].reshape(pair, corr)
                moving = near_ref[first * flow : (first + 2) * flow, :]
            else:
                fixed = far_ref[(first - half) * flow : (first + 2 - half) * flow, :]
                moving = moving_ref[0, own].reshape(pair, corr)
            scores = lax.dot_general(moving, fixed, (((1,), (1,)), ((), ())), preferred_element_type=F32)
            scores_ref[:, first * flow : (first + 2) * flow] = jnp.where(
                lower, scores[0:flow, :], scores[flow:pair, :]
            )
        next_line, next_columns, _ = unpack(near_ref[half * flow :, :], tiles)
        prev_line, prev_columns, shifts = unpack(far_ref[half * flow :, :], tiles)
        lines_ref[0:tiles, :] = next_line
        lines_ref[tiles:, :] = prev_line
        next_columns_ref[...] = next_columns
        prev_columns_ref[...] = prev_columns
        shifts_ref[...] = shifts

    first_core = lax.axis_index("core") == 0

    @pl.when(first_core)
    def _():
        receive(beside_ref, across_ref)

    @pl.when(jnp.logical_not(first_core))
    def _():
        receive(across_ref, beside_ref)

    next_line, next_columns, shifts = lines_ref[0:tiles, :], next_columns_ref[...], shifts_ref[...]
    scores = scores_ref[...]
    top = jnp.max(scores, axis=0, keepdims=True)
    likely = jnp.exp((scores - top) * (1.0 / math.sqrt(corr)))
    offsets = []
    for k in range(2):
        offsets.append(offsets_ref[0, 0:half, k, :].astype(F32))
        offsets.append(shifts[:, k * flow : (k + 1) * flow])
    sums = lax.dot_general(
        jnp.concatenate(offsets, 0),
        likely,
        (((1,), (0,)), ((), ())),
        precision=lax.Precision.HIGHEST,
        preferred_element_type=F32,
    )
    weight = row_sum(likely) * flow
    mine = lax.rem(iota(sums.shape, 0), patches) == lax.div(iota(sums.shape, 1), flow)
    ratio = lane_sum(jnp.where(mine, sums, 0.0) / weight)

    table = table_ref[...]
    lane = iota(table.shape, 1)

    def helper(n):
        return table[:, COLUMN_HELP + n : COLUMN_HELP + n + 1]

    line, above = line_ref[...], above_ref[...]
    step = above - pltpu.roll(above, TILE_W - 1, 1)
    top_energy = firsts_ref[0:tiles, :] * above * above + jnp.where(
        lane < TILE_W - 1, firsts_ref[tiles:, :] * step * step, 0.0
    )
    diagonal = iota(table.shape, 0) == lane
    across = row_sum(right_ref[...] * next_columns)
    columns = [
        (COLUMN_XTR, above[:, TILE_W - 1 :] * helper(0) + above[:, TILE_W - 2 : TILE_W - 1] * helper(1)),
        (COLUMN_XTL, above[:, 0:1] * helper(2) + above[:, 1:2] * helper(3)),
        (COLUMN_DT, lane_sum(top_energy)),
        (COLUMN_KXH, lane_sum(line * next_line)),
        (COLUMN_KXV, lane_sum(jnp.where(diagonal, across, 0.0))),
    ]
    for k in range(2):
        columns.append((COLUMN_NEAR + k, ratio[2 * k * half : (2 * k + 1) * half]))
        columns.append((COLUMN_FAR + k, ratio[(2 * k + 1) * half : (2 * k + 2) * half]))
    for column, value in columns:
        table = jnp.where(lane == column, value, table)

    table = jnp.where(lane < COLUMN_HELP, table, 0.0)
    pieces = [jnp.zeros((1, TILE_W), F32) for _ in range(out_ref.shape[1])]
    place = iota((1, TILE_W), 1)
    for j in range(tiles):
        part, start = divmod(j * GROUP_LANES, TILE_W)
        source = table[j : j + 1, :]
        source = pltpu.roll(source, start, 1) if start else source
        if start + GROUP_LANES > TILE_W:
            pieces[part] = pieces[part] + jnp.where(place >= start, source, 0.0)
            pieces[part + 1] = pieces[part + 1] + jnp.where(place < start, source, 0.0)
        else:
            pieces[part] = pieces[part] + source
    for part, piece in enumerate(pieces):
        for n in range(out_ref.shape[0]):
            out_ref[n, part : part + 1, :] = piece


def copies_kernel(seen_ref, out_ref):
    chips = seen_ref.shape[0] // 2
    half = chips // 2
    first = [seen_ref[pl.ds(n * chips, half, stride=2), :] for n in (1, 0)]
    low = seen_ref[pl.ds(1 + chips, half, stride=2), :]
    high = seen_ref[pl.ds(1, half, stride=2), :]
    second = low + pltpu.roll(high, TILE_W // 2, 1)
    for n in range(out_ref.shape[0]):
        out_ref[n, 0:half, :] = first[0]
        out_ref[n, half:chips, :] = first[1]
        out_ref[n, chips:, :] = second


def stack_kernel(
    dims, seen_ref, vert_ref, hori_ref, own_line_ref, own_above_ref,
    lines_ref, aboves_ref, next_columns_ref, prev_columns_ref,
    disp_ref, res_ref, rows_ref, turn_ref, sums_ref, out_ref, field_ref,
):
    groups, sections, rows, tiles, chips_z = dims
    per_chip = sections // chips_z
    count = groups * tiles
    nodes = float(rows * TILE_W)
    me, group = lax.axis_index(SEC), lax.axis_index("group")

    shared = chips_z // 2
    half_lanes = TILE_W // 2
    for core in range(CORES):
        for g in range(groups):
            for y in range(per_chip // CORES):
                place = core * groups * CHIPS_Y + plane_place(groups, core, g, y)
                base = place * (chips_z + shared)
                chip = y * CORES + core
                rows_ref[g, pl.ds(chip, chips_z, stride=per_chip), :] = seen_ref[base : base + chips_z, :]
                rows_ref[
                    groups + g // 2, pl.ds((g % 2) * (sections // 2) + chip, shared, stride=per_chip), :
                ] = seen_ref[base + chips_z : base + chips_z + shared, :]
    left_half = iota((half_lanes, sections), 1) < sections // 2
    for g in range(groups):
        turn_ref[g, 0:TILE_W, :] = jnp.transpose(rows_ref[g])
    for pair in range(groups // 2):
        turned = jnp.transpose(rows_ref[groups + pair])
        low_half, high_half = turned[0:half_lanes, :], turned[half_lanes:, :]
        turn_ref[2 * pair, TILE_W:, :] = jnp.where(
            left_half, low_half, pltpu.roll(high_half, sections // 2, 1)
        )
        turn_ref[2 * pair + 1, TILE_W:, :] = jnp.where(
            left_half, pltpu.roll(low_half, sections // 2, 1), high_half
        )

    def block(g, column):
        return turn_ref[g, pl.ds(column, tiles, stride=GROUP_LANES), :]

    def figure(column):
        return jnp.concatenate([block(g, column) for g in range(groups)], 0)

    def slots(near, far, turn):
        parts = []
        for g in range(groups):
            parts.append(block(g, near))
            other = block(g, far)
            parts.append(pltpu.roll(other, sections - 1, 1) if turn else other)
        return jnp.concatenate(parts, 0)

    lane = iota((count, sections), 1)
    tile_row = iota((count, sections), 0)
    along = lax.rem(tile_row, tiles)
    not_last = lane < sections - 1

    def up(x):
        return jnp.where(not_last, pltpu.roll(x, sections - 1, 1), 0.0)

    def low(x):
        return jnp.where(lane > 0, pltpu.roll(x, 1, 1), 0.0)

    zero_tiles = jnp.zeros((tiles, sections), F32)

    def from_above(x):
        return jnp.concatenate([zero_tiles, x[: count - tiles]], 0)

    def from_below(x):
        return jnp.concatenate([x[tiles:], zero_tiles], 0)

    def from_left(x):
        return jnp.where(along > 0, pltpu.roll(x, 1, 0), 0.0)

    def from_right(x):
        return jnp.where(along < tiles - 1, pltpu.roll(x, count - 1, 0), 0.0)

    owner = slots(COLUMN_OWNER, COLUMN_OWNER + 1, False)
    targets = [slots(COLUMN_NEAR + k, COLUMN_FAR + k, True) for k in range(2)]
    valid = jnp.where(owner >= 0.0, 1.0, 0.0)

    def tile_sums(miss):
        weight = valid / (1.0 + (miss[0] * miss[0] + miss[1] * miss[1]) / SPREAD_SQ)
        terms = (weight, weight * targets[0], weight * targets[1])
        for t in range(count):
            mine = owner == float(t)
            for n, term in enumerate(terms):
                sums_ref[n, t : t + 1, :] = row_sum(jnp.where(mine, term, 0.0))
        return [jnp.where(not_last, sums_ref[n], 0.0) for n in range(3)]

    kh, kv = figure(COLUMN_KH), figure(COLUMN_KV)
    k2h, k2v = figure(COLUMN_K2H), figure(COLUMN_K2V)
    kxh, kxv = figure(COLUMN_KXH), figure(COLUMN_KXV)
    vl, vr = figure(COLUMN_VL), figure(COLUMN_VR)
    ht, hb = figure(COLUMN_HT), figure(COLUMN_HB)
    dh, dt, dv = figure(COLUMN_DH), figure(COLUMN_DT), figure(COLUMN_DV)
    xbr, xbl, xtr, xtl = (figure(c) for c in (COLUMN_XBR, COLUMN_XBL, COLUMN_XTR, COLUMN_XTL))
    fold_h = jnp.where(tile_row < count - tiles, 2.0, 1.0)
    fold_v = jnp.where(along < tiles - 1, 2.0, 1.0)

    def differences(x):
        return x - from_below(x), x - from_right(x)

    def corners(diff_h, diff_v):
        return (
            (vr * diff_h, hb * diff_v),
            (vl * diff_h, -from_left(hb * diff_v)),
            (-from_above(vr * diff_h), ht * diff_v),
            (-from_above(vl * diff_h), -from_left(ht * diff_v)),
        )

    def tile_product(along_h, along_v, first, second):
        value = along_h + from_above(along_h) + along_v + from_left(along_v)
        for (ah, av), (bh, bv) in zip(first, second):
            value = value + ah * bv + av * bh
        return value

    weight, *pull = tile_sums(targets)
    flat = [e - low(e) for e in pull]
    step = [differences(d) for d in flat]
    gap = [d - up(d) for d in flat]
    norm = total(flat[0] * flat[0] + flat[1] * flat[1]) * nodes
    energy = sum(kh * h * h + kv * v * v for h, v in step)
    energy = energy + nodes * weight * (gap[0] * gap[0] + gap[1] * gap[1])
    alpha = norm / total(energy)

    for k in range(2):
        sums_ref[k] = alpha * gap[k]
    look = [jnp.zeros_like(owner), jnp.zeros_like(owner)]
    for t in range(count):
        mine = owner == float(t)
        for k in range(2):
            look[k] = jnp.where(mine, sums_ref[k, t : t + 1, :], look[k])
    weight, *pull = tile_sums([look[k] - targets[k] for k in range(2)])
    weight_low = low(weight)
    const = [
        pull[k] - low(pull[k]) - alpha * (weight * gap[k] - weight_low * low(gap[k]))
        for k in range(2)
    ]
    plain = jnp.zeros_like(kh)
    mixed = jnp.zeros_like(kh)
    quad = jnp.zeros_like(kh)
    p_energy = jnp.zeros_like(kh)
    m_energy = jnp.zeros_like(kh)
    q_energy = jnp.zeros_like(kh)
    for k in range(2):
        c = const[k]
        ch, cv = differences(c)
        h, v = step[k]
        ends = corners(h, v)
        c_ends = corners(ch, cv)
        square = tile_product(k2h * h * h, k2v * v * v, ends, ends)
        across = tile_product(
            kxh * h * up(h), kxv * v * up(v), ends, [(up(a), up(b)) for a, b in ends]
        )
        gap_square = square + up(square) - 2.0 * across
        flux_h, flux_v = kh * h, kv * v
        inner = flux_h - from_above(flux_h) + flux_v - from_left(flux_v)
        gap_c = c - up(c)
        gap_q = inner - up(inner)
        plain = plain + c * c
        mixed = mixed + c * inner
        quad = quad + square
        p_energy = p_energy + kh * ch * ch + kv * cv * cv + nodes * weight * gap_c * gap_c
        m_energy = (
            m_energy
            + tile_product(k2h * ch * h, k2v * cv * v, c_ends, ends)
            + weight * gap_c * gap_q
        )
        above_h, left_v = from_above(h), from_left(v)
        value = dh * h * h + dt * above_h * above_h + dv * v * v
        value = value + 2.0 * (
            xbr * h * v + xbl * h * left_v + xtr * above_h * v + xtl * above_h * left_v
        )
        (br_h, br_v), (bl_h, bl_v), (tr_h, tr_v), (tl_h, tl_v) = ends
        for stiff, part, extra, fold in (
            (vr, br_h, br_v - from_below(tr_v), fold_h),
            (vl, bl_h, bl_v - from_below(tl_v), fold_h),
            (hb, br_v, br_h - from_right(bl_h), fold_v),
            (ht, tr_v, tr_h - from_right(tl_h), fold_v),
        ):
            value = value + stiff * extra * (2.0 * fold * part + extra)
        q_energy = q_energy + value + weight * gap_square
    norm = nodes * total(plain) - 2.0 * alpha * total(mixed) + alpha * alpha * total(quad)
    energy = total(p_energy) - 2.0 * alpha * total(m_energy) + alpha * alpha * total(q_energy)
    beta = norm / energy

    own_figures = (*flat, *const, step[0][0], step[1][0], step[0][1], step[1][1], ht, hb, weight, weight_low)
    beside = (*const, step[0][0], step[1][0], step[0][1], step[1][1])
    wanted = [(x, me) for x in own_figures] + [(x, me + 1) for x in beside] + [(x, me - 1) for x in beside]
    for n, (x, section) in enumerate(wanted):
        out_ref[n, 0:tiles, :] = zero_tiles
        out_ref[n, tiles + count : 2 * tiles + count, :] = zero_tiles
        picked = lane_sum(jnp.where(lane == section, x, 0.0))
        out_ref[n, tiles : tiles + count, :] = jnp.broadcast_to(picked, (count, sections))

    def spread(n, shift):
        start = pl.multiple_of((group + 1 + shift) * tiles, tiles)
        return out_ref[n, pl.ds(start, tiles), :]

    wide_lane = iota((rows, TILE_W), 1)
    wide_row = iota((rows, TILE_W), 0)
    first_lane, last_lane = wide_lane == 0, wide_lane == TILE_W - 1
    first_row, last_row = wide_row == 0, wide_row == rows - 1
    line_first, line_last = first_lane[0:1], last_lane[0:1]
    inside = jnp.where(group < groups - 1, 1.0, 0.0).astype(F32)

    def image(edges, offset, k, j):
        last_line, above_line, columns = edges
        def line(n, shift=0, at=j):
            return spread(offset + n + k, shift)[at : at + 1, :]

        value = jnp.where(last_row, last_line[j : j + 1, :] * line(0), 0.0)
        value = value - jnp.where(first_row, above_line[j : j + 1, :] * line(0, -1), 0.0)
        value = value + jnp.where(last_lane, columns(j) * line(2), 0.0)
        if j:
            value = value - jnp.where(first_lane, columns(j - 1) * line(2, 0, j - 1), 0.0)
        return value

    own_line, own_above = own_line_ref[...], own_above_ref[...]
    next_columns, prev_columns = next_columns_ref[...], prev_columns_ref[...]
    own_edges = (own_line, own_above, lambda j: hori_ref[:, (j + 1) * TILE_W - 1 : (j + 1) * TILE_W])
    next_edges = (lines_ref[0:tiles, :], aboves_ref[0:tiles, :], lambda j: next_columns[:, j : j + 1])
    prev_edges = (lines_ref[tiles:, :], aboves_ref[tiles:, :], lambda j: prev_columns[:, j : j + 1])
    for k in range(2):
        for j in range(tiles):
            span = slice(j * TILE_W, (j + 1) * TILE_W)

            def line(n, shift, at=j):
                return spread(n + k, shift)[at : at + 1, :]

            field_ref[k, tiles : tiles + rows, span] = line(2, 0) - alpha * image(own_edges, 4, k, j)
            near = -inside * own_line[j : j + 1, :] * line(4, 0)
            near = near + jnp.where(line_last, spread(8, 1)[j : j + 1, :] * line(6, 1), 0.0)
            far = own_above[j : j + 1, :] * line(4, -1)
            far = far + jnp.where(line_last, spread(9, -1)[j : j + 1, :] * line(6, -1), 0.0)
            if j:
                near = near - jnp.where(line_first, spread(8, 1)[j - 1 : j, :] * line(6, 1, j - 1), 0.0)
                far = far - jnp.where(line_first, spread(9, -1)[j - 1 : j, :] * line(6, -1, j - 1), 0.0)
            field_ref[k, tiles + rows : tiles + rows + 1, span] = line(2, 1) - alpha * near
            field_ref[k, tiles - 1 : tiles, span] = line(2, -1) - alpha * far
    weight_rows, weight_low_rows = spread(10, 0), spread(11, 0)
    for k in range(2):
        flux_left = None
        for j in range(tiles):
            span = slice(j * TILE_W, (j + 1) * TILE_W)
            r = field_ref[k, tiles : tiles + rows, span]
            right = pltpu.roll(r, TILE_W - 1, 1)
            if j < tiles - 1:
                beyond = field_ref[k, tiles : tiles + rows, (j + 1) * TILE_W : (j + 2) * TILE_W]
                right = jnp.where(last_lane, pltpu.roll(beyond, TILE_W - 1, 1), right)
            else:
                right = jnp.where(last_lane, 0.0, right)
            flux = hori_ref[:, span] * (r - right)
            turned = pltpu.roll(flux, 1, 1)
            before = jnp.where(first_lane, 0.0 if flux_left is None else flux_left, turned)
            flux_left = turned
            below = field_ref[k, tiles + 1 : tiles + rows + 1, span]
            fall = vert_ref[:, span] * (r - below)
            edge = own_above[j : j + 1, :] * (field_ref[k, tiles - 1 : tiles, span] - r[0:1, :])
            fall_above = jnp.where(first_row, edge, pltpu.roll(fall, 1, 0))
            applied = flux - before + fall - fall_above
            r_next = spread(12 + k, 0)[j : j + 1, :] - alpha * image(next_edges, 14, k, j)
            r_prev = spread(18 + k, 0)[j : j + 1, :] - alpha * image(prev_edges, 20, k, j)
            applied = applied + weight_rows[j : j + 1, :] * (r - r_next) + weight_low_rows[j : j + 1, :] * (r - r_prev)
            disp_ref[k, :, span] = alpha * spread(k, 0)[j : j + 1, :] + beta * r
            res_ref[k, :, span] = r - beta * applied


def in_vmem(x):
    return pltpu.VMEM(x.shape, x.dtype)


def from_behind(block, axis, distance):
    devices = range(lax.axis_size(axis))
    route = [(i - distance, i) for i in devices if i - distance in devices]
    return lax.ppermute(block, axis, route)


def plane_place(groups, core, g, y):
    return (g - FIRST_GROUP) % groups * CHIPS_Y + (y - FIRST_CHIP[core]) % CHIPS_Y


def planes(groups, chips_z):
    lists = []
    for z in range(chips_z):
        for core in range(CORES):
            members = [None] * (groups * CHIPS_Y)
            for g in range(groups):
                for y in range(CHIPS_Y):
                    device = ((g * chips_z + z) * CHIPS_Y + y) * CORES + core
                    members[plane_place(groups, core, g, y)] = device
            lists.append(members)
    return lists


def swap(block, first):
    route = []
    for s in range(first, lax.axis_size(SEC) - 1, 2):
        route += [(s, s + 1), (s + 1, s)]
    return lax.ppermute(block, SEC, route)


def body(fixed_desc, moving_desc, offsets, owner, counts, vert, hori):
    groups = lax.axis_size("group")
    sections = lax.axis_size(SEC)
    chips_z = lax.axis_size("z")
    patches, flow, corr = fixed_desc.shape[1:]
    rows, cols = vert.shape[1:]
    tiles = cols // TILE_W
    length = patches * flow
    halves = -(-tiles * GROUP_LANES // TILE_W)

    hbm = pl.BlockSpec(memory_space=pltpu.HBM)
    local = pl.BlockSpec(memory_space=pltpu.VMEM)
    scalars = pl.BlockSpec(memory_space=pltpu.SMEM)
    modest = pltpu.CompilerParams(vmem_limit_bytes=16 << 20)
    border = jax.ShapeDtypeStruct((tiles, TILE_W), F32)
    upright = jax.ShapeDtypeStruct((rows, TILE_W), F32)
    lines_shape = jax.ShapeDtypeStruct((2 * tiles, TILE_W), F32)
    packed = pltpu.VMEM((length // 2 + rows, corr), fixed_desc.dtype)
    across, beside, line = pl.pallas_call(
        pack_kernel,
        out_shape=(packed, packed, in_vmem(border)),
        in_specs=[hbm] * 5,
        out_specs=(local,) * 3,
        scratch_shapes=[
            pltpu.VMEM((rows, cols), F32),
            pltpu.VMEM((rows, cols), F32),
            pltpu.VMEM(offsets.shape[1:], jnp.int32),
            pltpu.SemaphoreType.DMA((2 * PARTS + 3,)),
        ],
        compiler_params=modest,
        name="pack",
    )(
        *(
            pltpu.with_memory_space_constraint(x, pltpu.HBM)
            for x in (moving_desc.reshape(length, corr), fixed_desc.reshape(length, corr), vert, hori, offsets)
        )
    )
    across = swap(across, 1)
    beside = swap(beside, 0)
    above = from_behind(line, "group", 1)

    vert, hori = vert[0], hori[0]

    def borders(*refs):
        border_kernel(groups, *refs)

    table, firsts, right = pl.pallas_call(
        borders,
        out_shape=(in_vmem(border), in_vmem(lines_shape), in_vmem(upright)),
        in_specs=[scalars] * 2 + [local] * 3,
        out_specs=(local,) * 3,
        scratch_shapes=[pltpu.VMEM((TILE_W, TILE_W), F32)],
        compiler_params=modest,
        name="borders",
    )(owner, counts, vert, hori, line)
    mine, lines, next_columns, prev_columns = pl.pallas_call(
        match_kernel,
        out_shape=(
            pltpu.VMEM((chips_z, halves, TILE_W), F32),
            in_vmem(lines_shape), in_vmem(upright), in_vmem(upright),
        ),
        in_specs=[local] * 10,
        out_specs=(local,) * 4,
        scratch_shapes=[pltpu.VMEM((flow, length), F32), pltpu.VMEM((tiles, TILE_W), F32)],
        compiler_params=modest,
        name="match",
    )(fixed_desc, moving_desc, offsets, table, firsts, right, line, above, across, beside)

    turned = [(z + chips_z // 2) % chips_z for z in range(chips_z)]
    seen = lax.all_to_all(mine, "z", 0, 0, tiled=True, axis_index_groups=[turned]).reshape(-1, TILE_W)
    lines, seen = lax.optimization_barrier((lines, seen))
    aboves = from_behind(lines, "group", 1)
    peers = groups * lax.axis_size("y")
    block_rows = chips_z + chips_z // 2
    copies = pl.pallas_call(
        copies_kernel,
        out_shape=jax.ShapeDtypeStruct((peers, block_rows, TILE_W), F32),
        in_specs=[local],
        out_specs=local,
        compiler_params=modest,
        name="copies",
    )(seen)
    seen = lax.all_to_all(
        copies, ("group",) + SEC, 0, 0, tiled=True, axis_index_groups=planes(groups, chips_z)
    ).reshape(-1, TILE_W)
    seen = lax.all_gather(seen, "core", axis=0, tiled=True)

    dims = (groups, sections, rows, tiles, chips_z)
    count = groups * tiles

    def both_iterations(*refs):
        stack_kernel(dims, *refs)

    field = jax.ShapeDtypeStruct((2, rows, cols), F32)
    displacement, residual = pl.pallas_call(
        both_iterations,
        out_shape=(field, field),
        in_specs=[local] * 9,
        scratch_shapes=[
            pltpu.VMEM((groups + groups // 2, sections, TILE_W), F32),
            pltpu.VMEM((groups, tiles * GROUP_LANES, sections), F32),
            pltpu.VMEM((3, count, sections), F32),
            pltpu.VMEM((24, count + 2 * tiles, sections), F32),
            pltpu.VMEM((2, rows + 2 * tiles, cols), F32),
        ],
        compiler_params=modest,
        name="stack",
    )(seen, vert, hori, line, above, lines, aboves, next_columns, prev_columns)
    return (displacement[None], residual[None])


def solution(mesh):
    groups, sections = mesh.devices.shape
    devices = mesh.devices.reshape(groups, sections // (CHIPS_Y * CORES), CHIPS_Y, CORES)
    fine = Mesh(devices, ("group",) + SEC)
    in_specs = (
        P(SEC, "group", None, None),
        P(SEC, "group", None, None),
        P(SEC, "group", None, None),
        P(SEC, "group"),
        P(SEC, "group"),
        P(SEC, "group", None),
        P(SEC, "group", None),
    )
    out_specs = (P(SEC, None, "group", None), P(SEC, None, "group", None))
    return jax.shard_map(body, mesh=fine, in_specs=in_specs, out_specs=out_specs, check_vma=False)
```

```python
import math

import jax
import jax.numpy as jnp
from jax import lax
from jax.experimental import pallas as pl
from jax.experimental.pallas import tpu as pltpu
from jax.sharding import Mesh, PartitionSpec as P

TILE_W = 128
SPREAD_SQ = 4.0
CHIPS_Y = 4
CORES = 2
SEC = ("z", "y", "core")
F32 = jnp.float32

COLUMN_KV, COLUMN_K2V, COLUMN_KXV, COLUMN_VL, COLUMN_VR, COLUMN_HT, COLUMN_HB = range(7)
COLUMN_DV, COLUMN_XBR, COLUMN_XBL, COLUMN_XTR, COLUMN_XTL = range(7, 12)
COLUMN_KH, COLUMN_K2H, COLUMN_KXH, COLUMN_DH, COLUMN_DT = range(12, 17)
COLUMN_OWNER = 17
COLUMN_NEAR = 19
COLUMN_FAR = 21
COLUMN_HELP = 23
GROUP_LANES = 24
FIRST_Z = 8
FIRST_GROUP = 2
FIRST_CHIP = (2, 2)
ORIGIN = (0, 0)
ORIGIN_PLACE = 15
PARTS = 2


def iota(shape, axis):
    return lax.broadcasted_iota(jnp.int32, shape, axis)


def lane_sum(x):
    return jnp.sum(x, axis=1, keepdims=True)


def row_sum(x):
    return jnp.sum(x, axis=0, keepdims=True)


def total(x):
    return lane_sum(row_sum(x))


def three_parts(x):
    high = x.astype(jnp.bfloat16).astype(F32)
    middle = (x - high).astype(jnp.bfloat16).astype(F32)
    return high, middle, x - high - middle


def pack_kernel(
    moving_ref, fixed_ref, vert_ref, hori_ref, offsets_ref, across_ref, beside_ref, line_ref,
    vert, hori, offsets, sems,
):
    rows, cols = hori.shape
    tiles = cols // TILE_W
    length = moving_ref.shape[0] // 2
    part = length // PARTS
    loads = [
        pltpu.make_async_copy(vert_ref.at[0], vert, sems.at[0]),
        pltpu.make_async_copy(hori_ref.at[0], hori, sems.at[1]),
        pltpu.make_async_copy(offsets_ref.at[0], offsets, sems.at[2]),
    ]
    for copy in loads:
        copy.start()

    def features(back, ahead):
        copies = []
        for n in range(PARTS):
            at, behind = pl.ds(n * part, part), pl.ds(length + n * part, part)
            copies.append(pltpu.make_async_copy(moving_ref.at[at], back.at[at], sems.at[3 + 2 * n]))
            copies.append(pltpu.make_async_copy(fixed_ref.at[behind], ahead.at[at], sems.at[4 + 2 * n]))
        return copies

    first = lax.axis_index("core") == 0

    @pl.when(first)
    def _():
        for copy in features(across_ref, beside_ref):
            copy.start()

    @pl.when(jnp.logical_not(first))
    def _():
        for copy in features(beside_ref, across_ref):
            copy.start()

    for copy in loads:
        copy.wait()
    lane = iota((rows, TILE_W), 1)
    column = jnp.zeros((rows, TILE_W), F32)
    for j in range(tiles):
        span = slice(j * TILE_W, (j + 1) * TILE_W)
        line_ref[j : j + 1, :] = vert[rows - 1 : rows, span]
        end = (j + 1) * TILE_W - 1
        column = jnp.where(lane == j, hori[:, end : end + 1], column)
    high, middle, small = three_parts(column)
    columns = high + pltpu.roll(middle, tiles, 1) + pltpu.roll(small, 2 * tiles, 1)
    half = offsets.shape[0] // 2
    shifts = jnp.concatenate([offsets[half:, 0, :], offsets[half:, 1, :]], 1).astype(F32)
    blank = jnp.zeros((tiles, TILE_W), F32)
    for ref in (across_ref, beside_ref):
        for n, value in enumerate(three_parts(line_ref[...])):
            block = jnp.concatenate([value, blank if n else shifts], 0)
            ref[length:, n * TILE_W : (n + 1) * TILE_W] = block.astype(jnp.bfloat16)
        ref[length:, 3 * TILE_W :] = columns.astype(jnp.bfloat16)
    for copy in features(across_ref, beside_ref):
        copy.wait()


def unpack(extra, tiles):
    parts = [extra[:, n * TILE_W : (n + 1) * TILE_W].astype(F32) for n in range(4)]
    line = parts[0][:tiles] + (parts[1][:tiles] + parts[2][:tiles])
    columns = parts[3]
    back = TILE_W - tiles
    columns = columns + (pltpu.roll(columns, back, 1) + pltpu.roll(columns, back - tiles, 1))
    return line, columns, parts[0][tiles:]


def border_kernel(groups, owner_ref, counts_ref, vert_ref, hori_ref, line_ref, out_ref, firsts_ref, right_ref, stack):
    rows, cols = hori_ref.shape
    tiles = cols // TILE_W
    last_group = lax.axis_index("group") == groups - 1
    bottom = jnp.where(last_group, 1.0, 4.0).astype(F32)

    v_last = line_ref[...]
    for j in range(tiles):
        span = slice(j * TILE_W, (j + 1) * TILE_W)
        stack[j : j + 1, :] = vert_ref[rows - 2 : rows - 1, span]
        stack[tiles + j : tiles + j + 1, :] = hori_ref[rows - 1 : rows, span]
        firsts_ref[j : j + 1, :] = vert_ref[0:1, span]
        firsts_ref[tiles + j : tiles + j + 1, :] = hori_ref[0:1, span]
    v_second, h_last = stack[0:tiles, :], stack[tiles : 2 * tiles, :]
    lane = iota((tiles, TILE_W), 1)
    inside = lane < TILE_W - 1
    square = v_last * v_last
    step_last = v_last - pltpu.roll(v_last, TILE_W - 1, 1)
    dh = lane_sum(
        bottom * square * v_last
        + v_second * square
        + jnp.where(inside, h_last * step_last * step_last, 0.0)
    )
    sub = iota((tiles, TILE_W), 0)
    table = jnp.zeros((tiles, TILE_W), F32)
    for p in range(owner_ref.shape[1]):
        live = jnp.where(p < counts_ref[0, 0], owner_ref[0, p], -1).astype(F32)
        spot = (sub == p % tiles) & (lane == COLUMN_OWNER + p // tiles)
        table = jnp.where(spot, live, table)
    for column, value in (
        (COLUMN_KH, lane_sum(v_last)),
        (COLUMN_K2H, lane_sum(square)),
        (COLUMN_DH, dh),
    ):
        table = jnp.where(lane == column, value, table)

    tall = iota((rows, TILE_W), 1)
    zero = jnp.zeros((rows, TILE_W), F32)
    picked = {}
    for name, ref, column in (
        ("h127", hori_ref, TILE_W - 1),
        ("h0", hori_ref, 0),
        ("h126", hori_ref, TILE_W - 2),
        ("v0", vert_ref, 0),
        ("v1", vert_ref, 1),
        ("v126", vert_ref, TILE_W - 2),
        ("v127", vert_ref, TILE_W - 1),
    ):
        value = zero
        for j in range(tiles):
            at = j * TILE_W + column
            value = jnp.where(tall == j, ref[:, at : at + 1], value)
        picked[name] = value
    right = picked["h127"]
    left = pltpu.roll(right, 1, 1)
    row = iota((rows, TILE_W), 0)
    within = row < rows - 1
    inner_tile = iota((1, TILE_W), 1) < tiles - 1
    step_right = right - pltpu.roll(right, rows - 1, 0)
    step_left = left - pltpu.roll(left, rows - 1, 0)
    right_sq, left_sq = right * right, left * left
    side_right = row_sum(
        picked["h126"] * right_sq + jnp.where(within, picked["v127"] * step_right * step_right, 0.0)
    )
    side_left = row_sum(
        picked["h0"] * left_sq + jnp.where(within, picked["v0"] * step_left * step_left, 0.0)
    )
    cube = row_sum(right_sq * right)
    dv = side_right + jnp.where(
        inner_tile, pltpu.roll(side_left, TILE_W - 1, 1) + 4.0 * cube, cube
    )
    end, pre = rows - 1, rows - 2
    v0, v1, v126, v127 = (picked[n] for n in ("v0", "v1", "v126", "v127"))
    h0, h126 = picked["h0"], picked["h126"]

    def at(x, r):
        return x[r : r + 1, :]

    xbr = at(h126, end) * (at(v127, end) - at(v126, end)) * at(right, end) + at(v127, pre) * at(
        v127, end
    ) * (at(right, end) - at(right, pre))
    xbl = -(
        at(h0, end) * (at(v0, end) - at(v1, end)) * at(left, end)
        + at(v0, pre) * at(v0, end) * (at(left, end) - at(left, pre))
    )
    along_last, along_first = at(h126, 0) * at(right, 0), at(h0, 0) * at(left, 0)
    fall_last = at(v127, 0) * (at(right, 0) - at(right, 1))
    fall_first = at(v0, 0) * (at(left, 0) - at(left, 1))
    right_ref[...] = right
    stack[...] = jnp.zeros_like(stack)
    for column, value in (
        (COLUMN_KV, row_sum(right)),
        (COLUMN_K2V, row_sum(right_sq)),
        (COLUMN_VL, at(v0, end)),
        (COLUMN_VR, at(v127, end)),
        (COLUMN_HT, at(right, 0)),
        (COLUMN_HB, at(right, end)),
        (COLUMN_DV, dv),
        (COLUMN_XBR, xbr),
        (COLUMN_XBL, xbl),
        (COLUMN_HELP, -along_last - fall_last),
        (COLUMN_HELP + 1, along_last),
        (COLUMN_HELP + 2, along_first + fall_first),
        (COLUMN_HELP + 3, -along_first),
    ):
        stack[column : column + 1, :] = value
    turned = jnp.transpose(stack[...])[0:tiles, :]
    upright = (lane <= COLUMN_XTL) | (lane >= COLUMN_HELP)
    out_ref[...] = jnp.where(upright, turned, table)


def match_kernel(
    fixed_ref, moving_ref, offsets_ref, table_ref, firsts_ref, right_ref, line_ref, above_ref, across_ref, beside_ref,
    out_ref, lines_ref, next_columns_ref, prev_columns_ref, scores_ref, shifts_ref,
):
    patches, flow, corr = fixed_ref.shape[1:]
    half = patches // 2
    rows = right_ref.shape[0]
    tiles = line_ref.shape[0]
    pair = 2 * flow
    lower = iota((flow, pair), 1) < flow

    def receive(near_ref, far_ref):
        for first in range(0, patches, 2):
            own = slice(first, first + 2)
            if first < half:
                fixed = fixed_ref[0, own].reshape(pair, corr)
                moving = near_ref[first * flow : (first + 2) * flow, :]
            else:
                fixed = far_ref[(first - half) * flow : (first + 2 - half) * flow, :]
                moving = moving_ref[0, own].reshape(pair, corr)
            scores = lax.dot_general(moving, fixed, (((1,), (1,)), ((), ())), preferred_element_type=F32)
            scores_ref[:, first * flow : (first + 2) * flow] = jnp.where(
                lower, scores[0:flow, :], scores[flow:pair, :]
            )
        next_line, next_columns, _ = unpack(near_ref[half * flow :, :], tiles)
        prev_line, prev_columns, shifts = unpack(far_ref[half * flow :, :], tiles)
        lines_ref[0:tiles, :] = next_line
        lines_ref[tiles:, :] = prev_line
        next_columns_ref[...] = next_columns
        prev_columns_ref[...] = prev_columns
        shifts_ref[...] = shifts

    first_core = lax.axis_index("core") == 0

    @pl.when(first_core)
    def _():
        receive(beside_ref, across_ref)

    @pl.when(jnp.logical_not(first_core))
    def _():
        receive(across_ref, beside_ref)

    next_line, next_columns, shifts = lines_ref[0:tiles, :], next_columns_ref[...], shifts_ref[...]
    scores = scores_ref[...]
    top = jnp.max(scores, axis=0, keepdims=True)
    likely = jnp.exp((scores - top) * (1.0 / math.sqrt(corr)))
    offsets = []
    for k in range(2):
        offsets.append(offsets_ref[0, 0:half, k, :].astype(F32))
        offsets.append(shifts[:, k * flow : (k + 1) * flow])
    shifted = jnp.concatenate(offsets, 0).astype(jnp.bfloat16)
    parts = [part.astype(jnp.bfloat16) for part in three_parts(likely)]
    sums = lax.dot_general(
        jnp.concatenate([shifted] * 3, 1),
        jnp.concatenate(parts, 0),
        (((1,), (0,)), ((), ())),
        preferred_element_type=F32,
    )
    weight = row_sum(likely) * flow
    mine = lax.rem(iota(sums.shape, 0), patches) == lax.div(iota(sums.shape, 1), flow)
    ratio = lane_sum(jnp.where(mine, sums, 0.0) / weight)

    table = table_ref[...]
    lane = iota(table.shape, 1)

    def helper(n):
        return table[:, COLUMN_HELP + n : COLUMN_HELP + n + 1]

    line, above = line_ref[...], above_ref[...]
    step = above - pltpu.roll(above, TILE_W - 1, 1)
    top_energy = firsts_ref[0:tiles, :] * above * above + jnp.where(
        lane < TILE_W - 1, firsts_ref[tiles:, :] * step * step, 0.0
    )
    diagonal = iota(table.shape, 0) == lane
    across = row_sum(right_ref[...] * next_columns)
    columns = [
        (COLUMN_XTR, above[:, TILE_W - 1 :] * helper(0) + above[:, TILE_W - 2 : TILE_W - 1] * helper(1)),
        (COLUMN_XTL, above[:, 0:1] * helper(2) + above[:, 1:2] * helper(3)),
        (COLUMN_DT, lane_sum(top_energy)),
        (COLUMN_KXH, lane_sum(line * next_line)),
        (COLUMN_KXV, lane_sum(jnp.where(diagonal, across, 0.0))),
    ]
    for k in range(2):
        columns.append((COLUMN_NEAR + k, ratio[2 * k * half : (2 * k + 1) * half]))
        columns.append((COLUMN_FAR + k, ratio[(2 * k + 1) * half : (2 * k + 2) * half]))
    for column, value in columns:
        table = jnp.where(lane == column, value, table)

    table = jnp.where(lane < COLUMN_HELP, table, 0.0)
    pieces = [jnp.zeros((1, TILE_W), F32) for _ in range(out_ref.shape[1])]
    place = iota((1, TILE_W), 1)
    for j in range(tiles):
        part, start = divmod(j * GROUP_LANES, TILE_W)
        source = table[j : j + 1, :]
        source = pltpu.roll(source, start, 1) if start else source
        if start + GROUP_LANES > TILE_W:
            pieces[part] = pieces[part] + jnp.where(place >= start, source, 0.0)
            pieces[part + 1] = pieces[part + 1] + jnp.where(place < start, source, 0.0)
        else:
            pieces[part] = pieces[part] + source
    for part, piece in enumerate(pieces):
        for n in range(out_ref.shape[0]):
            out_ref[n, part : part + 1, :] = piece


def copies_kernel(seen_ref, out_ref, block):
    chips = seen_ref.shape[0] // 2
    shared = chips // 2
    lead = chips - FIRST_Z
    block[0:FIRST_Z, :] = seen_ref[pl.ds(2 * lead, FIRST_Z, stride=2), :]
    block[FIRST_Z:chips, :] = seen_ref[pl.ds(0, lead, stride=2), :]
    block[chips : chips + FIRST_Z, :] = seen_ref[pl.ds(2 * lead + 1, FIRST_Z, stride=2), :]
    block[chips + FIRST_Z :, :] = seen_ref[pl.ds(1, lead, stride=2), :]
    first = block[0:chips, :]
    second = block[chips : chips + shared, :] + pltpu.roll(block[chips + shared :, :], TILE_W // 2, 1)
    for n in range(out_ref.shape[0]):
        out_ref[n, 0:chips, :] = first
        out_ref[n, chips:, :] = second


def stack_kernel(
    dims, seen_ref, vert_ref, hori_ref, own_line_ref, own_above_ref,
    lines_ref, aboves_ref, next_columns_ref, prev_columns_ref,
    disp_ref, res_ref, rows_ref, turn_ref, sums_ref, out_ref, field_ref,
):
    groups, sections, rows, tiles, chips_z = dims
    per_chip = sections // chips_z
    count = groups * tiles
    nodes = float(rows * TILE_W)
    me, group = lax.axis_index(SEC), lax.axis_index("group")

    shared = chips_z // 2
    half_lanes = TILE_W // 2
    for core in range(CORES):
        for g in range(groups):
            for y in range(per_chip // CORES):
                place = (CORES - 1 - core) * groups * CHIPS_Y + plane_order(groups, core).index((g, y))
                base = place * (chips_z + shared)
                chip = y * CORES + core
                rows_ref[g, pl.ds(chip, chips_z, stride=per_chip), :] = seen_ref[base : base + chips_z, :]
                rows_ref[
                    groups + g // 2, pl.ds((g % 2) * (sections // 2) + chip, shared, stride=per_chip), :
                ] = seen_ref[base + chips_z : base + chips_z + shared, :]
    left_half = iota((half_lanes, sections), 1) < sections // 2
    for g in range(groups):
        turn_ref[g, 0:TILE_W, :] = jnp.transpose(rows_ref[g])
    for pair in range(groups // 2):
        turned = jnp.transpose(rows_ref[groups + pair])
        low_half, high_half = turned[0:half_lanes, :], turned[half_lanes:, :]
        turn_ref[2 * pair, TILE_W:, :] = jnp.where(
            left_half, low_half, pltpu.roll(high_half, sections // 2, 1)
        )
        turn_ref[2 * pair + 1, TILE_W:, :] = jnp.where(
            left_half, pltpu.roll(low_half, sections // 2, 1), high_half
        )

    def block(g, column):
        return turn_ref[g, pl.ds(column, tiles, stride=GROUP_LANES), :]

    def figure(column):
        return jnp.concatenate([block(g, column) for g in range(groups)], 0)

    def slots(near, far, turn):
        parts = []
        for g in range(groups):
            parts.append(block(g, near))
            other = block(g, far)
            parts.append(pltpu.roll(other, sections - 1, 1) if turn else other)
        return jnp.concatenate(parts, 0)

    lane = iota((count, sections), 1)
    tile_row = iota((count, sections), 0)
    along = lax.rem(tile_row, tiles)
    not_last = lane < sections - 1

    def up(x):
        return jnp.where(not_last, pltpu.roll(x, sections - 1, 1), 0.0)

    def low(x):
        return jnp.where(lane > 0, pltpu.roll(x, 1, 1), 0.0)

    zero_tiles = jnp.zeros((tiles, sections), F32)

    def from_above(x):
        return jnp.concatenate([zero_tiles, x[: count - tiles]], 0)

    def from_below(x):
        return jnp.concatenate([x[tiles:], zero_tiles], 0)

    def from_left(x):
        return jnp.where(along > 0, pltpu.roll(x, 1, 0), 0.0)

    def from_right(x):
        return jnp.where(along < tiles - 1, pltpu.roll(x, count - 1, 0), 0.0)

    owner = slots(COLUMN_OWNER, COLUMN_OWNER + 1, False)
    targets = [slots(COLUMN_NEAR + k, COLUMN_FAR + k, True) for k in range(2)]
    valid = jnp.where(owner >= 0.0, 1.0, 0.0)

    def tile_sums(miss):
        weight = valid / (1.0 + (miss[0] * miss[0] + miss[1] * miss[1]) / SPREAD_SQ)
        terms = (weight, weight * targets[0], weight * targets[1])
        for t in range(count):
            mine = owner == float(t)
            for n, term in enumerate(terms):
                sums_ref[n, t : t + 1, :] = row_sum(jnp.where(mine, term, 0.0))
        return [jnp.where(not_last, sums_ref[n], 0.0) for n in range(3)]

    kh, kv = figure(COLUMN_KH), figure(COLUMN_KV)
    k2h, k2v = figure(COLUMN_K2H), figure(COLUMN_K2V)
    kxh, kxv = figure(COLUMN_KXH), figure(COLUMN_KXV)
    vl, vr = figure(COLUMN_VL), figure(COLUMN_VR)
    ht, hb = figure(COLUMN_HT), figure(COLUMN_HB)
    dh, dt, dv = figure(COLUMN_DH), figure(COLUMN_DT), figure(COLUMN_DV)
    xbr, xbl, xtr, xtl = (figure(c) for c in (COLUMN_XBR, COLUMN_XBL, COLUMN_XTR, COLUMN_XTL))
    fold_h = jnp.where(tile_row < count - tiles, 2.0, 1.0)
    fold_v = jnp.where(along < tiles - 1, 2.0, 1.0)

    def differences(x):
        return x - from_below(x), x - from_right(x)

    def corners(diff_h, diff_v):
        return (
            (vr * diff_h, hb * diff_v),
            (vl * diff_h, -from_left(hb * diff_v)),
            (-from_above(vr * diff_h), ht * diff_v),
            (-from_above(vl * diff_h), -from_left(ht * diff_v)),
        )

    def tile_product(along_h, along_v, first, second):
        value = along_h + from_above(along_h) + along_v + from_left(along_v)
        for (ah, av), (bh, bv) in zip(first, second):
            value = value + ah * bv + av * bh
        return value

    weight, *pull = tile_sums(targets)
    flat = [e - low(e) for e in pull]
    step = [differences(d) for d in flat]
    gap = [d - up(d) for d in flat]
    norm = total(flat[0] * flat[0] + flat[1] * flat[1]) * nodes
    energy = sum(kh * h * h + kv * v * v for h, v in step)
    energy = energy + nodes * weight * (gap[0] * gap[0] + gap[1] * gap[1])
    alpha = norm / total(energy)

    index = jnp.maximum(owner, 0.0).astype(jnp.int32)
    inside_index = lax.rem(index, tiles)
    row_index = lax.div(index, tiles)
    look = []
    for k in range(2):
        shift = alpha * gap[k]
        rows_of = []
        for p in range(0, owner.shape[0], tiles):
            value = jnp.zeros((tiles, sections), F32)
            for g in range(groups):
                picked = jnp.take_along_axis(
                    shift[g * tiles : (g + 1) * tiles], inside_index[p : p + tiles], axis=0
                )
                value = jnp.where(row_index[p : p + tiles] == g, picked, value)
            rows_of.append(value)
        look.append(jnp.concatenate(rows_of, 0))
    weight, *pull = tile_sums([look[k] - targets[k] for k in range(2)])
    weight_low = low(weight)
    const = [
        pull[k] - low(pull[k]) - alpha * (weight * gap[k] - weight_low * low(gap[k]))
        for k in range(2)
    ]
    plain = jnp.zeros_like(kh)
    mixed = jnp.zeros_like(kh)
    quad = jnp.zeros_like(kh)
    p_energy = jnp.zeros_like(kh)
    m_energy = jnp.zeros_like(kh)
    q_energy = jnp.zeros_like(kh)
    for k in range(2):
        c = const[k]
        ch, cv = differences(c)
        h, v = step[k]
        ends = corners(h, v)
        c_ends = corners(ch, cv)
        square = tile_product(k2h * h * h, k2v * v * v, ends, ends)
        across = tile_product(
            kxh * h * up(h), kxv * v * up(v), ends, [(up(a), up(b)) for a, b in ends]
        )
        gap_square = square + up(square) - 2.0 * across
        flux_h, flux_v = kh * h, kv * v
        inner = flux_h - from_above(flux_h) + flux_v - from_left(flux_v)
        gap_c = c - up(c)
        gap_q = inner - up(inner)
        plain = plain + c * c
        mixed = mixed + c * inner
        quad = quad + square
        p_energy = p_energy + kh * ch * ch + kv * cv * cv + nodes * weight * gap_c * gap_c
        m_energy = (
            m_energy
            + tile_product(k2h * ch * h, k2v * cv * v, c_ends, ends)
            + weight * gap_c * gap_q
        )
        above_h, left_v = from_above(h), from_left(v)
        value = dh * h * h + dt * above_h * above_h + dv * v * v
        value = value + 2.0 * (
            xbr * h * v + xbl * h * left_v + xtr * above_h * v + xtl * above_h * left_v
        )
        (br_h, br_v), (bl_h, bl_v), (tr_h, tr_v), (tl_h, tl_v) = ends
        for stiff, part, extra, fold in (
            (vr, br_h, br_v - from_below(tr_v), fold_h),
            (vl, bl_h, bl_v - from_below(tl_v), fold_h),
            (hb, br_v, br_h - from_right(bl_h), fold_v),
            (ht, tr_v, tr_h - from_right(tl_h), fold_v),
        ):
            value = value + stiff * extra * (2.0 * fold * part + extra)
        q_energy = q_energy + value + weight * gap_square
    norm = nodes * total(plain) - 2.0 * alpha * total(mixed) + alpha * alpha * total(quad)
    energy = total(p_energy) - 2.0 * alpha * total(m_energy) + alpha * alpha * total(q_energy)
    beta = norm / energy

    own_figures = (*flat, *const, step[0][0], step[1][0], step[0][1], step[1][1], ht, hb, weight, weight_low)
    beside = (*const, step[0][0], step[1][0], step[0][1], step[1][1])
    wanted = [(x, me) for x in own_figures] + [(x, me + 1) for x in beside] + [(x, me - 1) for x in beside]
    for n, (x, section) in enumerate(wanted):
        out_ref[n, 0:tiles, :] = zero_tiles
        out_ref[n, tiles + count : 2 * tiles + count, :] = zero_tiles
        picked = lane_sum(jnp.where(lane == section, x, 0.0))
        out_ref[n, tiles : tiles + count, :] = jnp.broadcast_to(picked, (count, sections))

    def spread(n, shift):
        start = pl.multiple_of((group + 1 + shift) * tiles, tiles)
        return out_ref[n, pl.ds(start, tiles), :]

    wide_lane = iota((rows, TILE_W), 1)
    wide_row = iota((rows, TILE_W), 0)
    first_lane, last_lane = wide_lane == 0, wide_lane == TILE_W - 1
    first_row, last_row = wide_row == 0, wide_row == rows - 1
    line_first, line_last = first_lane[0:1], last_lane[0:1]
    inside = jnp.where(group < groups - 1, 1.0, 0.0).astype(F32)

    def image(edges, offset, k, j):
        last_line, above_line, columns = edges
        def line(n, shift=0, at=j):
            return spread(offset + n + k, shift)[at : at + 1, :]

        value = jnp.where(last_row, last_line[j : j + 1, :] * line(0), 0.0)
        value = value - jnp.where(first_row, above_line[j : j + 1, :] * line(0, -1), 0.0)
        value = value + jnp.where(last_lane, columns(j) * line(2), 0.0)
        if j:
            value = value - jnp.where(first_lane, columns(j - 1) * line(2, 0, j - 1), 0.0)
        return value

    own_line, own_above = own_line_ref[...], own_above_ref[...]
    next_columns, prev_columns = next_columns_ref[...], prev_columns_ref[...]
    own_edges = (own_line, own_above, lambda j: hori_ref[:, (j + 1) * TILE_W - 1 : (j + 1) * TILE_W])
    next_edges = (lines_ref[0:tiles, :], aboves_ref[0:tiles, :], lambda j: next_columns[:, j : j + 1])
    prev_edges = (lines_ref[tiles:, :], aboves_ref[tiles:, :], lambda j: prev_columns[:, j : j + 1])
    for k in range(2):
        for j in range(tiles):
            span = slice(j * TILE_W, (j + 1) * TILE_W)

            def line(n, shift, at=j):
                return spread(n + k, shift)[at : at + 1, :]

            field_ref[k, tiles : tiles + rows, span] = line(2, 0) - alpha * image(own_edges, 4, k, j)
            near = -inside * own_line[j : j + 1, :] * line(4, 0)
            near = near + jnp.where(line_last, spread(8, 1)[j : j + 1, :] * line(6, 1), 0.0)
            far = own_above[j : j + 1, :] * line(4, -1)
            far = far + jnp.where(line_last, spread(9, -1)[j : j + 1, :] * line(6, -1), 0.0)
            if j:
                near = near - jnp.where(line_first, spread(8, 1)[j - 1 : j, :] * line(6, 1, j - 1), 0.0)
                far = far - jnp.where(line_first, spread(9, -1)[j - 1 : j, :] * line(6, -1, j - 1), 0.0)
            field_ref[k, tiles + rows : tiles + rows + 1, span] = line(2, 1) - alpha * near
            field_ref[k, tiles - 1 : tiles, span] = line(2, -1) - alpha * far
    weight_rows, weight_low_rows = spread(10, 0), spread(11, 0)
    for k in range(2):
        flux_left = None
        for j in range(tiles):
            span = slice(j * TILE_W, (j + 1) * TILE_W)
            r = field_ref[k, tiles : tiles + rows, span]
            right = pltpu.roll(r, TILE_W - 1, 1)
            if j < tiles - 1:
                beyond = field_ref[k, tiles : tiles + rows, (j + 1) * TILE_W : (j + 2) * TILE_W]
                right = jnp.where(last_lane, pltpu.roll(beyond, TILE_W - 1, 1), right)
            else:
                right = jnp.where(last_lane, 0.0, right)
            flux = hori_ref[:, span] * (r - right)
            turned = pltpu.roll(flux, 1, 1)
            before = jnp.where(first_lane, 0.0 if flux_left is None else flux_left, turned)
            flux_left = turned
            below = field_ref[k, tiles + 1 : tiles + rows + 1, span]
            fall = vert_ref[:, span] * (r - below)
            edge = own_above[j : j + 1, :] * (field_ref[k, tiles - 1 : tiles, span] - r[0:1, :])
            fall_above = jnp.where(first_row, edge, pltpu.roll(fall, 1, 0))
            applied = flux - before + fall - fall_above
            r_next = spread(12 + k, 0)[j : j + 1, :] - alpha * image(next_edges, 14, k, j)
            r_prev = spread(18 + k, 0)[j : j + 1, :] - alpha * image(prev_edges, 20, k, j)
            applied = applied + weight_rows[j : j + 1, :] * (r - r_next) + weight_low_rows[j : j + 1, :] * (r - r_prev)
            disp_ref[k, :, span] = alpha * spread(k, 0)[j : j + 1, :] + beta * r
            res_ref[k, :, span] = r - beta * applied


def in_vmem(x):
    return pltpu.VMEM(x.shape, x.dtype)


def from_behind(block, axis, distance):
    devices = range(lax.axis_size(axis))
    route = [(i - distance, i) for i in devices if i - distance in devices]
    return lax.ppermute(block, axis, route)


def plane_order(groups, core):
    order = [
        ((FIRST_GROUP + g) % groups, (FIRST_CHIP[core] + y) % CHIPS_Y)
        for g in range(groups)
        for y in range(CHIPS_Y)
    ]
    order.remove(ORIGIN)
    order.insert(ORIGIN_PLACE, ORIGIN)
    return order


def planes(groups, chips_z):
    return [
        [((g * chips_z + z) * CHIPS_Y + y) * CORES + core for g, y in plane_order(groups, core)]
        for z in range(chips_z)
        for core in range(CORES)
    ]


def swap(block, first):
    route = []
    for s in range(first, lax.axis_size(SEC) - 1, 2):
        route += [(s, s + 1), (s + 1, s)]
    return lax.ppermute(block, SEC, route)


def body(fixed_desc, moving_desc, offsets, owner, counts, vert, hori):
    groups = lax.axis_size("group")
    sections = lax.axis_size(SEC)
    chips_z = lax.axis_size("z")
    patches, flow, corr = fixed_desc.shape[1:]
    rows, cols = vert.shape[1:]
    tiles = cols // TILE_W
    length = patches * flow
    halves = -(-tiles * GROUP_LANES // TILE_W)

    hbm = pl.BlockSpec(memory_space=pltpu.HBM)
    local = pl.BlockSpec(memory_space=pltpu.VMEM)
    scalars = pl.BlockSpec(memory_space=pltpu.SMEM)
    modest = pltpu.CompilerParams(vmem_limit_bytes=16 << 20)
    border = jax.ShapeDtypeStruct((tiles, TILE_W), F32)
    upright = jax.ShapeDtypeStruct((rows, TILE_W), F32)
    lines_shape = jax.ShapeDtypeStruct((2 * tiles, TILE_W), F32)
    packed = pltpu.VMEM((length // 2 + rows, corr), fixed_desc.dtype)
    across, beside, line = pl.pallas_call(
        pack_kernel,
        out_shape=(packed, packed, in_vmem(border)),
        in_specs=[hbm] * 5,
        out_specs=(local,) * 3,
        scratch_shapes=[
            pltpu.VMEM((rows, cols), F32),
            pltpu.VMEM((rows, cols), F32),
            pltpu.VMEM(offsets.shape[1:], jnp.int32),
            pltpu.SemaphoreType.DMA((2 * PARTS + 3,)),
        ],
        compiler_params=modest,
        name="pack",
    )(
        *(
            pltpu.with_memory_space_constraint(x, pltpu.HBM)
            for x in (moving_desc.reshape(length, corr), fixed_desc.reshape(length, corr), vert, hori, offsets)
        )
    )
    across = swap(across, 1)
    beside = swap(beside, 0)
    above = from_behind(line, "group", 1)

    vert, hori = vert[0], hori[0]

    def borders(*refs):
        border_kernel(groups, *refs)

    table, firsts, right = pl.pallas_call(
        borders,
        out_shape=(in_vmem(border), in_vmem(lines_shape), in_vmem(upright)),
        in_specs=[scalars] * 2 + [local] * 3,
        out_specs=(local,) * 3,
        scratch_shapes=[pltpu.VMEM((TILE_W, TILE_W), F32)],
        compiler_params=modest,
        name="borders",
    )(owner, counts, vert, hori, line)
    mine, lines, next_columns, prev_columns = pl.pallas_call(
        match_kernel,
        out_shape=(
            pltpu.VMEM((chips_z, halves, TILE_W), F32),
            in_vmem(lines_shape), in_vmem(upright), in_vmem(upright),
        ),
        in_specs=[local] * 10,
        out_specs=(local,) * 4,
        scratch_shapes=[pltpu.VMEM((flow, length), F32), pltpu.VMEM((tiles, TILE_W), F32)],
        compiler_params=modest,
        name="match",
    )(fixed_desc, moving_desc, offsets, table, firsts, right, line, above, across, beside)

    turned = [(z + FIRST_Z) % chips_z for z in range(chips_z)]
    seen = lax.all_to_all(mine, "z", 0, 0, tiled=True, axis_index_groups=[turned]).reshape(-1, TILE_W)
    lines, seen = lax.optimization_barrier((lines, seen))
    aboves = from_behind(lines, "group", 1)
    peers = groups * lax.axis_size("y")
    block_rows = chips_z + chips_z // 2
    copies = pl.pallas_call(
        copies_kernel,
        out_shape=jax.ShapeDtypeStruct((peers, block_rows, TILE_W), F32),
        in_specs=[local],
        out_specs=local,
        scratch_shapes=[pltpu.VMEM((2 * chips_z, TILE_W), F32)],
        compiler_params=modest,
        name="copies",
    )(seen)
    seen = lax.all_to_all(
        copies, ("group",) + SEC, 0, 0, tiled=True, axis_index_groups=planes(groups, chips_z)
    ).reshape(-1, TILE_W)
    cores = list(reversed(range(CORES)))
    seen = lax.all_gather(seen, "core", axis=0, tiled=True, axis_index_groups=[cores])

    dims = (groups, sections, rows, tiles, chips_z)
    count = groups * tiles

    def both_iterations(*refs):
        stack_kernel(dims, *refs)

    field = jax.ShapeDtypeStruct((2, rows, cols), F32)
    displacement, residual = pl.pallas_call(
        both_iterations,
        out_shape=(field, field),
        in_specs=[local] * 9,
        scratch_shapes=[
            pltpu.VMEM((groups + groups // 2, sections, TILE_W), F32),
            pltpu.VMEM((groups, tiles * GROUP_LANES, sections), F32),
            pltpu.VMEM((3, count, sections), F32),
            pltpu.VMEM((24, count + 2 * tiles, sections), F32),
            pltpu.VMEM((2, rows + 2 * tiles, cols), F32),
        ],
        compiler_params=modest,
        name="stack",
    )(seen, vert, hori, line, above, lines, aboves, next_columns, prev_columns)
    return (displacement[None], residual[None])


def solution(mesh):
    groups, sections = mesh.devices.shape
    devices = mesh.devices.reshape(groups, sections // (CHIPS_Y * CORES), CHIPS_Y, CORES)
    fine = Mesh(devices, ("group",) + SEC)
    in_specs = (
        P(SEC, "group", None, None),
        P(SEC, "group", None, None),
        P(SEC, "group", None, None),
        P(SEC, "group"),
        P(SEC, "group"),
        P(SEC, "group", None),
        P(SEC, "group", None),
    )
    out_specs = (P(SEC, None, "group", None), P(SEC, None, "group", None))
    return jax.shard_map(body, mesh=fine, in_specs=in_specs, out_specs=out_specs, check_vma=False)
```

```python
import math

import jax
import jax.numpy as jnp
from jax import lax
from jax.experimental import pallas as pl
from jax.experimental.pallas import tpu as pltpu
from jax.sharding import Mesh, PartitionSpec as P

TILE_W = 128
SPREAD_SQ = 4.0
CHIPS_Y = 4
CORES = 2
SEC = ("z", "y", "core")
F32 = jnp.float32

COLUMN_KV, COLUMN_K2V, COLUMN_KXV, COLUMN_VL, COLUMN_VR, COLUMN_HT, COLUMN_HB = range(7)
COLUMN_DV, COLUMN_XBR, COLUMN_XBL, COLUMN_XTR, COLUMN_XTL = range(7, 12)
COLUMN_KH, COLUMN_K2H, COLUMN_KXH, COLUMN_DH, COLUMN_DT = range(12, 17)
COLUMN_OWNER = 17
COLUMN_NEAR = 19
COLUMN_FAR = 21
COLUMN_HELP = 23
GROUP_LANES = 24
FIRST_Z = 8
FIRST_GROUP = 2
FIRST_CHIP = (2, 2)
ORIGIN = (0, 0)
ORIGIN_PLACE = 15
PARTS = 2
OWN_PARTS = 4


def iota(shape, axis):
    return lax.broadcasted_iota(jnp.int32, shape, axis)


def lane_sum(x):
    return jnp.sum(x, axis=1, keepdims=True)


def row_sum(x):
    return jnp.sum(x, axis=0, keepdims=True)


def total(x):
    return lane_sum(row_sum(x))


def three_parts(x):
    high = x.astype(jnp.bfloat16).astype(F32)
    middle = (x - high).astype(jnp.bfloat16).astype(F32)
    return high, middle, x - high - middle


def pack_kernel(
    moving_ref, fixed_ref, vert_ref, hori_ref, offsets_ref, across_ref, beside_ref, line_ref,
    vert, hori, offsets, sems,
):
    rows, cols = hori.shape
    tiles = cols // TILE_W
    length = moving_ref.shape[0] // 2
    part = length // PARTS
    loads = [
        pltpu.make_async_copy(vert_ref.at[0], vert, sems.at[0]),
        pltpu.make_async_copy(hori_ref.at[0], hori, sems.at[1]),
        pltpu.make_async_copy(offsets_ref.at[0], offsets, sems.at[2]),
    ]
    for copy in loads:
        copy.start()

    def features(back, ahead):
        copies = []
        for n in range(PARTS):
            at, behind = pl.ds(n * part, part), pl.ds(length + n * part, part)
            copies.append(pltpu.make_async_copy(moving_ref.at[at], back.at[at], sems.at[3 + 2 * n]))
            copies.append(pltpu.make_async_copy(fixed_ref.at[behind], ahead.at[at], sems.at[4 + 2 * n]))
        return copies

    first = lax.axis_index("core") == 0

    @pl.when(first)
    def _():
        for copy in features(across_ref, beside_ref):
            copy.start()

    @pl.when(jnp.logical_not(first))
    def _():
        for copy in features(beside_ref, across_ref):
            copy.start()

    for copy in loads:
        copy.wait()
    lane = iota((rows, TILE_W), 1)
    column = jnp.zeros((rows, TILE_W), F32)
    for j in range(tiles):
        span = slice(j * TILE_W, (j + 1) * TILE_W)
        line_ref[j : j + 1, :] = vert[rows - 1 : rows, span]
        end = (j + 1) * TILE_W - 1
        column = jnp.where(lane == j, hori[:, end : end + 1], column)
    high, middle, small = three_parts(column)
    columns = high + pltpu.roll(middle, tiles, 1) + pltpu.roll(small, 2 * tiles, 1)
    half = offsets.shape[0] // 2
    shifts = jnp.concatenate([offsets[half:, 0, :], offsets[half:, 1, :]], 1).astype(F32)
    blank = jnp.zeros((tiles, TILE_W), F32)
    for ref in (across_ref, beside_ref):
        for n, value in enumerate(three_parts(line_ref[...])):
            block = jnp.concatenate([value, blank if n else shifts], 0)
            ref[length:, n * TILE_W : (n + 1) * TILE_W] = block.astype(jnp.bfloat16)
        ref[length:, 3 * TILE_W :] = columns.astype(jnp.bfloat16)
    for copy in features(across_ref, beside_ref):
        copy.wait()


def unpack(extra, tiles):
    parts = [extra[:, n * TILE_W : (n + 1) * TILE_W].astype(F32) for n in range(4)]
    line = parts[0][:tiles] + (parts[1][:tiles] + parts[2][:tiles])
    columns = parts[3]
    back = TILE_W - tiles
    columns = columns + (pltpu.roll(columns, back, 1) + pltpu.roll(columns, back - tiles, 1))
    return line, columns, parts[0][tiles:]


def border_kernel(
    groups, owner_ref, counts_ref, vert_ref, hori_ref, line_ref, fixed_ref, moving_ref,
    out_ref, firsts_ref, right_ref, own_fixed_ref, own_moving_ref, stack, sems,
):
    length = own_fixed_ref.shape[0]
    part = length // OWN_PARTS
    own = []
    for n in range(OWN_PARTS):
        at, behind = pl.ds(n * part, part), pl.ds(length + n * part, part)
        own.append(pltpu.make_async_copy(fixed_ref.at[at], own_fixed_ref.at[at], sems.at[2 * n]))
        own.append(pltpu.make_async_copy(moving_ref.at[behind], own_moving_ref.at[at], sems.at[2 * n + 1]))
    for copy in own:
        copy.start()
    rows, cols = hori_ref.shape
    tiles = cols // TILE_W
    last_group = lax.axis_index("group") == groups - 1
    bottom = jnp.where(last_group, 1.0, 4.0).astype(F32)

    v_last = line_ref[...]
    for j in range(tiles):
        span = slice(j * TILE_W, (j + 1) * TILE_W)
        stack[j : j + 1, :] = vert_ref[rows - 2 : rows - 1, span]
        stack[tiles + j : tiles + j + 1, :] = hori_ref[rows - 1 : rows, span]
        firsts_ref[j : j + 1, :] = vert_ref[0:1, span]
        firsts_ref[tiles + j : tiles + j + 1, :] = hori_ref[0:1, span]
    v_second, h_last = stack[0:tiles, :], stack[tiles : 2 * tiles, :]
    lane = iota((tiles, TILE_W), 1)
    inside = lane < TILE_W - 1
    square = v_last * v_last
    step_last = v_last - pltpu.roll(v_last, TILE_W - 1, 1)
    dh = lane_sum(
        bottom * square * v_last
        + v_second * square
        + jnp.where(inside, h_last * step_last * step_last, 0.0)
    )
    sub = iota((tiles, TILE_W), 0)
    table = jnp.zeros((tiles, TILE_W), F32)
    for p in range(owner_ref.shape[1]):
        live = jnp.where(p < counts_ref[0, 0], owner_ref[0, p], -1).astype(F32)
        spot = (sub == p % tiles) & (lane == COLUMN_OWNER + p // tiles)
        table = jnp.where(spot, live, table)
    for column, value in (
        (COLUMN_KH, lane_sum(v_last)),
        (COLUMN_K2H, lane_sum(square)),
        (COLUMN_DH, dh),
    ):
        table = jnp.where(lane == column, value, table)

    tall = iota((rows, TILE_W), 1)
    zero = jnp.zeros((rows, TILE_W), F32)
    picked = {}
    for name, ref, column in (
        ("h127", hori_ref, TILE_W - 1),
        ("h0", hori_ref, 0),
        ("h126", hori_ref, TILE_W - 2),
        ("v0", vert_ref, 0),
        ("v1", vert_ref, 1),
        ("v126", vert_ref, TILE_W - 2),
        ("v127", vert_ref, TILE_W - 1),
    ):
        value = zero
        for j in range(tiles):
            at = j * TILE_W + column
            value = jnp.where(tall == j, ref[:, at : at + 1], value)
        picked[name] = value
    right = picked["h127"]
    left = pltpu.roll(right, 1, 1)
    row = iota((rows, TILE_W), 0)
    within = row < rows - 1
    inner_tile = iota((1, TILE_W), 1) < tiles - 1
    step_right = right - pltpu.roll(right, rows - 1, 0)
    step_left = left - pltpu.roll(left, rows - 1, 0)
    right_sq, left_sq = right * right, left * left
    side_right = row_sum(
        picked["h126"] * right_sq + jnp.where(within, picked["v127"] * step_right * step_right, 0.0)
    )
    side_left = row_sum(
        picked["h0"] * left_sq + jnp.where(within, picked["v0"] * step_left * step_left, 0.0)
    )
    cube = row_sum(right_sq * right)
    dv = side_right + jnp.where(
        inner_tile, pltpu.roll(side_left, TILE_W - 1, 1) + 4.0 * cube, cube
    )
    end, pre = rows - 1, rows - 2
    v0, v1, v126, v127 = (picked[n] for n in ("v0", "v1", "v126", "v127"))
    h0, h126 = picked["h0"], picked["h126"]

    def at(x, r):
        return x[r : r + 1, :]

    xbr = at(h126, end) * (at(v127, end) - at(v126, end)) * at(right, end) + at(v127, pre) * at(
        v127, end
    ) * (at(right, end) - at(right, pre))
    xbl = -(
        at(h0, end) * (at(v0, end) - at(v1, end)) * at(left, end)
        + at(v0, pre) * at(v0, end) * (at(left, end) - at(left, pre))
    )
    along_last, along_first = at(h126, 0) * at(right, 0), at(h0, 0) * at(left, 0)
    fall_last = at(v127, 0) * (at(right, 0) - at(right, 1))
    fall_first = at(v0, 0) * (at(left, 0) - at(left, 1))
    right_ref[...] = right
    stack[...] = jnp.zeros_like(stack)
    for column, value in (
        (COLUMN_KV, row_sum(right)),
        (COLUMN_K2V, row_sum(right_sq)),
        (COLUMN_VL, at(v0, end)),
        (COLUMN_VR, at(v127, end)),
        (COLUMN_HT, at(right, 0)),
        (COLUMN_HB, at(right, end)),
        (COLUMN_DV, dv),
        (COLUMN_XBR, xbr),
        (COLUMN_XBL, xbl),
        (COLUMN_HELP, -along_last - fall_last),
        (COLUMN_HELP + 1, along_last),
        (COLUMN_HELP + 2, along_first + fall_first),
        (COLUMN_HELP + 3, -along_first),
    ):
        stack[column : column + 1, :] = value
    turned = jnp.transpose(stack[...])[0:tiles, :]
    upright = (lane <= COLUMN_XTL) | (lane >= COLUMN_HELP)
    out_ref[...] = jnp.where(upright, turned, table)
    for copy in own:
        copy.wait()


def match_kernel(
    fixed_ref, moving_ref, offsets_ref, table_ref, firsts_ref, right_ref, line_ref, above_ref, across_ref, beside_ref,
    out_ref, lines_ref, next_columns_ref, prev_columns_ref, scores_ref, shifts_ref,
):
    patches, _, flow = offsets_ref.shape[1:]
    corr = fixed_ref.shape[1]
    half = patches // 2
    rows = right_ref.shape[0]
    tiles = line_ref.shape[0]
    pair = 2 * flow
    lower = iota((flow, pair), 1) < flow

    def receive(near_ref, far_ref):
        for first in range(0, patches, 2):
            start = first % half * flow
            if first < half:
                fixed, moving = fixed_ref[start : start + pair, :], near_ref[start : start + pair, :]
            else:
                fixed, moving = far_ref[start : start + pair, :], moving_ref[start : start + pair, :]
            scores = lax.dot_general(moving, fixed, (((1,), (1,)), ((), ())), preferred_element_type=F32)
            scores_ref[:, first * flow : (first + 2) * flow] = jnp.where(
                lower, scores[0:flow, :], scores[flow:pair, :]
            )
        next_line, next_columns, _ = unpack(near_ref[half * flow :, :], tiles)
        prev_line, prev_columns, shifts = unpack(far_ref[half * flow :, :], tiles)
        lines_ref[0:tiles, :] = next_line
        lines_ref[tiles:, :] = prev_line
        next_columns_ref[...] = next_columns
        prev_columns_ref[...] = prev_columns
        shifts_ref[...] = shifts

    first_core = lax.axis_index("core") == 0

    @pl.when(first_core)
    def _():
        receive(beside_ref, across_ref)

    @pl.when(jnp.logical_not(first_core))
    def _():
        receive(across_ref, beside_ref)

    next_line, next_columns, shifts = lines_ref[0:tiles, :], next_columns_ref[...], shifts_ref[...]
    scores = scores_ref[...]
    top = jnp.max(scores, axis=0, keepdims=True)
    likely = jnp.exp((scores - top) * (1.0 / math.sqrt(corr)))
    offsets = []
    for k in range(2):
        offsets.append(offsets_ref[0, 0:half, k, :].astype(F32))
        offsets.append(shifts[:, k * flow : (k + 1) * flow])
    shifted = jnp.concatenate(offsets, 0).astype(jnp.bfloat16)
    parts = [part.astype(jnp.bfloat16) for part in three_parts(likely)]
    sums = lax.dot_general(
        jnp.concatenate([shifted] * 3, 1),
        jnp.concatenate(parts, 0),
        (((1,), (0,)), ((), ())),
        preferred_element_type=F32,
    )
    weight = row_sum(likely) * flow
    mine = lax.rem(iota(sums.shape, 0), patches) == lax.div(iota(sums.shape, 1), flow)
    ratio = lane_sum(jnp.where(mine, sums, 0.0) / weight)

    table = table_ref[...]
    lane = iota(table.shape, 1)

    def helper(n):
        return table[:, COLUMN_HELP + n : COLUMN_HELP + n + 1]

    line, above = line_ref[...], above_ref[...]
    step = above - pltpu.roll(above, TILE_W - 1, 1)
    top_energy = firsts_ref[0:tiles, :] * above * above + jnp.where(
        lane < TILE_W - 1, firsts_ref[tiles:, :] * step * step, 0.0
    )
    diagonal = iota(table.shape, 0) == lane
    across = row_sum(right_ref[...] * next_columns)
    columns = [
        (COLUMN_XTR, above[:, TILE_W - 1 :] * helper(0) + above[:, TILE_W - 2 : TILE_W - 1] * helper(1)),
        (COLUMN_XTL, above[:, 0:1] * helper(2) + above[:, 1:2] * helper(3)),
        (COLUMN_DT, lane_sum(top_energy)),
        (COLUMN_KXH, lane_sum(line * next_line)),
        (COLUMN_KXV, lane_sum(jnp.where(diagonal, across, 0.0))),
    ]
    for k in range(2):
        columns.append((COLUMN_NEAR + k, ratio[2 * k * half : (2 * k + 1) * half]))
        columns.append((COLUMN_FAR + k, ratio[(2 * k + 1) * half : (2 * k + 2) * half]))
    for column, value in columns:
        table = jnp.where(lane == column, value, table)

    table = jnp.where(lane < COLUMN_HELP, table, 0.0)
    pieces = [jnp.zeros((1, TILE_W), F32) for _ in range(out_ref.shape[1])]
    place = iota((1, TILE_W), 1)
    for j in range(tiles):
        part, start = divmod(j * GROUP_LANES, TILE_W)
        source = table[j : j + 1, :]
        source = pltpu.roll(source, start, 1) if start else source
        if start + GROUP_LANES > TILE_W:
            pieces[part] = pieces[part] + jnp.where(place >= start, source, 0.0)
            pieces[part + 1] = pieces[part + 1] + jnp.where(place < start, source, 0.0)
        else:
            pieces[part] = pieces[part] + source
    for part, piece in enumerate(pieces):
        for n in range(out_ref.shape[0]):
            out_ref[n, part : part + 1, :] = piece


def copies_kernel(seen_ref, out_ref, block):
    chips = seen_ref.shape[0] // 2
    shared = chips // 2
    lead = chips - FIRST_Z
    block[0:FIRST_Z, :] = seen_ref[pl.ds(2 * lead, FIRST_Z, stride=2), :]
    block[FIRST_Z:chips, :] = seen_ref[pl.ds(0, lead, stride=2), :]
    block[chips : chips + FIRST_Z, :] = seen_ref[pl.ds(2 * lead + 1, FIRST_Z, stride=2), :]
    block[chips + FIRST_Z :, :] = seen_ref[pl.ds(1, lead, stride=2), :]
    first = block[0:chips, :]
    second = block[chips : chips + shared, :] + pltpu.roll(block[chips + shared :, :], TILE_W // 2, 1)
    for n in range(out_ref.shape[0]):
        out_ref[n, 0:chips, :] = first
        out_ref[n, chips:, :] = second


def stack_kernel(
    dims, seen_ref, vert_ref, hori_ref, own_line_ref, own_above_ref,
    lines_ref, aboves_ref, next_columns_ref, prev_columns_ref,
    disp_ref, res_ref, rows_ref, turn_ref, sums_ref, out_ref, field_ref,
):
    groups, sections, rows, tiles, chips_z = dims
    per_chip = sections // chips_z
    count = groups * tiles
    nodes = float(rows * TILE_W)
    me, group = lax.axis_index(SEC), lax.axis_index("group")

    shared = chips_z // 2
    half_lanes = TILE_W // 2
    for core in range(CORES):
        for g in range(groups):
            for y in range(per_chip // CORES):
                place = (CORES - 1 - core) * groups * CHIPS_Y + plane_order(groups, core).index((g, y))
                base = place * (chips_z + shared)
                chip = y * CORES + core
                rows_ref[g, pl.ds(chip, chips_z, stride=per_chip), :] = seen_ref[base : base + chips_z, :]
                rows_ref[
                    groups + g // 2, pl.ds((g % 2) * (sections // 2) + chip, shared, stride=per_chip), :
                ] = seen_ref[base + chips_z : base + chips_z + shared, :]
    left_half = iota((half_lanes, sections), 1) < sections // 2
    for g in range(groups):
        turn_ref[g, 0:TILE_W, :] = jnp.transpose(rows_ref[g])
    for pair in range(groups // 2):
        turned = jnp.transpose(rows_ref[groups + pair])
        low_half, high_half = turned[0:half_lanes, :], turned[half_lanes:, :]
        turn_ref[2 * pair, TILE_W:, :] = jnp.where(
            left_half, low_half, pltpu.roll(high_half, sections // 2, 1)
        )
        turn_ref[2 * pair + 1, TILE_W:, :] = jnp.where(
            left_half, pltpu.roll(low_half, sections // 2, 1), high_half
        )

    def block(g, column):
        return turn_ref[g, pl.ds(column, tiles, stride=GROUP_LANES), :]

    def figure(column):
        return jnp.concatenate([block(g, column) for g in range(groups)], 0)

    def slots(near, far, turn):
        parts = []
        for g in range(groups):
            parts.append(block(g, near))
            other = block(g, far)
            parts.append(pltpu.roll(other, sections - 1, 1) if turn else other)
        return jnp.concatenate(parts, 0)

    lane = iota((count, sections), 1)
    tile_row = iota((count, sections), 0)
    along = lax.rem(tile_row, tiles)
    not_last = lane < sections - 1

    def up(x):
        return jnp.where(not_last, pltpu.roll(x, sections - 1, 1), 0.0)

    def low(x):
        return jnp.where(lane > 0, pltpu.roll(x, 1, 1), 0.0)

    zero_tiles = jnp.zeros((tiles, sections), F32)

    def from_above(x):
        return jnp.concatenate([zero_tiles, x[: count - tiles]], 0)

    def from_below(x):
        return jnp.concatenate([x[tiles:], zero_tiles], 0)

    def from_left(x):
        return jnp.where(along > 0, pltpu.roll(x, 1, 0), 0.0)

    def from_right(x):
        return jnp.where(along < tiles - 1, pltpu.roll(x, count - 1, 0), 0.0)

    owner = slots(COLUMN_OWNER, COLUMN_OWNER + 1, False)
    targets = [slots(COLUMN_NEAR + k, COLUMN_FAR + k, True) for k in range(2)]
    valid = jnp.where(owner >= 0.0, 1.0, 0.0)

    def tile_sums(miss):
        weight = valid / (1.0 + (miss[0] * miss[0] + miss[1] * miss[1]) / SPREAD_SQ)
        terms = (weight, weight * targets[0], weight * targets[1])
        for t in range(count):
            mine = owner == float(t)
            for n, term in enumerate(terms):
                sums_ref[n, t : t + 1, :] = row_sum(jnp.where(mine, term, 0.0))
        return [jnp.where(not_last, sums_ref[n], 0.0) for n in range(3)]

    kh, kv = figure(COLUMN_KH), figure(COLUMN_KV)
    k2h, k2v = figure(COLUMN_K2H), figure(COLUMN_K2V)
    kxh, kxv = figure(COLUMN_KXH), figure(COLUMN_KXV)
    vl, vr = figure(COLUMN_VL), figure(COLUMN_VR)
    ht, hb = figure(COLUMN_HT), figure(COLUMN_HB)
    dh, dt, dv = figure(COLUMN_DH), figure(COLUMN_DT), figure(COLUMN_DV)
    xbr, xbl, xtr, xtl = (figure(c) for c in (COLUMN_XBR, COLUMN_XBL, COLUMN_XTR, COLUMN_XTL))
    fold_h = jnp.where(tile_row < count - tiles, 2.0, 1.0)
    fold_v = jnp.where(along < tiles - 1, 2.0, 1.0)

    def differences(x):
        return x - from_below(x), x - from_right(x)

    def corners(diff_h, diff_v):
        return (
            (vr * diff_h, hb * diff_v),
            (vl * diff_h, -from_left(hb * diff_v)),
            (-from_above(vr * diff_h), ht * diff_v),
            (-from_above(vl * diff_h), -from_left(ht * diff_v)),
        )

    def tile_product(along_h, along_v, first, second):
        value = along_h + from_above(along_h) + along_v + from_left(along_v)
        for (ah, av), (bh, bv) in zip(first, second):
            value = value + ah * bv + av * bh
        return value

    weight, *pull = tile_sums(targets)
    flat = [e - low(e) for e in pull]
    step = [differences(d) for d in flat]
    gap = [d - up(d) for d in flat]
    norm = total(flat[0] * flat[0] + flat[1] * flat[1]) * nodes
    energy = sum(kh * h * h + kv * v * v for h, v in step)
    energy = energy + nodes * weight * (gap[0] * gap[0] + gap[1] * gap[1])
    alpha = norm / total(energy)

    index = jnp.maximum(owner, 0.0).astype(jnp.int32)
    inside_index = lax.rem(index, tiles)
    row_index = lax.div(index, tiles)
    look = []
    for k in range(2):
        shift = alpha * gap[k]
        rows_of = []
        for p in range(0, owner.shape[0], tiles):
            value = jnp.zeros((tiles, sections), F32)
            for g in range(groups):
                picked = jnp.take_along_axis(
                    shift[g * tiles : (g + 1) * tiles], inside_index[p : p + tiles], axis=0
                )
                value = jnp.where(row_index[p : p + tiles] == g, picked, value)
            rows_of.append(value)
        look.append(jnp.concatenate(rows_of, 0))
    weight, *pull = tile_sums([look[k] - targets[k] for k in range(2)])
    weight_low = low(weight)
    const = [
        pull[k] - low(pull[k]) - alpha * (weight * gap[k] - weight_low * low(gap[k]))
        for k in range(2)
    ]
    plain = jnp.zeros_like(kh)
    mixed = jnp.zeros_like(kh)
    quad = jnp.zeros_like(kh)
    p_energy = jnp.zeros_like(kh)
    m_energy = jnp.zeros_like(kh)
    q_energy = jnp.zeros_like(kh)
    for k in range(2):
        c = const[k]
        ch, cv = differences(c)
        h, v = step[k]
        ends = corners(h, v)
        c_ends = corners(ch, cv)
        square = tile_product(k2h * h * h, k2v * v * v, ends, ends)
        across = tile_product(
            kxh * h * up(h), kxv * v * up(v), ends, [(up(a), up(b)) for a, b in ends]
        )
        gap_square = square + up(square) - 2.0 * across
        flux_h, flux_v = kh * h, kv * v
        inner = flux_h - from_above(flux_h) + flux_v - from_left(flux_v)
        gap_c = c - up(c)
        gap_q = inner - up(inner)
        plain = plain + c * c
        mixed = mixed + c * inner
        quad = quad + square
        p_energy = p_energy + kh * ch * ch + kv * cv * cv + nodes * weight * gap_c * gap_c
        m_energy = (
            m_energy
            + tile_product(k2h * ch * h, k2v * cv * v, c_ends, ends)
            + weight * gap_c * gap_q
        )
        above_h, left_v = from_above(h), from_left(v)
        value = dh * h * h + dt * above_h * above_h + dv * v * v
        value = value + 2.0 * (
            xbr * h * v + xbl * h * left_v + xtr * above_h * v + xtl * above_h * left_v
        )
        (br_h, br_v), (bl_h, bl_v), (tr_h, tr_v), (tl_h, tl_v) = ends
        for stiff, part, extra, fold in (
            (vr, br_h, br_v - from_below(tr_v), fold_h),
            (vl, bl_h, bl_v - from_below(tl_v), fold_h),
            (hb, br_v, br_h - from_right(bl_h), fold_v),
            (ht, tr_v, tr_h - from_right(tl_h), fold_v),
        ):
            value = value + stiff * extra * (2.0 * fold * part + extra)
        q_energy = q_energy + value + weight * gap_square
    norm = nodes * total(plain) - 2.0 * alpha * total(mixed) + alpha * alpha * total(quad)
    energy = total(p_energy) - 2.0 * alpha * total(m_energy) + alpha * alpha * total(q_energy)
    beta = norm / energy

    own_figures = (*flat, *const, step[0][0], step[1][0], step[0][1], step[1][1], ht, hb, weight, weight_low)
    beside = (*const, step[0][0], step[1][0], step[0][1], step[1][1])
    wanted = [(x, me) for x in own_figures] + [(x, me + 1) for x in beside] + [(x, me - 1) for x in beside]
    for n, (x, section) in enumerate(wanted):
        out_ref[n, 0:tiles, :] = zero_tiles
        out_ref[n, tiles + count : 2 * tiles + count, :] = zero_tiles
        picked = lane_sum(jnp.where(lane == section, x, 0.0))
        out_ref[n, tiles : tiles + count, :] = jnp.broadcast_to(picked, (count, sections))

    def spread(n, shift):
        start = pl.multiple_of((group + 1 + shift) * tiles, tiles)
        return out_ref[n, pl.ds(start, tiles), :]

    wide_lane = iota((rows, TILE_W), 1)
    wide_row = iota((rows, TILE_W), 0)
    first_lane, last_lane = wide_lane == 0, wide_lane == TILE_W - 1
    first_row, last_row = wide_row == 0, wide_row == rows - 1
    line_first, line_last = first_lane[0:1], last_lane[0:1]
    inside = jnp.where(group < groups - 1, 1.0, 0.0).astype(F32)

    def image(edges, offset, k, j):
        last_line, above_line, columns = edges
        def line(n, shift=0, at=j):
            return spread(offset + n + k, shift)[at : at + 1, :]

        value = jnp.where(last_row, last_line[j : j + 1, :] * line(0), 0.0)
        value = value - jnp.where(first_row, above_line[j : j + 1, :] * line(0, -1), 0.0)
        value = value + jnp.where(last_lane, columns(j) * line(2), 0.0)
        if j:
            value = value - jnp.where(first_lane, columns(j - 1) * line(2, 0, j - 1), 0.0)
        return value

    own_line, own_above = own_line_ref[...], own_above_ref[...]
    next_columns, prev_columns = next_columns_ref[...], prev_columns_ref[...]
    own_edges = (own_line, own_above, lambda j: hori_ref[:, (j + 1) * TILE_W - 1 : (j + 1) * TILE_W])
    next_edges = (lines_ref[0:tiles, :], aboves_ref[0:tiles, :], lambda j: next_columns[:, j : j + 1])
    prev_edges = (lines_ref[tiles:, :], aboves_ref[tiles:, :], lambda j: prev_columns[:, j : j + 1])
    for k in range(2):
        for j in range(tiles):
            span = slice(j * TILE_W, (j + 1) * TILE_W)

            def line(n, shift, at=j):
                return spread(n + k, shift)[at : at + 1, :]

            field_ref[k, tiles : tiles + rows, span] = line(2, 0) - alpha * image(own_edges, 4, k, j)
            near = -inside * own_line[j : j + 1, :] * line(4, 0)
            near = near + jnp.where(line_last, spread(8, 1)[j : j + 1, :] * line(6, 1), 0.0)
            far = own_above[j : j + 1, :] * line(4, -1)
            far = far + jnp.where(line_last, spread(9, -1)[j : j + 1, :] * line(6, -1), 0.0)
            if j:
                near = near - jnp.where(line_first, spread(8, 1)[j - 1 : j, :] * line(6, 1, j - 1), 0.0)
                far = far - jnp.where(line_first, spread(9, -1)[j - 1 : j, :] * line(6, -1, j - 1), 0.0)
            field_ref[k, tiles + rows : tiles + rows + 1, span] = line(2, 1) - alpha * near
            field_ref[k, tiles - 1 : tiles, span] = line(2, -1) - alpha * far
    weight_rows, weight_low_rows = spread(10, 0), spread(11, 0)
    for k in range(2):
        flux_left = None
        for j in range(tiles):
            span = slice(j * TILE_W, (j + 1) * TILE_W)
            r = field_ref[k, tiles : tiles + rows, span]
            right = pltpu.roll(r, TILE_W - 1, 1)
            if j < tiles - 1:
                beyond = field_ref[k, tiles : tiles + rows, (j + 1) * TILE_W : (j + 2) * TILE_W]
                right = jnp.where(last_lane, pltpu.roll(beyond, TILE_W - 1, 1), right)
            else:
                right = jnp.where(last_lane, 0.0, right)
            flux = hori_ref[:, span] * (r - right)
            turned = pltpu.roll(flux, 1, 1)
            before = jnp.where(first_lane, 0.0 if flux_left is None else flux_left, turned)
            flux_left = turned
            below = field_ref[k, tiles + 1 : tiles + rows + 1, span]
            fall = vert_ref[:, span] * (r - below)
            edge = own_above[j : j + 1, :] * (field_ref[k, tiles - 1 : tiles, span] - r[0:1, :])
            fall_above = jnp.where(first_row, edge, pltpu.roll(fall, 1, 0))
            applied = flux - before + fall - fall_above
            r_next = spread(12 + k, 0)[j : j + 1, :] - alpha * image(next_edges, 14, k, j)
            r_prev = spread(18 + k, 0)[j : j + 1, :] - alpha * image(prev_edges, 20, k, j)
            applied = applied + weight_rows[j : j + 1, :] * (r - r_next) + weight_low_rows[j : j + 1, :] * (r - r_prev)
            disp_ref[k, :, span] = alpha * spread(k, 0)[j : j + 1, :] + beta * r
            res_ref[k, :, span] = r - beta * applied


def in_vmem(x):
    return pltpu.VMEM(x.shape, x.dtype)


def from_behind(block, axis, distance):
    devices = range(lax.axis_size(axis))
    route = [(i - distance, i) for i in devices if i - distance in devices]
    return lax.ppermute(block, axis, route)


def plane_order(groups, core):
    order = [
        ((FIRST_GROUP + g) % groups, (FIRST_CHIP[core] + y) % CHIPS_Y)
        for g in range(groups)
        for y in range(CHIPS_Y)
    ]
    order.remove(ORIGIN)
    order.insert(ORIGIN_PLACE, ORIGIN)
    return order


def planes(groups, chips_z):
    return [
        [((g * chips_z + z) * CHIPS_Y + y) * CORES + core for g, y in plane_order(groups, core)]
        for z in range(chips_z)
        for core in range(CORES)
    ]


def swap(block, first):
    route = []
    for s in range(first, lax.axis_size(SEC) - 1, 2):
        route += [(s, s + 1), (s + 1, s)]
    return lax.ppermute(block, SEC, route)


def body(fixed_desc, moving_desc, offsets, owner, counts, vert, hori):
    groups = lax.axis_size("group")
    sections = lax.axis_size(SEC)
    chips_z = lax.axis_size("z")
    patches, flow, corr = fixed_desc.shape[1:]
    rows, cols = vert.shape[1:]
    tiles = cols // TILE_W
    length = patches * flow
    halves = -(-tiles * GROUP_LANES // TILE_W)

    hbm = pl.BlockSpec(memory_space=pltpu.HBM)
    local = pl.BlockSpec(memory_space=pltpu.VMEM)
    scalars = pl.BlockSpec(memory_space=pltpu.SMEM)
    modest = pltpu.CompilerParams(vmem_limit_bytes=16 << 20)
    border = jax.ShapeDtypeStruct((tiles, TILE_W), F32)
    upright = jax.ShapeDtypeStruct((rows, TILE_W), F32)
    lines_shape = jax.ShapeDtypeStruct((2 * tiles, TILE_W), F32)
    packed = pltpu.VMEM((length // 2 + rows, corr), fixed_desc.dtype)
    across, beside, line = pl.pallas_call(
        pack_kernel,
        out_shape=(packed, packed, in_vmem(border)),
        in_specs=[hbm] * 5,
        out_specs=(local,) * 3,
        scratch_shapes=[
            pltpu.VMEM((rows, cols), F32),
            pltpu.VMEM((rows, cols), F32),
            pltpu.VMEM(offsets.shape[1:], jnp.int32),
            pltpu.SemaphoreType.DMA((2 * PARTS + 3,)),
        ],
        compiler_params=modest,
        name="pack",
    )(
        *(
            pltpu.with_memory_space_constraint(x, pltpu.HBM)
            for x in (moving_desc.reshape(length, corr), fixed_desc.reshape(length, corr), vert, hori, offsets)
        )
    )
    across = swap(across, 1)
    beside = swap(beside, 0)
    above = from_behind(line, "group", 1)

    vert, hori = vert[0], hori[0]

    def borders(*refs):
        border_kernel(groups, *refs)

    half_features = pltpu.VMEM((length // 2, corr), fixed_desc.dtype)
    table, firsts, right, own_fixed, own_moving = pl.pallas_call(
        borders,
        out_shape=(in_vmem(border), in_vmem(lines_shape), in_vmem(upright), half_features, half_features),
        in_specs=[scalars] * 2 + [local] * 3 + [hbm] * 2,
        out_specs=(local,) * 5,
        scratch_shapes=[pltpu.VMEM((TILE_W, TILE_W), F32), pltpu.SemaphoreType.DMA((2 * OWN_PARTS,))],
        compiler_params=modest,
        name="borders",
    )(
        owner, counts, vert, hori, line,
        *(pltpu.with_memory_space_constraint(x.reshape(length, corr), pltpu.HBM) for x in (fixed_desc, moving_desc)),
    )
    mine, lines, next_columns, prev_columns = pl.pallas_call(
        match_kernel,
        out_shape=(
            pltpu.VMEM((chips_z, halves, TILE_W), F32),
            in_vmem(lines_shape), in_vmem(upright), in_vmem(upright),
        ),
        in_specs=[local] * 10,
        out_specs=(local,) * 4,
        scratch_shapes=[pltpu.VMEM((flow, length), F32), pltpu.VMEM((tiles, TILE_W), F32)],
        compiler_params=modest,
        name="match",
    )(own_fixed, own_moving, offsets, table, firsts, right, line, above, across, beside)

    turned = [(z + FIRST_Z) % chips_z for z in range(chips_z)]
    seen = lax.all_to_all(mine, "z", 0, 0, tiled=True, axis_index_groups=[turned]).reshape(-1, TILE_W)
    lines, seen = lax.optimization_barrier((lines, seen))
    aboves = from_behind(lines, "group", 1)
    peers = groups * lax.axis_size("y")
    block_rows = chips_z + chips_z // 2
    copies = pl.pallas_call(
        copies_kernel,
        out_shape=jax.ShapeDtypeStruct((peers, block_rows, TILE_W), F32),
        in_specs=[local],
        out_specs=local,
        scratch_shapes=[pltpu.VMEM((2 * chips_z, TILE_W), F32)],
        compiler_params=modest,
        name="copies",
    )(seen)
    seen = lax.all_to_all(
        copies, ("group",) + SEC, 0, 0, tiled=True, axis_index_groups=planes(groups, chips_z)
    ).reshape(-1, TILE_W)
    cores = list(reversed(range(CORES)))
    seen = lax.all_gather(seen, "core", axis=0, tiled=True, axis_index_groups=[cores])

    dims = (groups, sections, rows, tiles, chips_z)
    count = groups * tiles

    def both_iterations(*refs):
        stack_kernel(dims, *refs)

    field = jax.ShapeDtypeStruct((2, rows, cols), F32)
    displacement, residual = pl.pallas_call(
        both_iterations,
        out_shape=(field, field),
        in_specs=[local] * 9,
        scratch_shapes=[
            pltpu.VMEM((groups + groups // 2, sections, TILE_W), F32),
            pltpu.VMEM((groups, tiles * GROUP_LANES, sections), F32),
            pltpu.VMEM((3, count, sections), F32),
            pltpu.VMEM((24, count + 2 * tiles, sections), F32),
            pltpu.VMEM((2, rows + 2 * tiles, cols), F32),
        ],
        compiler_params=modest,
        name="stack",
    )(seen, vert, hori, line, above, lines, aboves, next_columns, prev_columns)
    return (displacement[None], residual[None])


def solution(mesh):
    groups, sections = mesh.devices.shape
    devices = mesh.devices.reshape(groups, sections // (CHIPS_Y * CORES), CHIPS_Y, CORES)
    fine = Mesh(devices, ("group",) + SEC)
    in_specs = (
        P(SEC, "group", None, None),
        P(SEC, "group", None, None),
        P(SEC, "group", None, None),
        P(SEC, "group"),
        P(SEC, "group"),
        P(SEC, "group", None),
        P(SEC, "group", None),
    )
    out_specs = (P(SEC, None, "group", None), P(SEC, None, "group", None))
    return jax.shard_map(body, mesh=fine, in_specs=in_specs, out_specs=out_specs, check_vma=False)
```

```python
import math

import jax
import jax.numpy as jnp
from jax import lax
from jax.experimental import pallas as pl
from jax.experimental.pallas import tpu as pltpu
from jax.sharding import Mesh, PartitionSpec as P

TILE_W = 128
SPREAD_SQ = 4.0
CHIPS_Y = 4
CORES = 2
SEC = ("z", "y", "core")
F32 = jnp.float32

COLUMN_KV, COLUMN_K2V, COLUMN_KXV, COLUMN_VL, COLUMN_VR, COLUMN_HT, COLUMN_HB = range(7)
COLUMN_DV, COLUMN_XBR, COLUMN_XBL, COLUMN_XTR, COLUMN_XTL = range(7, 12)
COLUMN_KH, COLUMN_K2H, COLUMN_KXH, COLUMN_DH, COLUMN_DT = range(12, 17)
COLUMN_OWNER = 17
COLUMN_NEAR = 19
COLUMN_FAR = 21
COLUMN_HELP = 23
GROUP_LANES = 24
FIRST_Z = 9
FIRST_GROUP = 2
FIRST_CHIP = (2, 2)
ORIGIN = (0, 0)
ORIGIN_PLACE = 15
PARTS = 2


def iota(shape, axis):
    return lax.broadcasted_iota(jnp.int32, shape, axis)


def lane_sum(x):
    return jnp.sum(x, axis=1, keepdims=True)


def row_sum(x):
    return jnp.sum(x, axis=0, keepdims=True)


def total(x):
    return lane_sum(row_sum(x))


def three_parts(x):
    high = x.astype(jnp.bfloat16).astype(F32)
    middle = (x - high).astype(jnp.bfloat16).astype(F32)
    return high, middle, x - high - middle


def pack_kernel(
    moving_ref, fixed_ref, vert_ref, hori_ref, offsets_ref, across_ref, beside_ref, line_ref,
    vert, hori, offsets, sems,
):
    rows, cols = hori.shape
    tiles = cols // TILE_W
    length = moving_ref.shape[0] // 2
    part = length // PARTS
    loads = [
        pltpu.make_async_copy(vert_ref.at[0], vert, sems.at[0]),
        pltpu.make_async_copy(hori_ref.at[0], hori, sems.at[1]),
        pltpu.make_async_copy(offsets_ref.at[0], offsets, sems.at[2]),
    ]
    for copy in loads:
        copy.start()

    def features(back, ahead):
        copies = []
        for n in range(PARTS):
            at, behind = pl.ds(n * part, part), pl.ds(length + n * part, part)
            copies.append(pltpu.make_async_copy(moving_ref.at[at], back.at[at], sems.at[3 + 2 * n]))
            copies.append(pltpu.make_async_copy(fixed_ref.at[behind], ahead.at[at], sems.at[4 + 2 * n]))
        return copies

    first = lax.axis_index("core") == 0

    @pl.when(first)
    def _():
        for copy in features(across_ref, beside_ref):
            copy.start()

    @pl.when(jnp.logical_not(first))
    def _():
        for copy in features(beside_ref, across_ref):
            copy.start()

    for copy in loads:
        copy.wait()
    lane = iota((rows, TILE_W), 1)
    column = jnp.zeros((rows, TILE_W), F32)
    for j in range(tiles):
        span = slice(j * TILE_W, (j + 1) * TILE_W)
        line_ref[j : j + 1, :] = vert[rows - 1 : rows, span]
        end = (j + 1) * TILE_W - 1
        column = jnp.where(lane == j, hori[:, end : end + 1], column)
    high, middle, small = three_parts(column)
    columns = high + pltpu.roll(middle, tiles, 1) + pltpu.roll(small, 2 * tiles, 1)
    half = offsets.shape[0] // 2
    shifts = jnp.concatenate([offsets[half:, 0, :], offsets[half:, 1, :]], 1).astype(F32)
    blank = jnp.zeros((tiles, TILE_W), F32)
    for ref in (across_ref, beside_ref):
        for n, value in enumerate(three_parts(line_ref[...])):
            block = jnp.concatenate([value, blank if n else shifts], 0)
            ref[length:, n * TILE_W : (n + 1) * TILE_W] = block.astype(jnp.bfloat16)
        ref[length:, 3 * TILE_W :] = columns.astype(jnp.bfloat16)
    for copy in features(across_ref, beside_ref):
        copy.wait()


def unpack(extra, tiles):
    parts = [extra[:, n * TILE_W : (n + 1) * TILE_W].astype(F32) for n in range(4)]
    line = parts[0][:tiles] + (parts[1][:tiles] + parts[2][:tiles])
    columns = parts[3]
    back = TILE_W - tiles
    columns = columns + (pltpu.roll(columns, back, 1) + pltpu.roll(columns, back - tiles, 1))
    return line, columns, parts[0][tiles:]


def border_kernel(groups, owner_ref, counts_ref, vert_ref, hori_ref, line_ref, out_ref, firsts_ref, right_ref, stack):
    rows, cols = hori_ref.shape
    tiles = cols // TILE_W
    last_group = lax.axis_index("group") == groups - 1
    bottom = jnp.where(last_group, 1.0, 4.0).astype(F32)

    v_last = line_ref[...]
    for j in range(tiles):
        span = slice(j * TILE_W, (j + 1) * TILE_W)
        stack[j : j + 1, :] = vert_ref[rows - 2 : rows - 1, span]
        stack[tiles + j : tiles + j + 1, :] = hori_ref[rows - 1 : rows, span]
        firsts_ref[j : j + 1, :] = vert_ref[0:1, span]
        firsts_ref[tiles + j : tiles + j + 1, :] = hori_ref[0:1, span]
    v_second, h_last = stack[0:tiles, :], stack[tiles : 2 * tiles, :]
    lane = iota((tiles, TILE_W), 1)
    inside = lane < TILE_W - 1
    square = v_last * v_last
    step_last = v_last - pltpu.roll(v_last, TILE_W - 1, 1)
    dh = lane_sum(
        bottom * square * v_last
        + v_second * square
        + jnp.where(inside, h_last * step_last * step_last, 0.0)
    )
    sub = iota((tiles, TILE_W), 0)
    table = jnp.zeros((tiles, TILE_W), F32)
    for p in range(owner_ref.shape[1]):
        live = jnp.where(p < counts_ref[0, 0], owner_ref[0, p], -1).astype(F32)
        spot = (sub == p % tiles) & (lane == COLUMN_OWNER + p // tiles)
        table = jnp.where(spot, live, table)
    for column, value in (
        (COLUMN_KH, lane_sum(v_last)),
        (COLUMN_K2H, lane_sum(square)),
        (COLUMN_DH, dh),
    ):
        table = jnp.where(lane == column, value, table)

    tall = iota((rows, TILE_W), 1)
    zero = jnp.zeros((rows, TILE_W), F32)
    picked = {}
    for name, ref, column in (
        ("h127", hori_ref, TILE_W - 1),
        ("h0", hori_ref, 0),
        ("h126", hori_ref, TILE_W - 2),
        ("v0", vert_ref, 0),
        ("v1", vert_ref, 1),
        ("v126", vert_ref, TILE_W - 2),
        ("v127", vert_ref, TILE_W - 1),
    ):
        value = zero
        for j in range(tiles):
            at = j * TILE_W + column
            value = jnp.where(tall == j, ref[:, at : at + 1], value)
        picked[name] = value
    right = picked["h127"]
    left = pltpu.roll(right, 1, 1)
    row = iota((rows, TILE_W), 0)
    within = row < rows - 1
    inner_tile = iota((1, TILE_W), 1) < tiles - 1
    step_right = right - pltpu.roll(right, rows - 1, 0)
    step_left = left - pltpu.roll(left, rows - 1, 0)
    right_sq, left_sq = right * right, left * left
    side_right = row_sum(
        picked["h126"] * right_sq + jnp.where(within, picked["v127"] * step_right * step_right, 0.0)
    )
    side_left = row_sum(
        picked["h0"] * left_sq + jnp.where(within, picked["v0"] * step_left * step_left, 0.0)
    )
    cube = row_sum(right_sq * right)
    dv = side_right + jnp.where(
        inner_tile, pltpu.roll(side_left, TILE_W - 1, 1) + 4.0 * cube, cube
    )
    end, pre = rows - 1, rows - 2
    v0, v1, v126, v127 = (picked[n] for n in ("v0", "v1", "v126", "v127"))
    h0, h126 = picked["h0"], picked["h126"]

    def at(x, r):
        return x[r : r + 1, :]

    xbr = at(h126, end) * (at(v127, end) - at(v126, end)) * at(right, end) + at(v127, pre) * at(
        v127, end
    ) * (at(right, end) - at(right, pre))
    xbl = -(
        at(h0, end) * (at(v0, end) - at(v1, end)) * at(left, end)
        + at(v0, pre) * at(v0, end) * (at(left, end) - at(left, pre))
    )
    along_last, along_first = at(h126, 0) * at(right, 0), at(h0, 0) * at(left, 0)
    fall_last = at(v127, 0) * (at(right, 0) - at(right, 1))
    fall_first = at(v0, 0) * (at(left, 0) - at(left, 1))
    right_ref[...] = right
    stack[...] = jnp.zeros_like(stack)
    for column, value in (
        (COLUMN_KV, row_sum(right)),
        (COLUMN_K2V, row_sum(right_sq)),
        (COLUMN_VL, at(v0, end)),
        (COLUMN_VR, at(v127, end)),
        (COLUMN_HT, at(right, 0)),
        (COLUMN_HB, at(right, end)),
        (COLUMN_DV, dv),
        (COLUMN_XBR, xbr),
        (COLUMN_XBL, xbl),
        (COLUMN_HELP, -along_last - fall_last),
        (COLUMN_HELP + 1, along_last),
        (COLUMN_HELP + 2, along_first + fall_first),
        (COLUMN_HELP + 3, -along_first),
    ):
        stack[column : column + 1, :] = value
    turned = jnp.transpose(stack[...])[0:tiles, :]
    upright = (lane <= COLUMN_XTL) | (lane >= COLUMN_HELP)
    out_ref[...] = jnp.where(upright, turned, table)


def match_kernel(
    fixed_ref, moving_ref, offsets_ref, table_ref, firsts_ref, right_ref, line_ref, above_ref, across_ref, beside_ref,
    out_ref, lines_ref, next_columns_ref, prev_columns_ref, scores_ref, shifts_ref,
):
    patches, flow, corr = fixed_ref.shape[1:]
    half = patches // 2
    rows = right_ref.shape[0]
    tiles = line_ref.shape[0]
    pair = 2 * flow
    lower = iota((flow, pair), 1) < flow

    def receive(near_ref, far_ref):
        for first in range(0, patches, 2):
            own = slice(first, first + 2)
            if first < half:
                fixed = fixed_ref[0, own].reshape(pair, corr)
                moving = near_ref[first * flow : (first + 2) * flow, :]
            else:
                fixed = far_ref[(first - half) * flow : (first + 2 - half) * flow, :]
                moving = moving_ref[0, own].reshape(pair, corr)
            scores = lax.dot_general(moving, fixed, (((1,), (1,)), ((), ())), preferred_element_type=F32)
            scores_ref[:, first * flow : (first + 2) * flow] = jnp.where(
                lower, scores[0:flow, :], scores[flow:pair, :]
            )
        next_line, next_columns, _ = unpack(near_ref[half * flow :, :], tiles)
        prev_line, prev_columns, shifts = unpack(far_ref[half * flow :, :], tiles)
        lines_ref[0:tiles, :] = next_line
        lines_ref[tiles:, :] = prev_line
        next_columns_ref[...] = next_columns
        prev_columns_ref[...] = prev_columns
        shifts_ref[...] = shifts

    first_core = lax.axis_index("core") == 0

    @pl.when(first_core)
    def _():
        receive(beside_ref, across_ref)

    @pl.when(jnp.logical_not(first_core))
    def _():
        receive(across_ref, beside_ref)

    next_line, next_columns, shifts = lines_ref[0:tiles, :], next_columns_ref[...], shifts_ref[...]
    scores = scores_ref[...]
    top = jnp.max(scores, axis=0, keepdims=True)
    likely = jnp.exp((scores - top) * (1.0 / math.sqrt(corr)))
    offsets = []
    for k in range(2):
        offsets.append(offsets_ref[0, 0:half, k, :].astype(F32))
        offsets.append(shifts[:, k * flow : (k + 1) * flow])
    shifted = jnp.concatenate(offsets, 0).astype(jnp.bfloat16)
    parts = [part.astype(jnp.bfloat16) for part in three_parts(likely)]
    sums = lax.dot_general(
        jnp.concatenate([shifted] * 3, 1),
        jnp.concatenate(parts, 0),
        (((1,), (0,)), ((), ())),
        preferred_element_type=F32,
    )
    weight = row_sum(likely) * flow
    mine = lax.rem(iota(sums.shape, 0), patches) == lax.div(iota(sums.shape, 1), flow)
    ratio = lane_sum(jnp.where(mine, sums, 0.0) / weight)

    table = table_ref[...]
    lane = iota(table.shape, 1)

    def helper(n):
        return table[:, COLUMN_HELP + n : COLUMN_HELP + n + 1]

    line, above = line_ref[...], above_ref[...]
    step = above - pltpu.roll(above, TILE_W - 1, 1)
    top_energy = firsts_ref[0:tiles, :] * above * above + jnp.where(
        lane < TILE_W - 1, firsts_ref[tiles:, :] * step * step, 0.0
    )
    diagonal = iota(table.shape, 0) == lane
    across = row_sum(right_ref[...] * next_columns)
    columns = [
        (COLUMN_XTR, above[:, TILE_W - 1 :] * helper(0) + above[:, TILE_W - 2 : TILE_W - 1] * helper(1)),
        (COLUMN_XTL, above[:, 0:1] * helper(2) + above[:, 1:2] * helper(3)),
        (COLUMN_DT, lane_sum(top_energy)),
        (COLUMN_KXH, lane_sum(line * next_line)),
        (COLUMN_KXV, lane_sum(jnp.where(diagonal, across, 0.0))),
    ]
    for k in range(2):
        columns.append((COLUMN_NEAR + k, ratio[2 * k * half : (2 * k + 1) * half]))
        columns.append((COLUMN_FAR + k, ratio[(2 * k + 1) * half : (2 * k + 2) * half]))
    for column, value in columns:
        table = jnp.where(lane == column, value, table)

    table = jnp.where(lane < COLUMN_HELP, table, 0.0)
    pieces = [jnp.zeros((1, TILE_W), F32) for _ in range(out_ref.shape[1])]
    place = iota((1, TILE_W), 1)
    for j in range(tiles):
        part, start = divmod(j * GROUP_LANES, TILE_W)
        source = table[j : j + 1, :]
        source = pltpu.roll(source, start, 1) if start else source
        if start + GROUP_LANES > TILE_W:
            pieces[part] = pieces[part] + jnp.where(place >= start, source, 0.0)
            pieces[part + 1] = pieces[part + 1] + jnp.where(place < start, source, 0.0)
        else:
            pieces[part] = pieces[part] + source
    for part, piece in enumerate(pieces):
        for n in range(out_ref.shape[0]):
            out_ref[n, part : part + 1, :] = piece


def copies_kernel(seen_ref, out_ref, block):
    chips = seen_ref.shape[0] // 2
    shared = chips // 2
    lead = chips - FIRST_Z
    block[0:FIRST_Z, :] = seen_ref[pl.ds(2 * lead, FIRST_Z, stride=2), :]
    block[FIRST_Z:chips, :] = seen_ref[pl.ds(0, lead, stride=2), :]
    block[chips : chips + FIRST_Z, :] = seen_ref[pl.ds(2 * lead + 1, FIRST_Z, stride=2), :]
    block[chips + FIRST_Z :, :] = seen_ref[pl.ds(1, lead, stride=2), :]
    first = block[0:chips, :]
    second = block[chips : chips + shared, :] + pltpu.roll(block[chips + shared :, :], TILE_W // 2, 1)
    for n in range(out_ref.shape[0]):
        out_ref[n, 0:chips, :] = first
        out_ref[n, chips:, :] = second


def stack_kernel(
    dims, seen_ref, vert_ref, hori_ref, own_line_ref, own_above_ref,
    lines_ref, aboves_ref, next_columns_ref, prev_columns_ref,
    disp_ref, res_ref, rows_ref, turn_ref, sums_ref, out_ref, field_ref,
):
    groups, sections, rows, tiles, chips_z = dims
    per_chip = sections // chips_z
    count = groups * tiles
    nodes = float(rows * TILE_W)
    me, group = lax.axis_index(SEC), lax.axis_index("group")

    shared = chips_z // 2
    half_lanes = TILE_W // 2
    for core in range(CORES):
        for g in range(groups):
            for y in range(per_chip // CORES):
                place = (CORES - 1 - core) * groups * CHIPS_Y + plane_order(groups, core).index((g, y))
                base = place * (chips_z + shared)
                chip = y * CORES + core
                rows_ref[g, pl.ds(chip, chips_z, stride=per_chip), :] = seen_ref[base : base + chips_z, :]
                rows_ref[
                    groups + g // 2, pl.ds((g % 2) * (sections // 2) + chip, shared, stride=per_chip), :
                ] = seen_ref[base + chips_z : base + chips_z + shared, :]
    left_half = iota((half_lanes, sections), 1) < sections // 2
    for g in range(groups):
        turn_ref[g, 0:TILE_W, :] = jnp.transpose(rows_ref[g])
    for pair in range(groups // 2):
        turned = jnp.transpose(rows_ref[groups + pair])
        low_half, high_half = turned[0:half_lanes, :], turned[half_lanes:, :]
        turn_ref[2 * pair, TILE_W:, :] = jnp.where(
            left_half, low_half, pltpu.roll(high_half, sections // 2, 1)
        )
        turn_ref[2 * pair + 1, TILE_W:, :] = jnp.where(
            left_half, pltpu.roll(low_half, sections // 2, 1), high_half
        )

    def block(g, column):
        return turn_ref[g, pl.ds(column, tiles, stride=GROUP_LANES), :]

    def figure(column):
        return jnp.concatenate([block(g, column) for g in range(groups)], 0)

    def slots(near, far, turn):
        parts = []
        for g in range(groups):
            parts.append(block(g, near))
            other = block(g, far)
            parts.append(pltpu.roll(other, sections - 1, 1) if turn else other)
        return jnp.concatenate(parts, 0)

    lane = iota((count, sections), 1)
    tile_row = iota((count, sections), 0)
    along = lax.rem(tile_row, tiles)
    not_last = lane < sections - 1

    def up(x):
        return jnp.where(not_last, pltpu.roll(x, sections - 1, 1), 0.0)

    def low(x):
        return jnp.where(lane > 0, pltpu.roll(x, 1, 1), 0.0)

    zero_tiles = jnp.zeros((tiles, sections), F32)

    def from_above(x):
        return jnp.concatenate([zero_tiles, x[: count - tiles]], 0)

    def from_below(x):
        return jnp.concatenate([x[tiles:], zero_tiles], 0)

    def from_left(x):
        return jnp.where(along > 0, pltpu.roll(x, 1, 0), 0.0)

    def from_right(x):
        return jnp.where(along < tiles - 1, pltpu.roll(x, count - 1, 0), 0.0)

    owner = slots(COLUMN_OWNER, COLUMN_OWNER + 1, False)
    targets = [slots(COLUMN_NEAR + k, COLUMN_FAR + k, True) for k in range(2)]
    valid = jnp.where(owner >= 0.0, 1.0, 0.0)

    def tile_sums(miss):
        weight = valid / (1.0 + (miss[0] * miss[0] + miss[1] * miss[1]) / SPREAD_SQ)
        terms = (weight, weight * targets[0], weight * targets[1])
        for t in range(count):
            mine = owner == float(t)
            for n, term in enumerate(terms):
                sums_ref[n, t : t + 1, :] = row_sum(jnp.where(mine, term, 0.0))
        return [jnp.where(not_last, sums_ref[n], 0.0) for n in range(3)]

    kh, kv = figure(COLUMN_KH), figure(COLUMN_KV)
    k2h, k2v = figure(COLUMN_K2H), figure(COLUMN_K2V)
    kxh, kxv = figure(COLUMN_KXH), figure(COLUMN_KXV)
    vl, vr = figure(COLUMN_VL), figure(COLUMN_VR)
    ht, hb = figure(COLUMN_HT), figure(COLUMN_HB)
    dh, dt, dv = figure(COLUMN_DH), figure(COLUMN_DT), figure(COLUMN_DV)
    xbr, xbl, xtr, xtl = (figure(c) for c in (COLUMN_XBR, COLUMN_XBL, COLUMN_XTR, COLUMN_XTL))
    fold_h = jnp.where(tile_row < count - tiles, 2.0, 1.0)
    fold_v = jnp.where(along < tiles - 1, 2.0, 1.0)

    def differences(x):
        return x - from_below(x), x - from_right(x)

    def corners(diff_h, diff_v):
        return (
            (vr * diff_h, hb * diff_v),
            (vl * diff_h, -from_left(hb * diff_v)),
            (-from_above(vr * diff_h), ht * diff_v),
            (-from_above(vl * diff_h), -from_left(ht * diff_v)),
        )

    def tile_product(along_h, along_v, first, second):
        value = along_h + from_above(along_h) + along_v + from_left(along_v)
        for (ah, av), (bh, bv) in zip(first, second):
            value = value + ah * bv + av * bh
        return value

    weight, *pull = tile_sums(targets)
    flat = [e - low(e) for e in pull]
    step = [differences(d) for d in flat]
    gap = [d - up(d) for d in flat]
    norm = total(flat[0] * flat[0] + flat[1] * flat[1]) * nodes
    energy = sum(kh * h * h + kv * v * v for h, v in step)
    energy = energy + nodes * weight * (gap[0] * gap[0] + gap[1] * gap[1])
    alpha = norm / total(energy)

    index = jnp.maximum(owner, 0.0).astype(jnp.int32)
    inside_index = lax.rem(index, tiles)
    row_index = lax.div(index, tiles)
    look = []
    for k in range(2):
        shift = alpha * gap[k]
        rows_of = []
        for p in range(0, owner.shape[0], tiles):
            value = jnp.zeros((tiles, sections), F32)
            for g in range(groups):
                picked = jnp.take_along_axis(
                    shift[g * tiles : (g + 1) * tiles], inside_index[p : p + tiles], axis=0
                )
                value = jnp.where(row_index[p : p + tiles] == g, picked, value)
            rows_of.append(value)
        look.append(jnp.concatenate(rows_of, 0))
    weight, *pull = tile_sums([look[k] - targets[k] for k in range(2)])
    weight_low = low(weight)
    const = [
        pull[k] - low(pull[k]) - alpha * (weight * gap[k] - weight_low * low(gap[k]))
        for k in range(2)
    ]
    plain = jnp.zeros_like(kh)
    mixed = jnp.zeros_like(kh)
    quad = jnp.zeros_like(kh)
    p_energy = jnp.zeros_like(kh)
    m_energy = jnp.zeros_like(kh)
    q_energy = jnp.zeros_like(kh)
    for k in range(2):
        c = const[k]
        ch, cv = differences(c)
        h, v = step[k]
        ends = corners(h, v)
        c_ends = corners(ch, cv)
        square = tile_product(k2h * h * h, k2v * v * v, ends, ends)
        across = tile_product(
            kxh * h * up(h), kxv * v * up(v), ends, [(up(a), up(b)) for a, b in ends]
        )
        gap_square = square + up(square) - 2.0 * across
        flux_h, flux_v = kh * h, kv * v
        inner = flux_h - from_above(flux_h) + flux_v - from_left(flux_v)
        gap_c = c - up(c)
        gap_q = inner - up(inner)
        plain = plain + c * c
        mixed = mixed + c * inner
        quad = quad + square
        p_energy = p_energy + kh * ch * ch + kv * cv * cv + nodes * weight * gap_c * gap_c
        m_energy = (
            m_energy
            + tile_product(k2h * ch * h, k2v * cv * v, c_ends, ends)
            + weight * gap_c * gap_q
        )
        above_h, left_v = from_above(h), from_left(v)
        value = dh * h * h + dt * above_h * above_h + dv * v * v
        value = value + 2.0 * (
            xbr * h * v + xbl * h * left_v + xtr * above_h * v + xtl * above_h * left_v
        )
        (br_h, br_v), (bl_h, bl_v), (tr_h, tr_v), (tl_h, tl_v) = ends
        for stiff, part, extra, fold in (
            (vr, br_h, br_v - from_below(tr_v), fold_h),
            (vl, bl_h, bl_v - from_below(tl_v), fold_h),
            (hb, br_v, br_h - from_right(bl_h), fold_v),
            (ht, tr_v, tr_h - from_right(tl_h), fold_v),
        ):
            value = value + stiff * extra * (2.0 * fold * part + extra)
        q_energy = q_energy + value + weight * gap_square
    norm = nodes * total(plain) - 2.0 * alpha * total(mixed) + alpha * alpha * total(quad)
    energy = total(p_energy) - 2.0 * alpha * total(m_energy) + alpha * alpha * total(q_energy)
    beta = norm / energy

    own_figures = (*flat, *const, step[0][0], step[1][0], step[0][1], step[1][1], ht, hb, weight, weight_low)
    beside = (*const, step[0][0], step[1][0], step[0][1], step[1][1])
    wanted = [(x, me) for x in own_figures] + [(x, me + 1) for x in beside] + [(x, me - 1) for x in beside]
    for n, (x, section) in enumerate(wanted):
        out_ref[n, 0:tiles, :] = zero_tiles
        out_ref[n, tiles + count : 2 * tiles + count, :] = zero_tiles
        picked = lane_sum(jnp.where(lane == section, x, 0.0))
        out_ref[n, tiles : tiles + count, :] = jnp.broadcast_to(picked, (count, sections))

    def spread(n, shift):
        start = pl.multiple_of((group + 1 + shift) * tiles, tiles)
        return out_ref[n, pl.ds(start, tiles), :]

    wide_lane = iota((rows, TILE_W), 1)
    wide_row = iota((rows, TILE_W), 0)
    first_lane, last_lane = wide_lane == 0, wide_lane == TILE_W - 1
    first_row, last_row = wide_row == 0, wide_row == rows - 1
    line_first, line_last = first_lane[0:1], last_lane[0:1]
    inside = jnp.where(group < groups - 1, 1.0, 0.0).astype(F32)

    def image(edges, offset, k, j):
        last_line, above_line, columns = edges
        def line(n, shift=0, at=j):
            return spread(offset + n + k, shift)[at : at + 1, :]

        value = jnp.where(last_row, last_line[j : j + 1, :] * line(0), 0.0)
        value = value - jnp.where(first_row, above_line[j : j + 1, :] * line(0, -1), 0.0)
        value = value + jnp.where(last_lane, columns(j) * line(2), 0.0)
        if j:
            value = value - jnp.where(first_lane, columns(j - 1) * line(2, 0, j - 1), 0.0)
        return value

    own_line, own_above = own_line_ref[...], own_above_ref[...]
    next_columns, prev_columns = next_columns_ref[...], prev_columns_ref[...]
    own_edges = (own_line, own_above, lambda j: hori_ref[:, (j + 1) * TILE_W - 1 : (j + 1) * TILE_W])
    next_edges = (lines_ref[0:tiles, :], aboves_ref[0:tiles, :], lambda j: next_columns[:, j : j + 1])
    prev_edges = (lines_ref[tiles:, :], aboves_ref[tiles:, :], lambda j: prev_columns[:, j : j + 1])
    for k in range(2):
        for j in range(tiles):
            span = slice(j * TILE_W, (j + 1) * TILE_W)

            def line(n, shift, at=j):
                return spread(n + k, shift)[at : at + 1, :]

            field_ref[k, tiles : tiles + rows, span] = line(2, 0) - alpha * image(own_edges, 4, k, j)
            near = -inside * own_line[j : j + 1, :] * line(4, 0)
            near = near + jnp.where(line_last, spread(8, 1)[j : j + 1, :] * line(6, 1), 0.0)
            far = own_above[j : j + 1, :] * line(4, -1)
            far = far + jnp.where(line_last, spread(9, -1)[j : j + 1, :] * line(6, -1), 0.0)
            if j:
                near = near - jnp.where(line_first, spread(8, 1)[j - 1 : j, :] * line(6, 1, j - 1), 0.0)
                far = far - jnp.where(line_first, spread(9, -1)[j - 1 : j, :] * line(6, -1, j - 1), 0.0)
            field_ref[k, tiles + rows : tiles + rows + 1, span] = line(2, 1) - alpha * near
            field_ref[k, tiles - 1 : tiles, span] = line(2, -1) - alpha * far
    weight_rows, weight_low_rows = spread(10, 0), spread(11, 0)
    for k in range(2):
        flux_left = None
        for j in range(tiles):
            span = slice(j * TILE_W, (j + 1) * TILE_W)
            r = field_ref[k, tiles : tiles + rows, span]
            right = pltpu.roll(r, TILE_W - 1, 1)
            if j < tiles - 1:
                beyond = field_ref[k, tiles : tiles + rows, (j + 1) * TILE_W : (j + 2) * TILE_W]
                right = jnp.where(last_lane, pltpu.roll(beyond, TILE_W - 1, 1), right)
            else:
                right = jnp.where(last_lane, 0.0, right)
            flux = hori_ref[:, span] * (r - right)
            turned = pltpu.roll(flux, 1, 1)
            before = jnp.where(first_lane, 0.0 if flux_left is None else flux_left, turned)
            flux_left = turned
            below = field_ref[k, tiles + 1 : tiles + rows + 1, span]
            fall = vert_ref[:, span] * (r - below)
            edge = own_above[j : j + 1, :] * (field_ref[k, tiles - 1 : tiles, span] - r[0:1, :])
            fall_above = jnp.where(first_row, edge, pltpu.roll(fall, 1, 0))
            applied = flux - before + fall - fall_above
            r_next = spread(12 + k, 0)[j : j + 1, :] - alpha * image(next_edges, 14, k, j)
            r_prev = spread(18 + k, 0)[j : j + 1, :] - alpha * image(prev_edges, 20, k, j)
            applied = applied + weight_rows[j : j + 1, :] * (r - r_next) + weight_low_rows[j : j + 1, :] * (r - r_prev)
            disp_ref[k, :, span] = alpha * spread(k, 0)[j : j + 1, :] + beta * r
            res_ref[k, :, span] = r - beta * applied


def in_vmem(x):
    return pltpu.VMEM(x.shape, x.dtype)


def from_behind(block, axis, distance):
    devices = range(lax.axis_size(axis))
    route = [(i - distance, i) for i in devices if i - distance in devices]
    return lax.ppermute(block, axis, route)


def plane_order(groups, core):
    order = [
        ((FIRST_GROUP + g) % groups, (FIRST_CHIP[core] + y) % CHIPS_Y)
        for g in range(groups)
        for y in range(CHIPS_Y)
    ]
    order.remove(ORIGIN)
    order.insert(ORIGIN_PLACE, ORIGIN)
    return order


def planes(groups, chips_z):
    return [
        [((g * chips_z + z) * CHIPS_Y + y) * CORES + core for g, y in plane_order(groups, core)]
        for z in range(chips_z)
        for core in range(CORES)
    ]


def swap(block, first):
    route = []
    for s in range(first, lax.axis_size(SEC) - 1, 2):
        route += [(s, s + 1), (s + 1, s)]
    return lax.ppermute(block, SEC, route)


def body(fixed_desc, moving_desc, offsets, owner, counts, vert, hori):
    groups = lax.axis_size("group")
    sections = lax.axis_size(SEC)
    chips_z = lax.axis_size("z")
    patches, flow, corr = fixed_desc.shape[1:]
    rows, cols = vert.shape[1:]
    tiles = cols // TILE_W
    length = patches * flow
    halves = -(-tiles * GROUP_LANES // TILE_W)

    hbm = pl.BlockSpec(memory_space=pltpu.HBM)
    local = pl.BlockSpec(memory_space=pltpu.VMEM)
    scalars = pl.BlockSpec(memory_space=pltpu.SMEM)
    modest = pltpu.CompilerParams(vmem_limit_bytes=16 << 20)
    border = jax.ShapeDtypeStruct((tiles, TILE_W), F32)
    upright = jax.ShapeDtypeStruct((rows, TILE_W), F32)
    lines_shape = jax.ShapeDtypeStruct((2 * tiles, TILE_W), F32)
    packed = pltpu.VMEM((length // 2 + rows, corr), fixed_desc.dtype)
    across, beside, line = pl.pallas_call(
        pack_kernel,
        out_shape=(packed, packed, in_vmem(border)),
        in_specs=[hbm] * 5,
        out_specs=(local,) * 3,
        scratch_shapes=[
            pltpu.VMEM((rows, cols), F32),
            pltpu.VMEM((rows, cols), F32),
            pltpu.VMEM(offsets.shape[1:], jnp.int32),
            pltpu.SemaphoreType.DMA((2 * PARTS + 3,)),
        ],
        compiler_params=modest,
        name="pack",
    )(
        *(
            pltpu.with_memory_space_constraint(x, pltpu.HBM)
            for x in (moving_desc.reshape(length, corr), fixed_desc.reshape(length, corr), vert, hori, offsets)
        )
    )
    across = swap(across, 1)
    beside = swap(beside, 0)
    above = from_behind(line, "group", 1)

    vert, hori = vert[0], hori[0]

    def borders(*refs):
        border_kernel(groups, *refs)

    table, firsts, right = pl.pallas_call(
        borders,
        out_shape=(in_vmem(border), in_vmem(lines_shape), in_vmem(upright)),
        in_specs=[scalars] * 2 + [local] * 3,
        out_specs=(local,) * 3,
        scratch_shapes=[pltpu.VMEM((TILE_W, TILE_W), F32)],
        compiler_params=modest,
        name="borders",
    )(owner, counts, vert, hori, line)
    mine, lines, next_columns, prev_columns = pl.pallas_call(
        match_kernel,
        out_shape=(
            pltpu.VMEM((chips_z, halves, TILE_W), F32),
            in_vmem(lines_shape), in_vmem(upright), in_vmem(upright),
        ),
        in_specs=[local] * 10,
        out_specs=(local,) * 4,
        scratch_shapes=[pltpu.VMEM((flow, length), F32), pltpu.VMEM((tiles, TILE_W), F32)],
        compiler_params=modest,
        name="match",
    )(fixed_desc, moving_desc, offsets, table, firsts, right, line, above, across, beside)

    turned = [(z + FIRST_Z) % chips_z for z in range(chips_z)]
    seen = lax.all_to_all(mine, "z", 0, 0, tiled=True, axis_index_groups=[turned]).reshape(-1, TILE_W)
    lines, seen = lax.optimization_barrier((lines, seen))
    aboves = from_behind(lines, "group", 1)
    peers = groups * lax.axis_size("y")
    block_rows = chips_z + chips_z // 2
    copies = pl.pallas_call(
        copies_kernel,
        out_shape=jax.ShapeDtypeStruct((peers, block_rows, TILE_W), F32),
        in_specs=[local],
        out_specs=local,
        scratch_shapes=[pltpu.VMEM((2 * chips_z, TILE_W), F32)],
        compiler_params=modest,
        name="copies",
    )(seen)
    seen = lax.all_to_all(
        copies, ("group",) + SEC, 0, 0, tiled=True, axis_index_groups=planes(groups, chips_z)
    ).reshape(-1, TILE_W)
    cores = list(reversed(range(CORES)))
    seen = lax.all_gather(seen, "core", axis=0, tiled=True, axis_index_groups=[cores])

    dims = (groups, sections, rows, tiles, chips_z)
    count = groups * tiles

    def both_iterations(*refs):
        stack_kernel(dims, *refs)

    field = jax.ShapeDtypeStruct((2, rows, cols), F32)
    displacement, residual = pl.pallas_call(
        both_iterations,
        out_shape=(field, field),
        in_specs=[local] * 9,
        scratch_shapes=[
            pltpu.VMEM((groups + groups // 2, sections, TILE_W), F32),
            pltpu.VMEM((groups, tiles * GROUP_LANES, sections), F32),
            pltpu.VMEM((3, count, sections), F32),
            pltpu.VMEM((24, count + 2 * tiles, sections), F32),
            pltpu.VMEM((2, rows + 2 * tiles, cols), F32),
        ],
        compiler_params=modest,
        name="stack",
    )(seen, vert, hori, line, above, lines, aboves, next_columns, prev_columns)
    return (displacement[None], residual[None])


def solution(mesh):
    groups, sections = mesh.devices.shape
    devices = mesh.devices.reshape(groups, sections // (CHIPS_Y * CORES), CHIPS_Y, CORES)
    fine = Mesh(devices, ("group",) + SEC)
    in_specs = (
        P(SEC, "group", None, None),
        P(SEC, "group", None, None),
        P(SEC, "group", None, None),
        P(SEC, "group"),
        P(SEC, "group"),
        P(SEC, "group", None),
        P(SEC, "group", None),
    )
    out_specs = (P(SEC, None, "group", None), P(SEC, None, "group", None))
    return jax.shard_map(body, mesh=fine, in_specs=in_specs, out_specs=out_specs, check_vma=False)
```

```python
import math

import jax
import jax.numpy as jnp
from jax import lax
from jax.experimental import pallas as pl
from jax.experimental.pallas import tpu as pltpu
from jax.sharding import Mesh, PartitionSpec as P

TILE_W = 128
SPREAD_SQ = 4.0
CHIPS_Y = 4
CORES = 2
SEC = ("z", "y", "core")
F32 = jnp.float32

COLUMN_KV, COLUMN_K2V, COLUMN_KXV, COLUMN_VL, COLUMN_VR, COLUMN_HT, COLUMN_HB = range(7)
COLUMN_DV, COLUMN_XBR, COLUMN_XBL, COLUMN_XTR, COLUMN_XTL = range(7, 12)
COLUMN_KH, COLUMN_K2H, COLUMN_KXH, COLUMN_DH, COLUMN_DT = range(12, 17)
COLUMN_OWNER = 17
COLUMN_NEAR = 19
COLUMN_FAR = 21
COLUMN_HELP = 23
GROUP_LANES = 24
FIRST_Z = 8
FIRST_GROUP = 2
FIRST_CHIP = (2, 2)
ORIGIN = (0, 0)
ORIGIN_PLACE = 15
PARTS = 1


def iota(shape, axis):
    return lax.broadcasted_iota(jnp.int32, shape, axis)


def lane_sum(x):
    return jnp.sum(x, axis=1, keepdims=True)


def row_sum(x):
    return jnp.sum(x, axis=0, keepdims=True)


def total(x):
    return lane_sum(row_sum(x))


def three_parts(x):
    high = x.astype(jnp.bfloat16).astype(F32)
    middle = (x - high).astype(jnp.bfloat16).astype(F32)
    return high, middle, x - high - middle


def pack_kernel(
    moving_ref, fixed_ref, vert_ref, hori_ref, offsets_ref, across_ref, beside_ref, line_ref,
    vert, hori, offsets, sems,
):
    rows, cols = hori.shape
    tiles = cols // TILE_W
    length = moving_ref.shape[0] // 2
    part = length // PARTS
    loads = [
        pltpu.make_async_copy(vert_ref.at[0], vert, sems.at[0]),
        pltpu.make_async_copy(hori_ref.at[0], hori, sems.at[1]),
        pltpu.make_async_copy(offsets_ref.at[0], offsets, sems.at[2]),
    ]
    for copy in loads:
        copy.start()

    def features(back, ahead):
        copies = []
        for n in range(PARTS):
            at, behind = pl.ds(n * part, part), pl.ds(length + n * part, part)
            copies.append(pltpu.make_async_copy(moving_ref.at[at], back.at[at], sems.at[3 + 2 * n]))
            copies.append(pltpu.make_async_copy(fixed_ref.at[behind], ahead.at[at], sems.at[4 + 2 * n]))
        return copies

    first = lax.axis_index("core") == 0

    @pl.when(first)
    def _():
        for copy in features(across_ref, beside_ref):
            copy.start()

    @pl.when(jnp.logical_not(first))
    def _():
        for copy in features(beside_ref, across_ref):
            copy.start()

    for copy in loads:
        copy.wait()
    lane = iota((rows, TILE_W), 1)
    column = jnp.zeros((rows, TILE_W), F32)
    for j in range(tiles):
        span = slice(j * TILE_W, (j + 1) * TILE_W)
        line_ref[j : j + 1, :] = vert[rows - 1 : rows, span]
        end = (j + 1) * TILE_W - 1
        column = jnp.where(lane == j, hori[:, end : end + 1], column)
    high, middle, small = three_parts(column)
    columns = high + pltpu.roll(middle, tiles, 1) + pltpu.roll(small, 2 * tiles, 1)
    half = offsets.shape[0] // 2
    shifts = jnp.concatenate([offsets[half:, 0, :], offsets[half:, 1, :]], 1).astype(F32)
    blank = jnp.zeros((tiles, TILE_W), F32)
    for ref in (across_ref, beside_ref):
        for n, value in enumerate(three_parts(line_ref[...])):
            block = jnp.concatenate([value, blank if n else shifts], 0)
            ref[length:, n * TILE_W : (n + 1) * TILE_W] = block.astype(jnp.bfloat16)
        ref[length:, 3 * TILE_W :] = columns.astype(jnp.bfloat16)
    for copy in features(across_ref, beside_ref):
        copy.wait()


def unpack(extra, tiles):
    parts = [extra[:, n * TILE_W : (n + 1) * TILE_W].astype(F32) for n in range(4)]
    line = parts[0][:tiles] + (parts[1][:tiles] + parts[2][:tiles])
    columns = parts[3]
    back = TILE_W - tiles
    columns = columns + (pltpu.roll(columns, back, 1) + pltpu.roll(columns, back - tiles, 1))
    return line, columns, parts[0][tiles:]


def border_kernel(groups, owner_ref, counts_ref, vert_ref, hori_ref, line_ref, out_ref, firsts_ref, right_ref, stack):
    rows, cols = hori_ref.shape
    tiles = cols // TILE_W
    last_group = lax.axis_index("group") == groups - 1
    bottom = jnp.where(last_group, 1.0, 4.0).astype(F32)

    v_last = line_ref[...]
    for j in range(tiles):
        span = slice(j * TILE_W, (j + 1) * TILE_W)
        stack[j : j + 1, :] = vert_ref[rows - 2 : rows - 1, span]
        stack[tiles + j : tiles + j + 1, :] = hori_ref[rows - 1 : rows, span]
        firsts_ref[j : j + 1, :] = vert_ref[0:1, span]
        firsts_ref[tiles + j : tiles + j + 1, :] = hori_ref[0:1, span]
    v_second, h_last = stack[0:tiles, :], stack[tiles : 2 * tiles, :]
    lane = iota((tiles, TILE_W), 1)
    inside = lane < TILE_W - 1
    square = v_last * v_last
    step_last = v_last - pltpu.roll(v_last, TILE_W - 1, 1)
    dh = lane_sum(
        bottom * square * v_last
        + v_second * square
        + jnp.where(inside, h_last * step_last * step_last, 0.0)
    )
    sub = iota((tiles, TILE_W), 0)
    table = jnp.zeros((tiles, TILE_W), F32)
    for p in range(owner_ref.shape[1]):
        live = jnp.where(p < counts_ref[0, 0], owner_ref[0, p], -1).astype(F32)
        spot = (sub == p % tiles) & (lane == COLUMN_OWNER + p // tiles)
        table = jnp.where(spot, live, table)
    for column, value in (
        (COLUMN_KH, lane_sum(v_last)),
        (COLUMN_K2H, lane_sum(square)),
        (COLUMN_DH, dh),
    ):
        table = jnp.where(lane == column, value, table)

    tall = iota((rows, TILE_W), 1)
    zero = jnp.zeros((rows, TILE_W), F32)
    picked = {}
    for name, ref, column in (
        ("h127", hori_ref, TILE_W - 1),
        ("h0", hori_ref, 0),
        ("h126", hori_ref, TILE_W - 2),
        ("v0", vert_ref, 0),
        ("v1", vert_ref, 1),
        ("v126", vert_ref, TILE_W - 2),
        ("v127", vert_ref, TILE_W - 1),
    ):
        value = zero
        for j in range(tiles):
            at = j * TILE_W + column
            value = jnp.where(tall == j, ref[:, at : at + 1], value)
        picked[name] = value
    right = picked["h127"]
    left = pltpu.roll(right, 1, 1)
    row = iota((rows, TILE_W), 0)
    within = row < rows - 1
    inner_tile = iota((1, TILE_W), 1) < tiles - 1
    step_right = right - pltpu.roll(right, rows - 1, 0)
    step_left = left - pltpu.roll(left, rows - 1, 0)
    right_sq, left_sq = right * right, left * left
    side_right = row_sum(
        picked["h126"] * right_sq + jnp.where(within, picked["v127"] * step_right * step_right, 0.0)
    )
    side_left = row_sum(
        picked["h0"] * left_sq + jnp.where(within, picked["v0"] * step_left * step_left, 0.0)
    )
    cube = row_sum(right_sq * right)
    dv = side_right + jnp.where(
        inner_tile, pltpu.roll(side_left, TILE_W - 1, 1) + 4.0 * cube, cube
    )
    end, pre = rows - 1, rows - 2
    v0, v1, v126, v127 = (picked[n] for n in ("v0", "v1", "v126", "v127"))
    h0, h126 = picked["h0"], picked["h126"]

    def at(x, r):
        return x[r : r + 1, :]

    xbr = at(h126, end) * (at(v127, end) - at(v126, end)) * at(right, end) + at(v127, pre) * at(
        v127, end
    ) * (at(right, end) - at(right, pre))
    xbl = -(
        at(h0, end) * (at(v0, end) - at(v1, end)) * at(left, end)
        + at(v0, pre) * at(v0, end) * (at(left, end) - at(left, pre))
    )
    along_last, along_first = at(h126, 0) * at(right, 0), at(h0, 0) * at(left, 0)
    fall_last = at(v127, 0) * (at(right, 0) - at(right, 1))
    fall_first = at(v0, 0) * (at(left, 0) - at(left, 1))
    right_ref[...] = right
    stack[...] = jnp.zeros_like(stack)
    for column, value in (
        (COLUMN_KV, row_sum(right)),
        (COLUMN_K2V, row_sum(right_sq)),
        (COLUMN_VL, at(v0, end)),
        (COLUMN_VR, at(v127, end)),
        (COLUMN_HT, at(right, 0)),
        (COLUMN_HB, at(right, end)),
        (COLUMN_DV, dv),
        (COLUMN_XBR, xbr),
        (COLUMN_XBL, xbl),
        (COLUMN_HELP, -along_last - fall_last),
        (COLUMN_HELP + 1, along_last),
        (COLUMN_HELP + 2, along_first + fall_first),
        (COLUMN_HELP + 3, -along_first),
    ):
        stack[column : column + 1, :] = value
    turned = jnp.transpose(stack[...])[0:tiles, :]
    upright = (lane <= COLUMN_XTL) | (lane >= COLUMN_HELP)
    out_ref[...] = jnp.where(upright, turned, table)


def match_kernel(
    fixed_ref, moving_ref, offsets_ref, table_ref, firsts_ref, right_ref, line_ref, above_ref, across_ref, beside_ref,
    out_ref, lines_ref, next_columns_ref, prev_columns_ref, scores_ref, shifts_ref,
):
    patches, flow, corr = fixed_ref.shape[1:]
    half = patches // 2
    rows = right_ref.shape[0]
    tiles = line_ref.shape[0]
    pair = 2 * flow
    lower = iota((flow, pair), 1) < flow

    def receive(near_ref, far_ref):
        for first in range(0, patches, 2):
            own = slice(first, first + 2)
            if first < half:
                fixed = fixed_ref[0, own].reshape(pair, corr)
                moving = near_ref[first * flow : (first + 2) * flow, :]
            else:
                fixed = far_ref[(first - half) * flow : (first + 2 - half) * flow, :]
                moving = moving_ref[0, own].reshape(pair, corr)
            scores = lax.dot_general(moving, fixed, (((1,), (1,)), ((), ())), preferred_element_type=F32)
            scores_ref[:, first * flow : (first + 2) * flow] = jnp.where(
                lower, scores[0:flow, :], scores[flow:pair, :]
            )
        next_line, next_columns, _ = unpack(near_ref[half * flow :, :], tiles)
        prev_line, prev_columns, shifts = unpack(far_ref[half * flow :, :], tiles)
        lines_ref[0:tiles, :] = next_line
        lines_ref[tiles:, :] = prev_line
        next_columns_ref[...] = next_columns
        prev_columns_ref[...] = prev_columns
        shifts_ref[...] = shifts

    first_core = lax.axis_index("core") == 0

    @pl.when(first_core)
    def _():
        receive(beside_ref, across_ref)

    @pl.when(jnp.logical_not(first_core))
    def _():
        receive(across_ref, beside_ref)

    next_line, next_columns, shifts = lines_ref[0:tiles, :], next_columns_ref[...], shifts_ref[...]
    scores = scores_ref[...]
    top = jnp.max(scores, axis=0, keepdims=True)
    likely = jnp.exp((scores - top) * (1.0 / math.sqrt(corr)))
    offsets = []
    for k in range(2):
        offsets.append(offsets_ref[0, 0:half, k, :].astype(F32))
        offsets.append(shifts[:, k * flow : (k + 1) * flow])
    shifted = jnp.concatenate(offsets, 0).astype(jnp.bfloat16)
    parts = [part.astype(jnp.bfloat16) for part in three_parts(likely)]
    sums = lax.dot_general(
        jnp.concatenate([shifted] * 3, 1),
        jnp.concatenate(parts, 0),
        (((1,), (0,)), ((), ())),
        preferred_element_type=F32,
    )
    weight = row_sum(likely) * flow
    mine = lax.rem(iota(sums.shape, 0), patches) == lax.div(iota(sums.shape, 1), flow)
    ratio = lane_sum(jnp.where(mine, sums, 0.0) / weight)

    table = table_ref[...]
    lane = iota(table.shape, 1)

    def helper(n):
        return table[:, COLUMN_HELP + n : COLUMN_HELP + n + 1]

    line, above = line_ref[...], above_ref[...]
    step = above - pltpu.roll(above, TILE_W - 1, 1)
    top_energy = firsts_ref[0:tiles, :] * above * above + jnp.where(
        lane < TILE_W - 1, firsts_ref[tiles:, :] * step * step, 0.0
    )
    diagonal = iota(table.shape, 0) == lane
    across = row_sum(right_ref[...] * next_columns)
    columns = [
        (COLUMN_XTR, above[:, TILE_W - 1 :] * helper(0) + above[:, TILE_W - 2 : TILE_W - 1] * helper(1)),
        (COLUMN_XTL, above[:, 0:1] * helper(2) + above[:, 1:2] * helper(3)),
        (COLUMN_DT, lane_sum(top_energy)),
        (COLUMN_KXH, lane_sum(line * next_line)),
        (COLUMN_KXV, lane_sum(jnp.where(diagonal, across, 0.0))),
    ]
    for k in range(2):
        columns.append((COLUMN_NEAR + k, ratio[2 * k * half : (2 * k + 1) * half]))
        columns.append((COLUMN_FAR + k, ratio[(2 * k + 1) * half : (2 * k + 2) * half]))
    for column, value in columns:
        table = jnp.where(lane == column, value, table)

    table = jnp.where(lane < COLUMN_HELP, table, 0.0)
    pieces = [jnp.zeros((1, TILE_W), F32) for _ in range(out_ref.shape[1])]
    place = iota((1, TILE_W), 1)
    for j in range(tiles):
        part, start = divmod(j * GROUP_LANES, TILE_W)
        source = table[j : j + 1, :]
        source = pltpu.roll(source, start, 1) if start else source
        if start + GROUP_LANES > TILE_W:
            pieces[part] = pieces[part] + jnp.where(place >= start, source, 0.0)
            pieces[part + 1] = pieces[part + 1] + jnp.where(place < start, source, 0.0)
        else:
            pieces[part] = pieces[part] + source
    for part, piece in enumerate(pieces):
        for n in range(out_ref.shape[0]):
            out_ref[n, part : part + 1, :] = piece


def copies_kernel(seen_ref, out_ref, block):
    chips = seen_ref.shape[0] // 2
    shared = chips // 2
    lead = chips - FIRST_Z
    block[0:FIRST_Z, :] = seen_ref[pl.ds(2 * lead, FIRST_Z, stride=2), :]
    block[FIRST_Z:chips, :] = seen_ref[pl.ds(0, lead, stride=2), :]
    block[chips : chips + FIRST_Z, :] = seen_ref[pl.ds(2 * lead + 1, FIRST_Z, stride=2), :]
    block[chips + FIRST_Z :, :] = seen_ref[pl.ds(1, lead, stride=2), :]
    first = block[0:chips, :]
    second = block[chips : chips + shared, :] + pltpu.roll(block[chips + shared :, :], TILE_W // 2, 1)
    for n in range(out_ref.shape[0]):
        out_ref[n, 0:chips, :] = first
        out_ref[n, chips:, :] = second


def stack_kernel(
    dims, seen_ref, vert_ref, hori_ref, own_line_ref, own_above_ref,
    lines_ref, aboves_ref, next_columns_ref, prev_columns_ref,
    disp_ref, res_ref, rows_ref, turn_ref, sums_ref, out_ref, field_ref,
):
    groups, sections, rows, tiles, chips_z = dims
    per_chip = sections // chips_z
    count = groups * tiles
    nodes = float(rows * TILE_W)
    me, group = lax.axis_index(SEC), lax.axis_index("group")

    shared = chips_z // 2
    half_lanes = TILE_W // 2
    for core in range(CORES):
        for g in range(groups):
            for y in range(per_chip // CORES):
                place = (CORES - 1 - core) * groups * CHIPS_Y + plane_order(groups, core).index((g, y))
                base = place * (chips_z + shared)
                chip = y * CORES + core
                rows_ref[g, pl.ds(chip, chips_z, stride=per_chip), :] = seen_ref[base : base + chips_z, :]
                rows_ref[
                    groups + g // 2, pl.ds((g % 2) * (sections // 2) + chip, shared, stride=per_chip), :
                ] = seen_ref[base + chips_z : base + chips_z + shared, :]
    left_half = iota((half_lanes, sections), 1) < sections // 2
    for g in range(groups):
        turn_ref[g, 0:TILE_W, :] = jnp.transpose(rows_ref[g])
    for pair in range(groups // 2):
        turned = jnp.transpose(rows_ref[groups + pair])
        low_half, high_half = turned[0:half_lanes, :], turned[half_lanes:, :]
        turn_ref[2 * pair, TILE_W:, :] = jnp.where(
            left_half, low_half, pltpu.roll(high_half, sections // 2, 1)
        )
        turn_ref[2 * pair + 1, TILE_W:, :] = jnp.where(
            left_half, pltpu.roll(low_half, sections // 2, 1), high_half
        )

    def block(g, column):
        return turn_ref[g, pl.ds(column, tiles, stride=GROUP_LANES), :]

    def figure(column):
        return jnp.concatenate([block(g, column) for g in range(groups)], 0)

    def slots(near, far, turn):
        parts = []
        for g in range(groups):
            parts.append(block(g, near))
            other = block(g, far)
            parts.append(pltpu.roll(other, sections - 1, 1) if turn else other)
        return jnp.concatenate(parts, 0)

    lane = iota((count, sections), 1)
    tile_row = iota((count, sections), 0)
    along = lax.rem(tile_row, tiles)
    not_last = lane < sections - 1

    def up(x):
        return jnp.where(not_last, pltpu.roll(x, sections - 1, 1), 0.0)

    def low(x):
        return jnp.where(lane > 0, pltpu.roll(x, 1, 1), 0.0)

    zero_tiles = jnp.zeros((tiles, sections), F32)

    def from_above(x):
        return jnp.concatenate([zero_tiles, x[: count - tiles]], 0)

    def from_below(x):
        return jnp.concatenate([x[tiles:], zero_tiles], 0)

    def from_left(x):
        return jnp.where(along > 0, pltpu.roll(x, 1, 0), 0.0)

    def from_right(x):
        return jnp.where(along < tiles - 1, pltpu.roll(x, count - 1, 0), 0.0)

    owner = slots(COLUMN_OWNER, COLUMN_OWNER + 1, False)
    targets = [slots(COLUMN_NEAR + k, COLUMN_FAR + k, True) for k in range(2)]
    valid = jnp.where(owner >= 0.0, 1.0, 0.0)

    def tile_sums(miss):
        weight = valid / (1.0 + (miss[0] * miss[0] + miss[1] * miss[1]) / SPREAD_SQ)
        terms = (weight, weight * targets[0], weight * targets[1])
        for t in range(count):
            mine = owner == float(t)
            for n, term in enumerate(terms):
                sums_ref[n, t : t + 1, :] = row_sum(jnp.where(mine, term, 0.0))
        return [jnp.where(not_last, sums_ref[n], 0.0) for n in range(3)]

    kh, kv = figure(COLUMN_KH), figure(COLUMN_KV)
    k2h, k2v = figure(COLUMN_K2H), figure(COLUMN_K2V)
    kxh, kxv = figure(COLUMN_KXH), figure(COLUMN_KXV)
    vl, vr = figure(COLUMN_VL), figure(COLUMN_VR)
    ht, hb = figure(COLUMN_HT), figure(COLUMN_HB)
    dh, dt, dv = figure(COLUMN_DH), figure(COLUMN_DT), figure(COLUMN_DV)
    xbr, xbl, xtr, xtl = (figure(c) for c in (COLUMN_XBR, COLUMN_XBL, COLUMN_XTR, COLUMN_XTL))
    fold_h = jnp.where(tile_row < count - tiles, 2.0, 1.0)
    fold_v = jnp.where(along < tiles - 1, 2.0, 1.0)

    def differences(x):
        return x - from_below(x), x - from_right(x)

    def corners(diff_h, diff_v):
        return (
            (vr * diff_h, hb * diff_v),
            (vl * diff_h, -from_left(hb * diff_v)),
            (-from_above(vr * diff_h), ht * diff_v),
            (-from_above(vl * diff_h), -from_left(ht * diff_v)),
        )

    def tile_product(along_h, along_v, first, second):
        value = along_h + from_above(along_h) + along_v + from_left(along_v)
        for (ah, av), (bh, bv) in zip(first, second):
            value = value + ah * bv + av * bh
        return value

    weight, *pull = tile_sums(targets)
    flat = [e - low(e) for e in pull]
    step = [differences(d) for d in flat]
    gap = [d - up(d) for d in flat]
    norm = total(flat[0] * flat[0] + flat[1] * flat[1]) * nodes
    energy = sum(kh * h * h + kv * v * v for h, v in step)
    energy = energy + nodes * weight * (gap[0] * gap[0] + gap[1] * gap[1])
    alpha = norm / total(energy)

    index = jnp.maximum(owner, 0.0).astype(jnp.int32)
    inside_index = lax.rem(index, tiles)
    row_index = lax.div(index, tiles)
    look = []
    for k in range(2):
        shift = alpha * gap[k]
        rows_of = []
        for p in range(0, owner.shape[0], tiles):
            value = jnp.zeros((tiles, sections), F32)
            for g in range(groups):
                picked = jnp.take_along_axis(
                    shift[g * tiles : (g + 1) * tiles], inside_index[p : p + tiles], axis=0
                )
                value = jnp.where(row_index[p : p + tiles] == g, picked, value)
            rows_of.append(value)
        look.append(jnp.concatenate(rows_of, 0))
    weight, *pull = tile_sums([look[k] - targets[k] for k in range(2)])
    weight_low = low(weight)
    const = [
        pull[k] - low(pull[k]) - alpha * (weight * gap[k] - weight_low * low(gap[k]))
        for k in range(2)
    ]
    plain = jnp.zeros_like(kh)
    mixed = jnp.zeros_like(kh)
    quad = jnp.zeros_like(kh)
    p_energy = jnp.zeros_like(kh)
    m_energy = jnp.zeros_like(kh)
    q_energy = jnp.zeros_like(kh)
    for k in range(2):
        c = const[k]
        ch, cv = differences(c)
        h, v = step[k]
        ends = corners(h, v)
        c_ends = corners(ch, cv)
        square = tile_product(k2h * h * h, k2v * v * v, ends, ends)
        across = tile_product(
            kxh * h * up(h), kxv * v * up(v), ends, [(up(a), up(b)) for a, b in ends]
        )
        gap_square = square + up(square) - 2.0 * across
        flux_h, flux_v = kh * h, kv * v
        inner = flux_h - from_above(flux_h) + flux_v - from_left(flux_v)
        gap_c = c - up(c)
        gap_q = inner - up(inner)
        plain = plain + c * c
        mixed = mixed + c * inner
        quad = quad + square
        p_energy = p_energy + kh * ch * ch + kv * cv * cv + nodes * weight * gap_c * gap_c
        m_energy = (
            m_energy
            + tile_product(k2h * ch * h, k2v * cv * v, c_ends, ends)
            + weight * gap_c * gap_q
        )
        above_h, left_v = from_above(h), from_left(v)
        value = dh * h * h + dt * above_h * above_h + dv * v * v
        value = value + 2.0 * (
            xbr * h * v + xbl * h * left_v + xtr * above_h * v + xtl * above_h * left_v
        )
        (br_h, br_v), (bl_h, bl_v), (tr_h, tr_v), (tl_h, tl_v) = ends
        for stiff, part, extra, fold in (
            (vr, br_h, br_v - from_below(tr_v), fold_h),
            (vl, bl_h, bl_v - from_below(tl_v), fold_h),
            (hb, br_v, br_h - from_right(bl_h), fold_v),
            (ht, tr_v, tr_h - from_right(tl_h), fold_v),
        ):
            value = value + stiff * extra * (2.0 * fold * part + extra)
        q_energy = q_energy + value + weight * gap_square
    norm = nodes * total(plain) - 2.0 * alpha * total(mixed) + alpha * alpha * total(quad)
    energy = total(p_energy) - 2.0 * alpha * total(m_energy) + alpha * alpha * total(q_energy)
    beta = norm / energy

    own_figures = (*flat, *const, step[0][0], step[1][0], step[0][1], step[1][1], ht, hb, weight, weight_low)
    beside = (*const, step[0][0], step[1][0], step[0][1], step[1][1])
    wanted = [(x, me) for x in own_figures] + [(x, me + 1) for x in beside] + [(x, me - 1) for x in beside]
    for n, (x, section) in enumerate(wanted):
        out_ref[n, 0:tiles, :] = zero_tiles
        out_ref[n, tiles + count : 2 * tiles + count, :] = zero_tiles
        picked = lane_sum(jnp.where(lane == section, x, 0.0))
        out_ref[n, tiles : tiles + count, :] = jnp.broadcast_to(picked, (count, sections))

    def spread(n, shift):
        start = pl.multiple_of((group + 1 + shift) * tiles, tiles)
        return out_ref[n, pl.ds(start, tiles), :]

    wide_lane = iota((rows, TILE_W), 1)
    wide_row = iota((rows, TILE_W), 0)
    first_lane, last_lane = wide_lane == 0, wide_lane == TILE_W - 1
    first_row, last_row = wide_row == 0, wide_row == rows - 1
    line_first, line_last = first_lane[0:1], last_lane[0:1]
    inside = jnp.where(group < groups - 1, 1.0, 0.0).astype(F32)

    def image(edges, offset, k, j):
        last_line, above_line, columns = edges
        def line(n, shift=0, at=j):
            return spread(offset + n + k, shift)[at : at + 1, :]

        value = jnp.where(last_row, last_line[j : j + 1, :] * line(0), 0.0)
        value = value - jnp.where(first_row, above_line[j : j + 1, :] * line(0, -1), 0.0)
        value = value + jnp.where(last_lane, columns(j) * line(2), 0.0)
        if j:
            value = value - jnp.where(first_lane, columns(j - 1) * line(2, 0, j - 1), 0.0)
        return value

    own_line, own_above = own_line_ref[...], own_above_ref[...]
    next_columns, prev_columns = next_columns_ref[...], prev_columns_ref[...]
    own_edges = (own_line, own_above, lambda j: hori_ref[:, (j + 1) * TILE_W - 1 : (j + 1) * TILE_W])
    next_edges = (lines_ref[0:tiles, :], aboves_ref[0:tiles, :], lambda j: next_columns[:, j : j + 1])
    prev_edges = (lines_ref[tiles:, :], aboves_ref[tiles:, :], lambda j: prev_columns[:, j : j + 1])
    for k in range(2):
        for j in range(tiles):
            span = slice(j * TILE_W, (j + 1) * TILE_W)

            def line(n, shift, at=j):
                return spread(n + k, shift)[at : at + 1, :]

            field_ref[k, tiles : tiles + rows, span] = line(2, 0) - alpha * image(own_edges, 4, k, j)
            near = -inside * own_line[j : j + 1, :] * line(4, 0)
            near = near + jnp.where(line_last, spread(8, 1)[j : j + 1, :] * line(6, 1), 0.0)
            far = own_above[j : j + 1, :] * line(4, -1)
            far = far + jnp.where(line_last, spread(9, -1)[j : j + 1, :] * line(6, -1), 0.0)
            if j:
                near = near - jnp.where(line_first, spread(8, 1)[j - 1 : j, :] * line(6, 1, j - 1), 0.0)
                far = far - jnp.where(line_first, spread(9, -1)[j - 1 : j, :] * line(6, -1, j - 1), 0.0)
            field_ref[k, tiles + rows : tiles + rows + 1, span] = line(2, 1) - alpha * near
            field_ref[k, tiles - 1 : tiles, span] = line(2, -1) - alpha * far
    weight_rows, weight_low_rows = spread(10, 0), spread(11, 0)
    for k in range(2):
        flux_left = None
        for j in range(tiles):
            span = slice(j * TILE_W, (j + 1) * TILE_W)
            r = field_ref[k, tiles : tiles + rows, span]
            right = pltpu.roll(r, TILE_W - 1, 1)
            if j < tiles - 1:
                beyond = field_ref[k, tiles : tiles + rows, (j + 1) * TILE_W : (j + 2) * TILE_W]
                right = jnp.where(last_lane, pltpu.roll(beyond, TILE_W - 1, 1), right)
            else:
                right = jnp.where(last_lane, 0.0, right)
            flux = hori_ref[:, span] * (r - right)
            turned = pltpu.roll(flux, 1, 1)
            before = jnp.where(first_lane, 0.0 if flux_left is None else flux_left, turned)
            flux_left = turned
            below = field_ref[k, tiles + 1 : tiles + rows + 1, span]
            fall = vert_ref[:, span] * (r - below)
            edge = own_above[j : j + 1, :] * (field_ref[k, tiles - 1 : tiles, span] - r[0:1, :])
            fall_above = jnp.where(first_row, edge, pltpu.roll(fall, 1, 0))
            applied = flux - before + fall - fall_above
            r_next = spread(12 + k, 0)[j : j + 1, :] - alpha * image(next_edges, 14, k, j)
            r_prev = spread(18 + k, 0)[j : j + 1, :] - alpha * image(prev_edges, 20, k, j)
            applied = applied + weight_rows[j : j + 1, :] * (r - r_next) + weight_low_rows[j : j + 1, :] * (r - r_prev)
            disp_ref[k, :, span] = alpha * spread(k, 0)[j : j + 1, :] + beta * r
            res_ref[k, :, span] = r - beta * applied


def in_vmem(x):
    return pltpu.VMEM(x.shape, x.dtype)


def from_behind(block, axis, distance):
    devices = range(lax.axis_size(axis))
    route = [(i - distance, i) for i in devices if i - distance in devices]
    return lax.ppermute(block, axis, route)


def plane_order(groups, core):
    order = [
        ((FIRST_GROUP + g) % groups, (FIRST_CHIP[core] + y) % CHIPS_Y)
        for g in range(groups)
        for y in range(CHIPS_Y)
    ]
    order.remove(ORIGIN)
    order.insert(ORIGIN_PLACE, ORIGIN)
    return order


def planes(groups, chips_z):
    return [
        [((g * chips_z + z) * CHIPS_Y + y) * CORES + core for g, y in plane_order(groups, core)]
        for z in range(chips_z)
        for core in range(CORES)
    ]


def swap(block, first):
    route = []
    for s in range(first, lax.axis_size(SEC) - 1, 2):
        route += [(s, s + 1), (s + 1, s)]
    return lax.ppermute(block, SEC, route)


def body(fixed_desc, moving_desc, offsets, owner, counts, vert, hori):
    groups = lax.axis_size("group")
    sections = lax.axis_size(SEC)
    chips_z = lax.axis_size("z")
    patches, flow, corr = fixed_desc.shape[1:]
    rows, cols = vert.shape[1:]
    tiles = cols // TILE_W
    length = patches * flow
    halves = -(-tiles * GROUP_LANES // TILE_W)

    hbm = pl.BlockSpec(memory_space=pltpu.HBM)
    local = pl.BlockSpec(memory_space=pltpu.VMEM)
    scalars = pl.BlockSpec(memory_space=pltpu.SMEM)
    modest = pltpu.CompilerParams(vmem_limit_bytes=16 << 20)
    border = jax.ShapeDtypeStruct((tiles, TILE_W), F32)
    upright = jax.ShapeDtypeStruct((rows, TILE_W), F32)
    lines_shape = jax.ShapeDtypeStruct((2 * tiles, TILE_W), F32)
    packed = pltpu.VMEM((length // 2 + rows, corr), fixed_desc.dtype)
    across, beside, line = pl.pallas_call(
        pack_kernel,
        out_shape=(packed, packed, in_vmem(border)),
        in_specs=[hbm] * 5,
        out_specs=(local,) * 3,
        scratch_shapes=[
            pltpu.VMEM((rows, cols), F32),
            pltpu.VMEM((rows, cols), F32),
            pltpu.VMEM(offsets.shape[1:], jnp.int32),
            pltpu.SemaphoreType.DMA((2 * PARTS + 3,)),
        ],
        compiler_params=modest,
        name="pack",
    )(
        *(
            pltpu.with_memory_space_constraint(x, pltpu.HBM)
            for x in (moving_desc.reshape(length, corr), fixed_desc.reshape(length, corr), vert, hori, offsets)
        )
    )
    across = swap(across, 1)
    beside = swap(beside, 0)
    above = from_behind(line, "group", 1)

    vert, hori = vert[0], hori[0]

    def borders(*refs):
        border_kernel(groups, *refs)

    table, firsts, right = pl.pallas_call(
        borders,
        out_shape=(in_vmem(border), in_vmem(lines_shape), in_vmem(upright)),
        in_specs=[scalars] * 2 + [local] * 3,
        out_specs=(local,) * 3,
        scratch_shapes=[pltpu.VMEM((TILE_W, TILE_W), F32)],
        compiler_params=modest,
        name="borders",
    )(owner, counts, vert, hori, line)
    mine, lines, next_columns, prev_columns = pl.pallas_call(
        match_kernel,
        out_shape=(
            pltpu.VMEM((chips_z, halves, TILE_W), F32),
            in_vmem(lines_shape), in_vmem(upright), in_vmem(upright),
        ),
        in_specs=[local] * 10,
        out_specs=(local,) * 4,
        scratch_shapes=[pltpu.VMEM((flow, length), F32), pltpu.VMEM((tiles, TILE_W), F32)],
        compiler_params=modest,
        name="match",
    )(fixed_desc, moving_desc, offsets, table, firsts, right, line, above, across, beside)

    turned = [(z + FIRST_Z) % chips_z for z in range(chips_z)]
    seen = lax.all_to_all(mine, "z", 0, 0, tiled=True, axis_index_groups=[turned]).reshape(-1, TILE_W)
    lines, seen = lax.optimization_barrier((lines, seen))
    aboves = from_behind(lines, "group", 1)
    peers = groups * lax.axis_size("y")
    block_rows = chips_z + chips_z // 2
    copies = pl.pallas_call(
        copies_kernel,
        out_shape=jax.ShapeDtypeStruct((peers, block_rows, TILE_W), F32),
        in_specs=[local],
        out_specs=local,
        scratch_shapes=[pltpu.VMEM((2 * chips_z, TILE_W), F32)],
        compiler_params=modest,
        name="copies",
    )(seen)
    seen = lax.all_to_all(
        copies, ("group",) + SEC, 0, 0, tiled=True, axis_index_groups=planes(groups, chips_z)
    ).reshape(-1, TILE_W)
    cores = list(reversed(range(CORES)))
    seen = lax.all_gather(seen, "core", axis=0, tiled=True, axis_index_groups=[cores])

    dims = (groups, sections, rows, tiles, chips_z)
    count = groups * tiles

    def both_iterations(*refs):
        stack_kernel(dims, *refs)

    field = jax.ShapeDtypeStruct((2, rows, cols), F32)
    displacement, residual = pl.pallas_call(
        both_iterations,
        out_shape=(field, field),
        in_specs=[local] * 9,
        scratch_shapes=[
            pltpu.VMEM((groups + groups // 2, sections, TILE_W), F32),
            pltpu.VMEM((groups, tiles * GROUP_LANES, sections), F32),
            pltpu.VMEM((3, count, sections), F32),
            pltpu.VMEM((24, count + 2 * tiles, sections), F32),
            pltpu.VMEM((2, rows + 2 * tiles, cols), F32),
        ],
        compiler_params=modest,
        name="stack",
    )(seen, vert, hori, line, above, lines, aboves, next_columns, prev_columns)
    return (displacement[None], residual[None])


def solution(mesh):
    groups, sections = mesh.devices.shape
    devices = mesh.devices.reshape(groups, sections // (CHIPS_Y * CORES), CHIPS_Y, CORES)
    fine = Mesh(devices, ("group",) + SEC)
    in_specs = (
        P(SEC, "group", None, None),
        P(SEC, "group", None, None),
        P(SEC, "group", None, None),
        P(SEC, "group"),
        P(SEC, "group"),
        P(SEC, "group", None),
        P(SEC, "group", None),
    )
    out_specs = (P(SEC, None, "group", None), P(SEC, None, "group", None))
    return jax.shard_map(body, mesh=fine, in_specs=in_specs, out_specs=out_specs, check_vma=False)
```
